256 devices in a mesh: dp: 4 (over y), segment: 2 (over x_hi), tm: 32 (over z, x_lo, core).
Axes of the slice: x: 4 (x_hi: 2, x_lo: 2; x = x_hi * 2 + x_lo), y: 4, z: 8, core: 2. Of those that a mesh axis runs over, the one named last changes fastest.
Arguments:
- inputs: bfloat16 [4, 4096, 1536], P('dp', 'tm'), may hold values from -6 to 6
- lengths: int32 [4], P('dp'), may hold values from 1024 to 4096, as said below
- w_first: bfloat16 [2, 1536, 1536], P('segment'), may hold values from -0.15625 to 0.15625
- kernel: float32 [2, 31, 768], P('segment'), may hold values from -1 to 1
- gain_first: float32 [2, 1536], P('segment'), may hold values from 0.1 to 1.9
- gain_second: float32 [2, 768], P('segment'), may hold values from 0.1 to 1.9
- w_second: bfloat16 [2, 768, 1536], P('segment'), may hold values from -0.21875 to 0.21875
- grad_output: bfloat16 [4, 4096, 1536], P('dp', 'tm'), may hold values from -6 to 6
Outputs:
- segment_outputs: bfloat16 [2, 4, 4096, 1536], P('segment', 'dp', 'tm')
- segment_grads: bfloat16 [2, 4, 4096, 1536], P('segment', 'dp', 'tm')
- grad_w_first: float32 [2, 1536, 1536], P('segment', ('dp', 'tm'))
- grad_kernel: float32 [2, 31, 768], P('segment', None, ('dp', 'tm'))
- grad_gain_first: float32 [2, 1536], P('segment', ('dp', 'tm'))
- grad_gain_second: float32 [2, 768], P('segment', ('dp', 'tm'))
- grad_w_second: float32 [2, 768, 1536], P('segment', ('dp', 'tm'))
The draws below stay inside these ranges and needn't reach their ends.
Inputs may be any that keep to these rules, and one draw needn't show every extreme that they name: `lengths`: at least one utterance has all 4096 frames valid.
All inputs are finite; a program needn't handle non-finite values.
Results may differ from the reference program's by a relative error of at most 0.04.
Values may be sent and summed in bfloat16 or wider, within the bound.
A program may use at most 128 MiB of HBM per device.

```python
import jax
import jax.numpy as jnp
from jax import lax

D = 1536
CH = 768
KW = 31
FR = 128
SEGMENTS = 2
BATCH = 4
FRAMES = 4096
N_TM = 32


def draw_lengths(key, part):
    key = jax.random.fold_in(key, 11)
    first_key, second_key = jax.random.split(key)
    spans = jax.random.randint(first_key, (BATCH,), FRAMES // 4, FRAMES + 1)
    chosen = jax.random.randint(second_key, (), 0, BATCH)
    return jnp.where(jnp.arange(BATCH) == chosen, FRAMES, spans).astype(jnp.int32)


def steps_of(rng, dims, shards, low, top_value):
    factor_of = 1.0
    for dim, blocks in shards:
        heights = jax.random.uniform(jax.random.fold_in(jax.random.fold_in(rng, 6), dim), (blocks,), jnp.float32, low / len(shards), top_value / len(shards))
        factor_of = factor_of * jnp.repeat(jnp.exp(heights), dims[dim] // blocks).reshape((-1,) + (1,) * (len(dims) - 1 - dim))
    return factor_of


def scatter_about(rng, shape, scale, reach, shards=(), held_as=jnp.bfloat16):
    entries = scale * jax.random.normal(rng, shape, jnp.float32)
    if shards:
        entries = entries * steps_of(rng, shape, shards, -0.22, 0.18)
    return jnp.clip(entries, -reach, reach).astype(held_as)


def setup_inputs(seed: int = 0) -> dict:
    arg_keys = jax.random.split(jax.random.key(seed), 9)
    return {
        "inputs": scatter_about(arg_keys[0], (BATCH, FRAMES, D), 1.0, 6.0, ((0, 4), (1, 32))),
        "lengths": draw_lengths(jax.random.fold_in(arg_keys[8], 71), 0),
        "w_first": scatter_about(arg_keys[2], (SEGMENTS, D, 2 * CH), D ** -0.5, 0.15625, ((0, 2),)),
        "kernel": scatter_about(arg_keys[3], (SEGMENTS, KW, CH), KW ** -0.5, 1.0, ((0, 2),), jnp.float32),
        "gain_first": jnp.clip(1.0 + 0.18 * jax.random.normal(arg_keys[4], (SEGMENTS, D), jnp.float32), 0.1, 1.9),
        "gain_second": jnp.clip(1.0 + 0.18 * jax.random.normal(arg_keys[5], (SEGMENTS, CH), jnp.float32), 0.1, 1.9),
        "w_second": scatter_about(arg_keys[6], (SEGMENTS, CH, D), CH ** -0.5, 0.21875, ((0, 2),)),
        "grad_output": scatter_about(arg_keys[7], (BATCH, FRAMES, D), 1.0, 6.0, ((0, 4), (1, 32))),
    }


EPS = 1e-05

def normalize(values, gain):
    mean = lax.optimization_barrier(jnp.mean(values, axis=-1, keepdims=True))
    centred = values - mean
    spread = lax.optimization_barrier(jnp.mean(centred * centred, axis=-1, keepdims=True))
    return centred * lax.rsqrt(spread + EPS) * gain

def swish_norm(values, gain):
    normal = normalize(values, gain)
    return normal * jax.nn.sigmoid(normal)

def depthwise(padded, kern):
    count = padded.shape[0] - kern.shape[0] + 1
    total = jnp.zeros((count, padded.shape[1]), jnp.float32)
    for shift_k in range(kern.shape[0]):
        total = total + kern[shift_k] * padded[shift_k:shift_k + count]
    return total

def round_partials(parts):
    rounded = lax.optimization_barrier(parts.astype(jnp.bfloat16))
    return lax.optimization_barrier(jnp.sum(rounded.astype(jnp.float32), axis=0))

def block_product(left, right):
    left_blocks = left.reshape(N_TM, FR, left.shape[1])
    right_blocks = right.reshape(N_TM, FR, right.shape[1])

    def step_fn(total, pair):
        part = jnp.dot(pair[0].T, pair[1], preferred_element_type=jnp.float32)
        rounded = lax.optimization_barrier(part.astype(jnp.bfloat16))
        return (total + rounded.astype(jnp.float32), None)
    init = jnp.zeros((left.shape[1], right.shape[1]), jnp.float32)
    total, _ = lax.scan(step_fn, init, (left_blocks, right_blocks))
    return total

def block_vjp(func, values, gain, cotangent):
    value_blocks = values.reshape(N_TM, FR, values.shape[1])
    cot_blocks = cotangent.reshape(N_TM, FR, cotangent.shape[1])

    def one_block(vals, cots):
        _, pull = jax.vjp(func, vals, gain)
        return pull(cots)
    d_values, d_gains = jax.vmap(one_block)(value_blocks, cot_blocks)
    return (d_values.reshape(values.shape), round_partials(d_gains))

def front(hidden, maskf, w_one, gain_one):
    normed = normalize(hidden.astype(jnp.float32), gain_one).astype(jnp.bfloat16)
    pre = jnp.dot(normed, w_one, preferred_element_type=jnp.float32)
    width = pre.shape[1] // 2
    gated = (pre[:, :width] * jax.nn.sigmoid(pre[:, width:]) * maskf).astype(jnp.bfloat16)
    return (normed, pre, gated)

def tail(hidden, maskf, padded, kern, gain_two, w_two):
    conv = depthwise(padded, kern)
    act = swish_norm(conv, gain_two).astype(jnp.bfloat16)
    out = jnp.dot(act, w_two, preferred_element_type=jnp.float32)
    result = (hidden.astype(jnp.float32) + maskf * out).astype(jnp.bfloat16)
    return (result, conv, act)

def back_tail(maskf, conv, act, gain_two, w_two, grad_in):
    upstream = grad_in.astype(jnp.float32)
    d_out = (upstream * maskf).astype(jnp.bfloat16)
    grad_two = block_product(act, d_out)
    d_act = jnp.dot(d_out, w_two.T, preferred_element_type=jnp.float32)
    d_conv, grad_gain_two = block_vjp(swish_norm, conv, gain_two, d_act)
    return (upstream, grad_two, d_conv, grad_gain_two)

def back_front(hidden, maskf, normed, pre, padded, d_conv, d_padded, w_one, kern, gain_one, upstream):
    count = d_conv.shape[0]
    width_c = d_conv.shape[1]
    grad_kern = jnp.stack([round_partials((padded[k:k + count] * d_conv).reshape(N_TM, FR, width_c).sum(axis=1)) for k in range(kern.shape[0])])
    d_gated = depthwise(d_padded, kern[::-1]) * maskf
    width = pre.shape[1] // 2
    first = pre[:, :width]
    sig = jax.nn.sigmoid(pre[:, width:])
    d_pre = jnp.concatenate([d_gated * sig, d_gated * first * sig * (1.0 - sig)], axis=1).astype(jnp.bfloat16)
    grad_one = block_product(normed, d_pre)
    d_normed = jnp.dot(d_pre, w_one.T, preferred_element_type=jnp.float32)
    d_hidden, grad_gain_one = block_vjp(normalize, hidden.astype(jnp.float32), gain_one, d_normed)
    grad_hidden = (upstream + d_hidden).astype(jnp.bfloat16)
    return (grad_hidden, grad_one, grad_kern, grad_gain_one)

def reference(inputs, lengths, w_first, kernel, gain_first, gain_second, w_second, grad_output):
    half = KW // 2
    outs_all = []
    grads_all = []
    acc = [[jnp.zeros((D, 2 * CH), jnp.float32), jnp.zeros((KW, CH), jnp.float32), jnp.zeros((D,), jnp.float32), jnp.zeros((CH,), jnp.float32), jnp.zeros((CH, D), jnp.float32)] for s in range(SEGMENTS)]
    for utter in range(BATCH):
        maskf = (jnp.arange(FRAMES, dtype=jnp.int32) < lengths[utter]).astype(jnp.float32)[:, None]
        hidden = inputs[utter]
        saved = []
        outs_here = []
        for s in range(SEGMENTS):
            normed, pre, gated = front(hidden, maskf, w_first[s], gain_first[s])
            padded = jnp.pad(gated, ((half, half), (0, 0))).astype(jnp.float32)
            result, conv, act = tail(hidden, maskf, padded, kernel[s], gain_second[s], w_second[s])
            saved.append((hidden, normed, pre, padded, conv, act))
            outs_here.append(result)
            hidden = result
        grad = grad_output[utter]
        grads_here = [None] * SEGMENTS
        for s in reversed(range(SEGMENTS)):
            hid, normed, pre, padded, conv, act = saved[s]
            upstream, grad_two, d_conv, grad_gain_two = back_tail(maskf, conv, act, gain_second[s], w_second[s], grad)
            d_padded = jnp.pad(d_conv, ((half, half), (0, 0)))
            grad, grad_one, grad_kern, grad_gain_one = back_front(hid, maskf, normed, pre, padded, d_conv, d_padded, w_first[s], kernel[s], gain_first[s], upstream)
            grads_here[s] = grad
            acc[s] = [acc[s][0] + grad_one, acc[s][1] + grad_kern, acc[s][2] + grad_gain_one, acc[s][3] + grad_gain_two, acc[s][4] + grad_two]
        outs_all.append(jnp.stack(outs_here))
        grads_all.append(jnp.stack(grads_here))
    segment_outputs = jnp.stack(outs_all, axis=1)
    segment_grads = jnp.stack(grads_all, axis=1)
    return (segment_outputs, segment_grads, jnp.stack([a[0] for a in acc]), jnp.stack([a[1] for a in acc]), jnp.stack([a[2] for a in acc]), jnp.stack([a[3] for a in acc]), jnp.stack([a[4] for a in acc]))
```

```python
import functools

import jax
import jax.numpy as jnp
from jax import lax
from jax.experimental import pallas as pl
from jax.experimental.pallas import tpu as pltpu
from jax.sharding import PartitionSpec as P

EPS = 1e-05
F32 = jnp.float32
BF16 = jnp.bfloat16
MESH = pl.DeviceIdType.MESH
NT = (((1,), (1,)), ((), ()))
HALO = 16
TAPS = 31
LANE = 128
ROWS = 32


def dot(a, b):
    return jnp.dot(a, b, preferred_element_type=F32)


def dot_t(a, b):
    return lax.dot_general(a, b, NT, preferred_element_type=F32)


def kernel(
    n_y,
    n_z,
    n_tm,
    len_ref,
    inp,
    gout,
    w1,
    w2,
    kern,
    gain1,
    gain2,
    out_ref,
    grad_ref,
    o_one,
    o_two,
    o_small,
    cur,
    e,
    xhat,
    rstd1,
    normed,
    p_buf,
    sig_buf,
    gpad,
    dpad,
    conv,
    zhat,
    rstd2,
    zn_buf,
    act,
    d_act,
    d_norm,
    edge_g,
    edge_d,
    halo_g,
    halo_d,
    dout4,
    dpre4,
    dout_r,
    dpre_r,
    n_t,
    a_t,
    gk,
    gg1,
    ebuf,
    tbuf,
    pa,
    pb,
    ya,
    yb,
    qa,
    qb,
    za,
    zb,
    fs,
    fr,
    sem_h,
    sem_out,
    sem_grad,
    sem_x,
    sem_y,
    sem_z,
    sem_f,
):
    frames, model = inp.shape
    width = w2.shape[0]
    dy = lax.axis_index("dp")
    seg = lax.axis_index("segment")
    t = lax.axis_index("tm")
    c = t % 2
    xl = (t // 2) % 2
    z = t // 4
    j = t % 4
    base = z * 4
    group = [base + xl * 2 + (1 - c), base + (1 - xl) * 2 + c, base + (1 - xl) * 2 + (1 - c)]
    right = (t + 1) % n_tm
    left = (t + n_tm - 1) % n_tm
    first_seg = seg == 0
    last_seg = seg == 1

    def remote(src, dst, sems, index, axis, peer):
        return pltpu.make_async_remote_copy(
            src_ref=src,
            dst_ref=dst,
            send_sem=sems.at[0, index],
            recv_sem=sems.at[1, index],
            device_id={axis: peer},
            device_id_type=MESH,
        )

    barrier = pltpu.get_barrier_semaphore()
    greet = [("tm", left), ("tm", right), ("segment", 1 - seg)]
    greet += [("tm", g) for g in group]
    greet += [("dp", (dy + d) % n_y) for d in range(1, n_y)]
    greet += [("tm", ((z + d) % n_z) * 4 + j) for d in range(1, n_z)]
    for axis, peer in greet:
        pl.semaphore_signal(barrier, inc=1, device_id={axis: peer}, device_id_type=MESH)

    length = len_ref[0]

    def mask_of(start, rows):
        ids = t * frames + start + lax.broadcasted_iota(jnp.int32, (rows, 1), 0)
        return (ids < length).astype(F32)

    def over_rows(work):
        def step(i, carry):
            start = pl.multiple_of(i * ROWS, ROWS)
            work(start, pl.ds(start, ROWS))
            return carry

        lax.fori_loop(0, frames // ROWS, step, 0)

    def out_copies():
        return [
            remote(
                out_ref.at[pl.ds(64 * i, 64)], cur.at[pl.ds(64 * i, 64)], sem_out, i, "segment", 1 - seg
            )
            for i in range(2)
        ]

    def grad_copies():
        return [
            remote(
                grad_ref.at[pl.ds(64 * i, 64)], e.at[pl.ds(64 * i, 64)], sem_grad, i, "segment", 1 - seg
            )
            for i in range(2)
        ]

    def halo_copies(edge, halo, offset):
        return [
            remote(edge.at[0], halo.at[1], sem_h, offset, "tm", left),
            remote(edge.at[1], halo.at[0], sem_h, offset + 1, "tm", right),
        ]

    def peer_j(d):
        return group[d] % 4

    def dout_copies():
        return [
            remote(dout4.at[peer_j(d)], dout_r.at[d], sem_x, d, "tm", group[d]) for d in range(3)
        ]

    def dpre_copies():
        return [
            remote(dpre4.at[peer_j(d)], dpre_r.at[d], sem_x, 3 + d, "tm", group[d]) for d in range(3)
        ]

    def turned_copies():
        return [
            remote(n_t.at[0], n_t.at[d + 1], sem_x, 6 + d, "tm", group[d]) for d in range(3)
        ] + [remote(a_t.at[0], a_t.at[d + 1], sem_x, 9 + d, "tm", group[d]) for d in range(3)]

    def start_all(copies):
        for copy in copies:
            copy.start()

    def upper():
        def mask_rows(start, rows):
            d_out = (e[rows, :].astype(F32) * mask_of(start, ROWS)).astype(BF16)
            for i in range(4):
                dout4[i, rows, :] = d_out[:, 384 * i : 384 * (i + 1)]

        over_rows(mask_rows)
        d_out = jnp.concatenate([dout4[i] for i in range(4)], axis=1)
        for n in range(width // 256):
            d_act[:, 256 * n : 256 * (n + 1)] = dot_t(d_out, w2[256 * n : 256 * (n + 1), :])

    def taps_over(src, block, flip):
        cols = pl.ds(pl.multiple_of(block * LANE, LANE), LANE)
        whole = src[:, cols]
        total = jnp.zeros((frames, LANE), F32)
        for r in range(8):
            moved = whole if r == 0 else pltpu.roll(whole, whole.shape[0] - r, 0)
            for k in range(TAPS):
                if (k + 1) % 8 == r:
                    at = k + 1 - r
                    tap = TAPS - 1 - k if flip else k
                    total = total + kern[tap : tap + 1, cols] * moved[at : at + frames]
        return cols, total

    def turn():
        for i in range(model // LANE):
            cols = slice(LANE * i, LANE * (i + 1))
            n_t[0, cols, :] = normed[:, cols].astype(F32).T.astype(BF16)
        for i in range(width // LANE):
            cols = slice(LANE * i, LANE * (i + 1))
            a_t[0, cols, :] = act[:, cols].astype(F32).T.astype(BF16)

    @pl.when(last_seg)
    def _():
        e[...] = gout[...]
        upper()

    pl.semaphore_wait(barrier, len(greet))

    @pl.when(last_seg)
    def _():
        start_all(dout_copies())
        for copy in out_copies():
            copy.wait_recv()

    @pl.when(first_seg)
    def _():
        cur[...] = inp[...]

    def norm_rows(start, rows):
        x = cur[rows, :].astype(F32)
        centred = x - jnp.mean(x, axis=-1, keepdims=True)
        rstd = lax.rsqrt(jnp.mean(centred * centred, axis=-1, keepdims=True) + EPS)
        hat = centred * rstd
        xhat[rows, :] = hat
        rstd1[rows, :] = jnp.broadcast_to(rstd, (ROWS, LANE))
        normed[rows, :] = (hat * gain1[...]).astype(BF16)

    over_rows(norm_rows)
    maskf = mask_of(0, frames)
    for n in range(width // 256):
        cols = slice(256 * n, 256 * (n + 1))
        q_cols = slice(width + 256 * n, width + 256 * (n + 1))
        p = dot(normed[...], w1[:, cols])
        sig = jax.nn.sigmoid(dot(normed[...], w1[:, q_cols]))
        p_buf[:, cols] = p
        sig_buf[:, cols] = sig
        gated = (p * sig * maskf).astype(BF16)
        gpad[HALO : HALO + frames, cols] = gated.astype(F32)
        edge_g[0, :, cols] = gated[:HALO]
        edge_g[1, :, cols] = gated[frames - HALO :]
    copies = halo_copies(edge_g, halo_g, 0)
    start_all(copies)
    for copy in copies:
        copy.wait()
    has_left = (t > 0).astype(F32)
    has_right = (t < n_tm - 1).astype(F32)
    gpad[0:HALO, :] = halo_g[0].astype(F32) * has_left
    gpad[HALO + frames :, :] = halo_g[1].astype(F32) * has_right

    def conv_block(block, carry):
        cols, total = taps_over(gpad, block, False)
        conv[:, cols] = total
        return carry

    lax.fori_loop(0, width // LANE, conv_block, 0)

    def act_rows(start, rows):
        x = conv[rows, :]
        centred = x - jnp.mean(x, axis=-1, keepdims=True)
        rstd = lax.rsqrt(jnp.mean(centred * centred, axis=-1, keepdims=True) + EPS)
        hat = centred * rstd
        zn = hat * gain2[...]
        zhat[rows, :] = hat
        zn_buf[rows, :] = zn
        rstd2[rows, :] = jnp.broadcast_to(rstd, (ROWS, LANE))
        act[rows, :] = (zn * jax.nn.sigmoid(zn)).astype(BF16)

    over_rows(act_rows)
    for n in range(model // 512):
        cols = slice(512 * n, 512 * (n + 1))
        out = dot(act[...], w2[:, cols])
        out_ref[:, cols] = (cur[:, cols].astype(F32) + maskf * out).astype(BF16)

    @pl.when(first_seg)
    def _():
        copies = out_copies()
        start_all(copies)
        turn()
        for copy in copies:
            copy.wait_send()
        start_all(turned_copies())
        for copy in grad_copies():
            copy.wait_recv()
        upper()

    gg1[...] = jnp.zeros_like(gg1)
    gk[...] = jnp.zeros_like(gk)

    def conv_grad_rows(start, rows):
        zn = zn_buf[rows, :]
        hat = zhat[rows, :]
        sg = jax.nn.sigmoid(zn)
        d_zn = d_act[rows, :] * (sg + zn * sg * (1.0 - sg))
        gk[TAPS : TAPS + 1, :] += jnp.sum(d_zn * hat, axis=0, keepdims=True)
        d_hat = d_zn * gain2[...]
        m_one = jnp.mean(d_hat, axis=-1, keepdims=True)
        m_two = jnp.mean(d_hat * hat, axis=-1, keepdims=True)
        d_conv = rstd2[rows, 0:1] * (d_hat - m_one - hat * m_two)
        dpad[pl.ds(HALO + start, ROWS), :] = d_conv

    over_rows(conv_grad_rows)
    edge_d[0] = dpad[HALO : 2 * HALO, :].astype(BF16)
    edge_d[1] = dpad[frames : HALO + frames, :].astype(BF16)
    copies = halo_copies(edge_d, halo_d, 2)
    start_all(copies)

    @pl.when(first_seg)
    def _():
        start_all(dout_copies())

    def tap_grads(block, carry):
        cols = pl.ds(pl.multiple_of(block * LANE, LANE), LANE)
        whole = gpad[:, cols]
        d_conv = dpad[HALO : HALO + frames, cols]
        for r in range(8):
            moved = whole if r == 0 else pltpu.roll(whole, whole.shape[0] - r, 0)
            for k in range(TAPS):
                if (k + 1) % 8 == r:
                    at = k + 1 - r
                    gk[k : k + 1, cols] = jnp.sum(
                        moved[at : at + frames] * d_conv, axis=0, keepdims=True
                    )
        return carry

    lax.fori_loop(0, width // LANE, tap_grads, 0)
    for copy in copies:
        copy.wait()
    dpad[0:HALO, :] = halo_d[0].astype(F32) * has_left
    dpad[HALO + frames :, :] = halo_d[1].astype(F32) * has_right

    for half in range(2):

        def pre_block(block, carry):
            cols, total = taps_over(dpad, half * 3 + block, True)
            d_gated = total * maskf
            sig = sig_buf[:, cols]
            d_p = d_gated * sig
            d_q = d_p * p_buf[:, cols] * (1.0 - sig)
            part = pl.ds(pl.multiple_of(block * LANE, LANE), LANE)
            dpre4[half, :, part] = d_p.astype(BF16)
            dpre4[2 + half, :, part] = d_q.astype(BF16)
            return carry

        lax.fori_loop(0, 3, pre_block, 0)

    @pl.when(first_seg)
    def _():
        start_all(dpre_copies())

    d_pre = jnp.concatenate([dpre4[i] for i in range(4)], axis=1)
    for n in range(model // 512):
        rows = slice(512 * n, 512 * (n + 1))
        d_norm[:, rows] = dot_t(d_pre, w1[rows, :])

    def grad_rows(start, rows):
        d_normed = d_norm[rows, :]
        hat = xhat[rows, :]
        gg1[0:1, :] += jnp.sum(d_normed * hat, axis=0, keepdims=True)
        d_hat = d_normed * gain1[...]
        m_one = jnp.mean(d_hat, axis=-1, keepdims=True)
        m_two = jnp.mean(d_hat * hat, axis=-1, keepdims=True)
        d_h = rstd1[rows, 0:1] * (d_hat - m_one - hat * m_two)
        grad_ref[rows, :] = (e[rows, :].astype(F32) + d_h).astype(BF16)

    over_rows(grad_rows)

    @pl.when(last_seg)
    def _():
        copies = grad_copies()
        start_all(copies)
        turn()
        for copy in copies:
            copy.wait_send()
        start_all(dpre_copies())
        start_all(turned_copies())

    for i in range(width // LANE):
        cols = slice(LANE * i, LANE * (i + 1))
        ebuf[cols, :] = gk[:, cols].T
    for i in range(model // LANE):
        cols = slice(LANE * i, LANE * (i + 1))
        tbuf[cols, :] = jnp.broadcast_to(gg1[0:1, cols], (LANE, LANE)).T

    for copy in dpre_copies() + turned_copies() + dout_copies():
        copy.wait()
    own_pre = dpre4[j]
    rhs_one = jnp.concatenate([own_pre] + [dpre_r[d] for d in range(3)], axis=0)

    def y_copy(buf, got, d, offset):
        peer = (dy + d) % n_y
        return remote(buf.at[peer], got.at[d - 1], sem_y, offset + d - 1, "dp", peer)

    def z_copy(buf, got, d, offset):
        peer = (z + d) % n_z
        return remote(buf.at[peer], got.at[d - 1], sem_z, offset + d - 1, "tm", peer * 4 + j)

    y_order = list(range(1, n_y)) + [0]
    rows_one = model // n_y
    rows_two = width // n_y
    for d in y_order:
        peer = (dy + d) % n_y
        start = pl.multiple_of(peer * rows_one, rows_one)
        lhs = jnp.concatenate([n_t[i, pl.ds(start, rows_one), :] for i in range(4)], axis=1)
        part = dot(lhs, rhs_one)
        for i in range(n_z):
            pa[peer, i] = part[48 * i : 48 * (i + 1)].astype(BF16)
        if d:
            y_copy(pa, ya, d, 0).start()

    rhs_two = jnp.concatenate([dout4[j]] + [dout_r[d] for d in range(3)], axis=0)
    lane = lax.broadcasted_iota(jnp.int32, (24, LANE), 1)
    for d in y_order:
        peer = (dy + d) % n_y
        start = pl.multiple_of(peer * rows_two, rows_two)
        lhs = jnp.concatenate([a_t[i, pl.ds(start, rows_two), :] for i in range(4)], axis=1)
        part = dot(lhs, rhs_two)
        for i in range(n_z):
            at = pl.multiple_of(peer * rows_two + 24 * i, 8)
            at_t = pl.multiple_of(peer * rows_one + 48 * i, 8)
            extra = ebuf[pl.ds(at, 24), :]
            extra = jnp.where(lane == 32, tbuf[pl.ds(at_t, 24), :], extra)
            extra = jnp.where(lane == 33, tbuf[pl.ds(at_t + 24, 24), :], extra)
            mine = part[24 * i : 24 * (i + 1)]
            low = jnp.concatenate([mine[:, 256:], extra], axis=1)
            pb[peer, i] = jnp.concatenate([mine[:, :256], low], axis=0).astype(BF16)
        if d:
            y_copy(pb, yb, d, n_y - 1).start()

    for buf, got, q_buf, z_got, off_y, off_z in (
        (pa, ya, qa, za, 0, 0),
        (pb, yb, qb, zb, n_y - 1, n_z - 1),
    ):
        for d in range(1, n_y):
            y_copy(buf, got, d, off_y).wait()
        for i in range(n_z):
            total = buf[dy, i].astype(F32)
            for d in range(n_y - 1):
                total = total + got[d, i].astype(F32)
            q_buf[i] = total.astype(BF16)
        for d in range(1, n_z):
            z_copy(q_buf, z_got, d, off_z).start()

    fs[...] = jnp.zeros_like(fs)
    for d in range(1, n_z):
        z_copy(qa, za, d, 0).wait()
    total = qa[z].astype(F32)
    for d in range(n_z - 1):
        total = total + za[d].astype(F32)
    for i in range(4):
        fs[i, 0:12, :] = total[12 * i : 12 * (i + 1)]
    for d in range(1, n_z):
        z_copy(qb, zb, d, n_z - 1).wait()
    total = qb[z].astype(F32)
    for d in range(n_z - 1):
        total = total + zb[d].astype(F32)
    two = jnp.concatenate([total[:24], total[24:, :LANE]], axis=1)
    extra = total[24:, LANE:]
    for i in range(4):
        fs[i, 16:22, :] = two[6 * i : 6 * (i + 1)]
        for m in range(3):
            fs[i, 24:32, LANE * m : LANE * (m + 1)] = extra[8 * m : 8 * (m + 1)]
    copies = [remote(fs.at[peer_j(d)], fr.at[j], sem_f, d, "tm", group[d]) for d in range(3)]
    start_all(copies)
    fr[j] = fs[j]
    for copy in copies:
        copy.wait()
    small = jnp.zeros((8, 3 * LANE), F32)
    for i in range(4):
        cols = slice(384 * i, 384 * (i + 1))
        o_one[:, cols] = fr[i, 0:12, :]
        o_two[:, cols] = fr[i, 16:22, :]
        small = small + fr[i, 24:32, :]
    for m in range(3):
        o_small[8 * m : 8 * (m + 1), :] = small[:, LANE * m : LANE * (m + 1)]


def per_device(inputs, lengths, w_first, kernel_w, gain_first, gain_second, w_second, grad_output):
    n_y = lax.axis_size("dp")
    n_tm = lax.axis_size("tm")
    n_z = n_tm // 4
    frames, model = inputs.shape[1:]
    width = w_second.shape[1]
    groups = n_y * n_tm
    vmem = pl.BlockSpec(memory_space=pltpu.VMEM)

    def buf(shape, dtype):
        return pltpu.VMEM(shape, dtype)

    wide = (frames, model)
    thin = (frames, width)
    padded = (frames + 2 * HALO, width)
    third = (4, frames, 384)
    scratch = [
        buf(wide, BF16),
        buf(wide, BF16),
        buf(wide, F32),
        buf((frames, LANE), F32),
        buf(wide, BF16),
        buf(thin, F32),
        buf(thin, F32),
        buf(padded, F32),
        buf(padded, F32),
        buf(thin, F32),
        buf(thin, F32),
        buf((frames, LANE), F32),
        buf(thin, F32),
        buf(thin, BF16),
        buf(thin, F32),
        buf(wide, F32),
        buf((2, HALO, width), BF16),
        buf((2, HALO, width), BF16),
        buf((2, HALO, width), BF16),
        buf((2, HALO, width), BF16),
        buf(third, BF16),
        buf(third, BF16),
        buf((3, frames, 384), BF16),
        buf((3, frames, 384), BF16),
        buf((4, model, LANE), BF16),
        buf((4, width, LANE), BF16),
        buf((LANE, width), F32),
        buf((8, model), F32),
        buf((width, LANE), F32),
        buf((model, LANE), F32),
        buf((n_y, n_z, 48, 384), BF16),
        buf((n_y, n_z, 48, 256), BF16),
        buf((n_y - 1, n_z, 48, 384), BF16),
        buf((n_y - 1, n_z, 48, 256), BF16),
        buf((n_z, 48, 384), BF16),
        buf((n_z, 48, 256), BF16),
        buf((n_z - 1, 48, 384), BF16),
        buf((n_z - 1, 48, 256), BF16),
        buf((4, 32, 384), F32),
        buf((4, 32, 384), F32),
        pltpu.SemaphoreType.DMA((2, 4)),
        pltpu.SemaphoreType.DMA((2, 2)),
        pltpu.SemaphoreType.DMA((2, 2)),
        pltpu.SemaphoreType.DMA((2, 12)),
        pltpu.SemaphoreType.DMA((2, 2 * (n_y - 1))),
        pltpu.SemaphoreType.DMA((2, 2 * (n_z - 1))),
        pltpu.SemaphoreType.DMA((2, 3)),
    ]
    out, grad, one, two, small = pl.pallas_call(
        functools.partial(kernel, n_y, n_z, n_tm),
        out_shape=(
            jax.ShapeDtypeStruct(wide, BF16),
            jax.ShapeDtypeStruct(wide, BF16),
            jax.ShapeDtypeStruct((model // groups, model), F32),
            jax.ShapeDtypeStruct((width // groups, model), F32),
            jax.ShapeDtypeStruct((24, LANE), F32),
        ),
        in_specs=[pl.BlockSpec(memory_space=pltpu.SMEM)] + [vmem] * 7,
        out_specs=(vmem,) * 5,
        scratch_shapes=scratch,
        compiler_params=pltpu.CompilerParams(
            collective_id=0, has_side_effects=True, vmem_limit_bytes=60 * 1024 * 1024
        ),
        cost_estimate=pl.CostEstimate(
            flops=2 * 3 * frames * model * 3 * width, bytes_accessed=12_000_000, transcendentals=0
        ),
    )(
        lengths,
        inputs[0],
        grad_output[0],
        w_first[0],
        w_second[0],
        kernel_w[0],
        gain_first,
        gain_second,
    )
    j = lax.axis_index("tm") % 4
    mine = lax.dynamic_slice(small, (6 * j, 0), (6, LANE))
    g_one = lax.dynamic_slice(small[:, 32:34].T.reshape(48), (12 * j,), (12,))
    return (
        out[None, None],
        grad[None, None],
        one[None],
        mine[:, :TAPS].T[None],
        g_one[None],
        mine[:, TAPS][None],
        two[None],
    )


def solution(mesh):
    in_specs = (
        P("dp", "tm", None),
        P("dp"),
        P("segment", None, None),
        P("segment", None, None),
        P("segment", None),
        P("segment", None),
        P("segment", None, None),
        P("dp", "tm", None),
    )
    out_specs = (
        P("segment", "dp", "tm", None),
        P("segment", "dp", "tm", None),
        P("segment", ("dp", "tm"), None),
        P("segment", None, ("dp", "tm")),
        P("segment", ("dp", "tm")),
        P("segment", ("dp", "tm")),
        P("segment", ("dp", "tm"), None),
    )
    return jax.shard_map(
        per_device, mesh=mesh, in_specs=in_specs, out_specs=out_specs, check_vma=False
    )
```

```python
import functools

import jax
import jax.numpy as jnp
from jax import lax
from jax.experimental import pallas as pl
from jax.experimental.pallas import tpu as pltpu
from jax.sharding import PartitionSpec as P

EPS = 1e-05
F32 = jnp.float32
BF16 = jnp.bfloat16
MESH = pl.DeviceIdType.MESH
NT = (((1,), (1,)), ((), ()))
HALO = 16
TAPS = 31
LANE = 128
ROWS = 32


def dot(a, b):
    return jnp.dot(a, b, preferred_element_type=F32)


def dot_t(a, b):
    return lax.dot_general(a, b, NT, preferred_element_type=F32)


def kernel(
    n_y,
    n_z,
    n_tm,
    len_ref,
    inp,
    gout,
    w1_hbm,
    w2_hbm,
    kern,
    gain1,
    gain2,
    out_hbm,
    grad_hbm,
    o_one,
    o_two,
    o_kern,
    o_gain1,
    o_gain2,
    w1,
    w2,
    out_ref,
    grad_ref,
    cur,
    e,
    xhat,
    rstd1,
    normed,
    p_buf,
    sig_buf,
    gpad,
    dpad,
    conv,
    zhat,
    rstd2,
    zn_buf,
    act,
    d_act,
    d_norm,
    edge_g,
    edge_d,
    halo_g,
    halo_d,
    dout4,
    dpre4,
    dout_r,
    dpre_r,
    n_t,
    a_t,
    gk,
    gg1,
    ebuf,
    tbuf,
    pa,
    pb,
    ya_in,
    yb_in,
    ya,
    yb,
    qa,
    qb,
    za,
    zb,
    fs,
    fr,
    sem_w,
    sem_h,
    sem_out,
    sem_grad,
    sem_x,
    sem_y,
    sem_z,
    sem_f,
):
    frames, model = inp.shape
    width = w2.shape[0]
    dy = lax.axis_index("dp")
    seg = lax.axis_index("segment")
    t = lax.axis_index("tm")
    c = t % 2
    xl = (t // 2) % 2
    z = t // 4
    j = t % 4
    base = z * 4
    group = [base + xl * 2 + (1 - c), base + (1 - xl) * 2 + c, base + (1 - xl) * 2 + (1 - c)]
    right = (t + 1) % n_tm
    left = (t + n_tm - 1) % n_tm
    first_seg = seg == 0
    last_seg = seg == 1

    def remote(src, dst, sems, index, axis, peer):
        return pltpu.make_async_remote_copy(
            src_ref=src,
            dst_ref=dst,
            send_sem=sems.at[0, index],
            recv_sem=sems.at[1, index],
            device_id={axis: peer},
            device_id_type=MESH,
        )

    load_w1 = pltpu.make_async_copy(w1_hbm, w1, sem_w.at[0])
    load_w2 = pltpu.make_async_copy(w2_hbm, w2, sem_w.at[1])
    store_out = pltpu.make_async_copy(out_ref, out_hbm, sem_w.at[2])
    store_grad = pltpu.make_async_copy(grad_ref, grad_hbm, sem_w.at[3])
    barrier = pltpu.get_barrier_semaphore()
    greet = [("tm", left), ("tm", right), ("segment", 1 - seg)]
    greet += [("tm", g) for g in group]
    greet += [("dp", (dy + d) % n_y) for d in range(1, n_y)]
    greet += [("tm", ((z + d) % n_z) * 4 + j) for d in range(1, n_z)]
    for axis, peer in greet:
        pl.semaphore_signal(barrier, inc=1, device_id={axis: peer}, device_id_type=MESH)

    @pl.when(first_seg)
    def _():
        load_w1.start()
        load_w2.start()

    @pl.when(last_seg)
    def _():
        load_w2.start()
        load_w1.start()

    length = len_ref[0]

    def mask_of(start, rows):
        ids = t * frames + start + lax.broadcasted_iota(jnp.int32, (rows, 1), 0)
        return (ids < length).astype(F32)

    def over_rows(work):
        def step(i, carry):
            start = pl.multiple_of(i * ROWS, ROWS)
            work(start, pl.ds(start, ROWS))
            return carry

        lax.fori_loop(0, frames // ROWS, step, 0)

    def out_copies():
        return [
            remote(
                out_ref.at[pl.ds(64 * i, 64)], cur.at[pl.ds(64 * i, 64)], sem_out, i, "segment", 1 - seg
            )
            for i in range(2)
        ]

    def grad_copies():
        return [
            remote(
                grad_ref.at[pl.ds(64 * i, 64)], e.at[pl.ds(64 * i, 64)], sem_grad, i, "segment", 1 - seg
            )
            for i in range(2)
        ]

    def halo_copies(edge, halo, offset):
        return [
            remote(edge.at[0], halo.at[1], sem_h, offset, "tm", left),
            remote(edge.at[1], halo.at[0], sem_h, offset + 1, "tm", right),
        ]

    def peer_j(d):
        return group[d] % 4

    def dout_copies():
        return [
            remote(dout4.at[peer_j(d)], dout_r.at[d], sem_x, d, "tm", group[d]) for d in range(3)
        ]

    def dpre_copies():
        return [
            remote(dpre4.at[peer_j(d)], dpre_r.at[d], sem_x, 3 + d, "tm", group[d]) for d in range(3)
        ]

    mid = model // 2

    def turned_copies(part, forward=False):
        buf = a_t if part == 2 else n_t
        rows = pl.ds(mid * part if part < 2 else 0, mid)

        def one(src, dst, d):
            return remote(
                buf.at[src, rows], buf.at[dst, rows], sem_x, 6 + 3 * part + d, "tm", group[d % 2]
            )

        return [one(2, 3, 2)] if forward else [one(0, 1, 0), one(0, 2, 1)]

    def forward_turned():
        for part in range(3):
            turned_copies(part)[1].wait_recv()
            turned_copies(part, True)[0].start()

    def start_all(copies):
        for copy in copies:
            copy.start()

    def upper():
        def mask_rows(start, rows):
            d_out = (e[rows, :].astype(F32) * mask_of(start, ROWS)).astype(BF16)
            for i in range(4):
                dout4[i, rows, :] = d_out[:, 384 * i : 384 * (i + 1)]

        over_rows(mask_rows)
        d_out = jnp.concatenate([dout4[i] for i in range(4)], axis=1)
        for n in range(width // 256):
            d_act[:, 256 * n : 256 * (n + 1)] = dot_t(d_out, w2[256 * n : 256 * (n + 1), :])

    def taps_over(src, block, flip):
        cols = pl.ds(pl.multiple_of(block * LANE, LANE), LANE)
        whole = src[:, cols]
        total = jnp.zeros((frames, LANE), F32)
        for r in range(8):
            moved = whole if r == 0 else pltpu.roll(whole, whole.shape[0] - r, 0)
            for k in range(TAPS):
                if (k + 1) % 8 == r:
                    at = k + 1 - r
                    tap = TAPS - 1 - k if flip else k
                    total = total + kern[tap, :, cols] * moved[at : at + frames]
        return cols, total

    def turn_normed():
        for i in range(model // LANE):
            cols = slice(LANE * i, LANE * (i + 1))
            n_t[0, cols, :] = normed[:, cols].astype(F32).T.astype(BF16)

    def turn_act():
        for i in range(width // LANE):
            cols = slice(LANE * i, LANE * (i + 1))
            a_t[0, cols, :] = act[:, cols].astype(F32).T.astype(BF16)

    @pl.when(last_seg)
    def _():
        e[...] = gout[...]
        load_w2.wait()
        upper()

    pl.semaphore_wait(barrier, len(greet))

    @pl.when(last_seg)
    def _():
        start_all(dout_copies())
        for copy in out_copies():
            copy.wait_recv()

    @pl.when(first_seg)
    def _():
        cur[...] = inp[...]

    def norm_rows(start, rows):
        x = cur[rows, :].astype(F32)
        centred = x - jnp.mean(x, axis=-1, keepdims=True)
        rstd = lax.rsqrt(jnp.mean(centred * centred, axis=-1, keepdims=True) + EPS)
        hat = centred * rstd
        xhat[rows, :] = hat
        rstd1[rows, :] = jnp.broadcast_to(rstd, (ROWS, LANE))
        normed[rows, :] = (hat * gain1[...]).astype(BF16)

    over_rows(norm_rows)
    load_w1.wait()
    maskf = mask_of(0, frames)
    for n in range(width // 256):
        cols = slice(256 * n, 256 * (n + 1))
        q_cols = slice(width + 256 * n, width + 256 * (n + 1))
        p = dot(normed[...], w1[:, cols])
        sig = jax.nn.sigmoid(dot(normed[...], w1[:, q_cols]))
        p_buf[:, cols] = p
        sig_buf[:, cols] = sig
        gated = (p * sig * maskf).astype(BF16)
        gpad[HALO : HALO + frames, cols] = gated.astype(F32)
        edge_g[0, :, cols] = gated[:HALO]
        edge_g[1, :, cols] = gated[frames - HALO :]
    copies = halo_copies(edge_g, halo_g, 0)
    start_all(copies)
    turn_normed()
    start_all(turned_copies(0))
    for copy in copies:
        copy.wait()
    has_left = (t > 0).astype(F32)
    has_right = (t < n_tm - 1).astype(F32)
    gpad[0:HALO, :] = halo_g[0].astype(F32) * has_left
    gpad[HALO + frames :, :] = halo_g[1].astype(F32) * has_right

    def conv_block(block, carry):
        cols, total = taps_over(gpad, block, False)
        conv[:, cols] = total
        return carry

    lax.fori_loop(0, width // LANE, conv_block, 0)

    def act_rows(start, rows):
        x = conv[rows, :]
        centred = x - jnp.mean(x, axis=-1, keepdims=True)
        rstd = lax.rsqrt(jnp.mean(centred * centred, axis=-1, keepdims=True) + EPS)
        hat = centred * rstd
        zn = hat * gain2[...]
        zhat[rows, :] = hat
        zn_buf[rows, :] = zn
        rstd2[rows, :] = jnp.broadcast_to(rstd, (ROWS, LANE))
        act[rows, :] = (zn * jax.nn.sigmoid(zn)).astype(BF16)

    over_rows(act_rows)

    @pl.when(first_seg)
    def _():
        load_w2.wait()

    for n in range(model // 512):
        cols = slice(512 * n, 512 * (n + 1))
        out = dot(act[...], w2[:, cols])
        out_ref[:, cols] = (cur[:, cols].astype(F32) + maskf * out).astype(BF16)

    @pl.when(first_seg)
    def _():
        copies = out_copies()
        start_all(copies)
        store_out.start()
        turn_act()
        for copy in copies:
            copy.wait_send()
        start_all(turned_copies(1))
        start_all(turned_copies(2))
        forward_turned()
        for copy in grad_copies():
            copy.wait_recv()
        upper()

    gg1[...] = jnp.zeros_like(gg1)
    gk[...] = jnp.zeros_like(gk)

    def conv_grad_rows(start, rows):
        zn = zn_buf[rows, :]
        hat = zhat[rows, :]
        sg = jax.nn.sigmoid(zn)
        d_zn = d_act[rows, :] * (sg + zn * sg * (1.0 - sg))
        gk[TAPS : TAPS + 1, :] += jnp.sum(d_zn * hat, axis=0, keepdims=True)
        d_hat = d_zn * gain2[...]
        m_one = jnp.mean(d_hat, axis=-1, keepdims=True)
        m_two = jnp.mean(d_hat * hat, axis=-1, keepdims=True)
        d_conv = rstd2[rows, 0:1] * (d_hat - m_one - hat * m_two)
        dpad[pl.ds(HALO + start, ROWS), :] = d_conv

    over_rows(conv_grad_rows)
    edge_d[0] = dpad[HALO : 2 * HALO, :].astype(BF16)
    edge_d[1] = dpad[frames : HALO + frames, :].astype(BF16)
    copies = halo_copies(edge_d, halo_d, 2)
    start_all(copies)

    @pl.when(first_seg)
    def _():
        start_all(dout_copies())

    @pl.when(last_seg)
    def _():
        store_out.start()
        start_all(turned_copies(1))
        turn_act()
        start_all(turned_copies(2))

    def tap_grads(block, carry):
        cols = pl.ds(pl.multiple_of(block * LANE, LANE), LANE)
        whole = gpad[:, cols]
        d_conv = dpad[HALO : HALO + frames, cols]
        for r in range(8):
            moved = whole if r == 0 else pltpu.roll(whole, whole.shape[0] - r, 0)
            for k in range(TAPS):
                if (k + 1) % 8 == r:
                    at = k + 1 - r
                    gk[k : k + 1, cols] = jnp.sum(
                        moved[at : at + frames] * d_conv, axis=0, keepdims=True
                    )
        return carry

    lax.fori_loop(0, width // LANE, tap_grads, 0)
    for copy in copies:
        copy.wait()
    dpad[0:HALO, :] = halo_d[0].astype(F32) * has_left
    dpad[HALO + frames :, :] = halo_d[1].astype(F32) * has_right

    for half in range(2):

        def pre_block(block, carry):
            cols, total = taps_over(dpad, half * 3 + block, True)
            d_gated = total * maskf
            sig = sig_buf[:, cols]
            d_p = d_gated * sig
            d_q = d_p * p_buf[:, cols] * (1.0 - sig)
            part = pl.ds(pl.multiple_of(block * LANE, LANE), LANE)
            dpre4[half, :, part] = d_p.astype(BF16)
            dpre4[2 + half, :, part] = d_q.astype(BF16)
            return carry

        lax.fori_loop(0, 3, pre_block, 0)

    @pl.when(first_seg)
    def _():
        start_all(dpre_copies())

    d_pre = jnp.concatenate([dpre4[i] for i in range(4)], axis=1)
    for n in range(model // 512):
        rows = slice(512 * n, 512 * (n + 1))
        d_norm[:, rows] = dot_t(d_pre, w1[rows, :])

    def grad_rows(start, rows):
        d_normed = d_norm[rows, :]
        hat = xhat[rows, :]
        gg1[0:1, :] += jnp.sum(d_normed * hat, axis=0, keepdims=True)
        d_hat = d_normed * gain1[...]
        m_one = jnp.mean(d_hat, axis=-1, keepdims=True)
        m_two = jnp.mean(d_hat * hat, axis=-1, keepdims=True)
        d_h = rstd1[rows, 0:1] * (d_hat - m_one - hat * m_two)
        grad_ref[rows, :] = (e[rows, :].astype(F32) + d_h).astype(BF16)

    over_rows(grad_rows)

    @pl.when(last_seg)
    def _():
        copies = grad_copies()
        start_all(copies)
        forward_turned()
        for copy in copies:
            copy.wait_send()
        start_all(dpre_copies())

    store_grad.start()
    for i in range(width // LANE):
        cols = slice(LANE * i, LANE * (i + 1))
        ebuf[cols, :] = gk[:, cols].T
    for i in range(model // LANE):
        cols = slice(LANE * i, LANE * (i + 1))
        tbuf[cols, :] = jnp.broadcast_to(gg1[0:1, cols], (LANE, LANE)).T

    low, high = pl.ds(0, n_z // 2), pl.ds(n_z // 2, n_z // 2)
    up, down, far = (dy + 1) % n_y, (dy + n_y - 1) % n_y, (dy + 2) % n_y

    def y_far(buf, inner, base_sem):
        return [
            remote(buf.at[far, low], inner.at[0], sem_y, base_sem, "dp", up),
            remote(buf.at[far, high], inner.at[1], sem_y, base_sem + 1, "dp", down),
        ]

    def y_direct(buf, got, base_sem):
        return [
            remote(buf.at[up, high], got.at[0, high], sem_y, base_sem + 2, "dp", up),
            remote(buf.at[down, low], got.at[1, low], sem_y, base_sem + 3, "dp", down),
        ]

    def y_summed(buf, got, base_sem):
        return [
            remote(buf.at[up, low], got.at[0, low], sem_y, base_sem + 4, "dp", up),
            remote(buf.at[down, high], got.at[1, high], sem_y, base_sem + 5, "dp", down),
        ]

    def z_copy(buf, got, d, offset):
        peer = (z + d) % n_z
        return remote(buf.at[peer], got.at[d - 1], sem_z, offset + d - 1, "tm", peer * 4 + j)

    rows_one = model // n_y
    rows_two = width // n_y

    for copy in dout_copies() + [c for part in range(3) for c in turned_copies(part)[:1]]:
        copy.wait()
    for part in range(3):
        turned_copies(part)[1].wait_send()
        turned_copies(part, True)[0].wait()
    rhs_two = jnp.concatenate([dout4[j]] + [dout_r[d] for d in range(3)], axis=0)
    lane = lax.broadcasted_iota(jnp.int32, (24, LANE), 1)

    def part_two(peer):
        start = pl.multiple_of(peer * rows_two, rows_two)
        lhs = jnp.concatenate([a_t[i, pl.ds(start, rows_two), :] for i in range(4)], axis=1)
        part = dot(lhs, rhs_two)
        for i in range(n_z):
            at = pl.multiple_of(peer * rows_two + 24 * i, 8)
            at_t = pl.multiple_of(peer * rows_one + 48 * i, 8)
            extra = ebuf[pl.ds(at, 24), :]
            extra = jnp.where(lane == 32, tbuf[pl.ds(at_t, 24), :], extra)
            extra = jnp.where(lane == 33, tbuf[pl.ds(at_t + 24, 24), :], extra)
            mine = part[24 * i : 24 * (i + 1)]
            lower = jnp.concatenate([mine[:, 256:], extra], axis=1)
            pb[peer, i] = jnp.concatenate([mine[:, :256], lower], axis=0).astype(BF16)

    part_two(far)
    start_all(y_far(pb, yb_in, 6))
    part_two(up)
    part_two(down)
    start_all(y_direct(pb, yb, 6))
    part_two(dy)

    for copy in dpre_copies():
        copy.wait()
    rhs_one = jnp.concatenate([dpre4[j]] + [dpre_r[d] for d in range(3)], axis=0)

    def part_one(peer):
        start = pl.multiple_of(peer * rows_one, rows_one)
        lhs = jnp.concatenate([n_t[i, pl.ds(start, rows_one), :] for i in range(4)], axis=1)
        part = dot(lhs, rhs_one)
        for i in range(n_z):
            pa[peer, i] = part[48 * i : 48 * (i + 1)].astype(BF16)

    def y_relay(buf, inner, got, base_sem):
        for copy in y_far(buf, inner, base_sem):
            copy.wait()
        for i in range(n_z // 2):
            k = n_z // 2 + i
            buf[up, i] = (buf[up, i].astype(F32) + inner[0, i].astype(F32)).astype(BF16)
            buf[down, k] = (buf[down, k].astype(F32) + inner[1, i].astype(F32)).astype(BF16)
        start_all(y_summed(buf, got, base_sem))

    def y_finish(buf, got, q_buf, z_got, base_sem, z_sem):
        for copy in y_direct(buf, got, base_sem) + y_summed(buf, got, base_sem):
            copy.wait()
        for i in range(n_z):
            total = buf[dy, i].astype(F32) + got[0, i].astype(F32) + got[1, i].astype(F32)
            q_buf[i] = total.astype(BF16)
        for d in range(1, n_z):
            z_copy(q_buf, z_got, d, z_sem).start()

    part_one(far)
    start_all(y_far(pa, ya_in, 0))
    part_one(up)
    part_one(down)
    start_all(y_direct(pa, ya, 0))
    y_relay(pb, yb_in, yb, 6)
    part_one(dy)
    y_relay(pa, ya_in, ya, 0)
    y_finish(pb, yb, qb, zb, 6, n_z - 1)
    y_finish(pa, ya, qa, za, 0, 0)

    fs[...] = jnp.zeros_like(fs)
    for d in range(1, n_z):
        z_copy(qa, za, d, 0).wait()
    total = qa[z].astype(F32)
    for d in range(n_z - 1):
        total = total + za[d].astype(F32)
    for i in range(4):
        fs[i, 0:12, :] = total[12 * i : 12 * (i + 1)]
    for d in range(1, n_z):
        z_copy(qb, zb, d, n_z - 1).wait()
    total = qb[z].astype(F32)
    for d in range(n_z - 1):
        total = total + zb[d].astype(F32)
    two = jnp.concatenate([total[:24], total[24:, :LANE]], axis=1)
    extra = total[24:, LANE:]
    for i in range(4):
        fs[i, 16:22, :] = two[6 * i : 6 * (i + 1)]
        fs[i, 24:30, 0:LANE] = extra[6 * i : 6 * (i + 1)]
        for m in range(2):
            at = 12 * (i % 2) + 6 * m
            fs[i, 24:30, LANE * (m + 1) : LANE * (m + 2)] = extra[at : at + 6]
    copies = [remote(fs.at[peer_j(d)], fr.at[j], sem_f, d, "tm", group[d]) for d in range(3)]
    start_all(copies)
    fr[j] = fs[j]
    for copy in copies:
        copy.wait()
    small = jnp.zeros((8, 3 * LANE), F32)
    for i in range(4):
        cols = slice(384 * i, 384 * (i + 1))
        for row in range(12):
            o_one[row, :, cols] = fr[i, row : row + 1, :]
        for row in range(6):
            o_two[row, :, cols] = fr[i, 16 + row : 17 + row, :]
        small = small + fr[i, 24:32, :]
    for i in range(6):
        o_kern[i] = small[i : i + 1, :TAPS]
    fill = jnp.zeros((LANE - 8, LANE), F32)
    turned = [
        jnp.concatenate([small[:, LANE * m : LANE * (m + 1)], fill], axis=0).T for m in range(3)
    ]
    o_gain2[...] = turned[0][TAPS : TAPS + 1, :6]
    for m in range(2):
        pair = turned[m + 1][32:34, :6]
        o_gain1[:, 6 * m : 6 * (m + 1)] = jnp.where(j < 2, pair[0:1], pair[1:2])
    store_out.wait()
    store_grad.wait()


def hand_over(*refs):
    n = (len(refs) - 1) // 2
    sems = refs[-1]
    copies = [pltpu.make_async_copy(refs[i], refs[n + i], sems.at[i]) for i in range(n)]
    for copy in copies:
        copy.start()
    for copy in copies:
        copy.wait()


def per_device(inputs, lengths, w_first, kernel_w, gain_first, gain_second, w_second, grad_output):
    n_y = lax.axis_size("dp")
    n_tm = lax.axis_size("tm")
    n_z = n_tm // 4
    frames, model = inputs.shape[1:]
    width = w_second.shape[1]
    groups = n_y * n_tm
    vmem = pl.BlockSpec(memory_space=pltpu.VMEM)

    def buf(shape, dtype):
        return pltpu.VMEM(shape, dtype)

    wide = (frames, model)
    thin = (frames, width)
    padded = (frames + 2 * HALO, width)
    third = (4, frames, 384)
    scratch = [
        buf((model, 2 * width), BF16),
        buf((width, model), BF16),
        buf(wide, BF16),
        buf(wide, BF16),
        buf(wide, BF16),
        buf(wide, BF16),
        buf(wide, F32),
        buf((frames, LANE), F32),
        buf(wide, BF16),
        buf(thin, F32),
        buf(thin, F32),
        buf(padded, F32),
        buf(padded, F32),
        buf(thin, F32),
        buf(thin, F32),
        buf((frames, LANE), F32),
        buf(thin, F32),
        buf(thin, BF16),
        buf(thin, F32),
        buf(wide, F32),
        buf((2, HALO, width), BF16),
        buf((2, HALO, width), BF16),
        buf((2, HALO, width), BF16),
        buf((2, HALO, width), BF16),
        buf(third, BF16),
        buf(third, BF16),
        buf((3, frames, 384), BF16),
        buf((3, frames, 384), BF16),
        buf((4, model, LANE), BF16),
        buf((4, width, LANE), BF16),
        buf((LANE, width), F32),
        buf((8, model), F32),
        buf((width, LANE), F32),
        buf((model, LANE), F32),
        buf((n_y, n_z, 48, 384), BF16),
        buf((n_y, n_z, 48, 256), BF16),
        buf((2, n_z // 2, 48, 384), BF16),
        buf((2, n_z // 2, 48, 256), BF16),
        buf((2, n_z, 48, 384), BF16),
        buf((2, n_z, 48, 256), BF16),
        buf((n_z, 48, 384), BF16),
        buf((n_z, 48, 256), BF16),
        buf((n_z - 1, 48, 384), BF16),
        buf((n_z - 1, 48, 256), BF16),
        buf((4, 32, 384), F32),
        buf((4, 32, 384), F32),
        pltpu.SemaphoreType.DMA((4,)),
        pltpu.SemaphoreType.DMA((2, 4)),
        pltpu.SemaphoreType.DMA((2, 2)),
        pltpu.SemaphoreType.DMA((2, 2)),
        pltpu.SemaphoreType.DMA((2, 15)),
        pltpu.SemaphoreType.DMA((2, 12)),
        pltpu.SemaphoreType.DMA((2, 2 * (n_z - 1))),
        pltpu.SemaphoreType.DMA((2, 3)),
    ]
    hbm = pl.BlockSpec(memory_space=pl.ANY)
    shapes = (
        jax.ShapeDtypeStruct(wide, BF16),
        jax.ShapeDtypeStruct(wide, BF16),
        jax.ShapeDtypeStruct((model // groups, 1, model), F32),
        jax.ShapeDtypeStruct((width // groups, 1, model), F32),
        jax.ShapeDtypeStruct((width // groups, 1, TAPS), F32),
        jax.ShapeDtypeStruct((1, model // groups), F32),
        jax.ShapeDtypeStruct((1, width // groups), F32),
    )
    results = pl.pallas_call(
        functools.partial(kernel, n_y, n_z, n_tm),
        out_shape=shapes,
        in_specs=[pl.BlockSpec(memory_space=pltpu.SMEM), vmem, vmem, hbm, hbm, vmem, vmem, vmem],
        out_specs=(hbm, hbm) + (vmem,) * 5,
        scratch_shapes=scratch,
        compiler_params=pltpu.CompilerParams(
            collective_id=0, has_side_effects=True, vmem_limit_bytes=60 * 1024 * 1024
        ),
        cost_estimate=pl.CostEstimate(
            flops=2 * 3 * frames * model * 3 * width, bytes_accessed=12_000_000, transcendentals=0
        ),
    )(
        lengths,
        inputs[0],
        grad_output[0],
        w_first[0],
        w_second[0],
        kernel_w.transpose(1, 0, 2),
        gain_first,
        gain_second,
    )
    out, grad, one, two, taps, g_one, g_two = pl.pallas_call(
        hand_over,
        out_shape=shapes,
        in_specs=[hbm] * 7,
        out_specs=(hbm,) * 7,
        scratch_shapes=[pltpu.SemaphoreType.DMA((7,))],
        compiler_params=pltpu.CompilerParams(vmem_limit_bytes=60 * 1024 * 1024),
    )(*results)
    return (
        out[None, None],
        grad[None, None],
        one.transpose(1, 0, 2),
        taps.transpose(1, 2, 0),
        g_one,
        g_two,
        two.transpose(1, 0, 2),
    )


def solution(mesh):
    in_specs = (
        P("dp", "tm", None),
        P("dp"),
        P("segment", None, None),
        P("segment", None, None),
        P("segment", None),
        P("segment", None),
        P("segment", None, None),
        P("dp", "tm", None),
    )
    out_specs = (
        P("segment", "dp", "tm", None),
        P("segment", "dp", "tm", None),
        P("segment", ("dp", "tm"), None),
        P("segment", None, ("dp", "tm")),
        P("segment", ("dp", "tm")),
        P("segment", ("dp", "tm")),
        P("segment", ("dp", "tm"), None),
    )
    return jax.shard_map(
        per_device, mesh=mesh, in_specs=in_specs, out_specs=out_specs, check_vma=False
    )
```

```python
import functools

import jax
import jax.numpy as jnp
from jax import lax
from jax.experimental import pallas as pl
from jax.experimental.pallas import tpu as pltpu
from jax.sharding import PartitionSpec as P

EPS = 1e-05
F32 = jnp.float32
BF16 = jnp.bfloat16
MESH = pl.DeviceIdType.MESH
NT = (((1,), (1,)), ((), ()))
HALO = 16
TAPS = 31
LANE = 128
ROWS = 32


def dot(a, b):
    return jnp.dot(a, b, preferred_element_type=F32)


def dot_t(a, b):
    return lax.dot_general(a, b, NT, preferred_element_type=F32)


def kernel(
    n_y,
    n_z,
    n_tm,
    len_ref,
    inp,
    gout,
    w1_hbm,
    w2_hbm,
    kern,
    gain1,
    gain2,
    out_hbm,
    grad_hbm,
    o_one,
    o_two,
    o_kern,
    o_gain1,
    o_gain2,
    w1,
    w2,
    out_ref,
    grad_ref,
    cur,
    e,
    xhat,
    rstd1,
    normed,
    p_buf,
    sig_buf,
    gpad,
    dpad,
    conv,
    zhat,
    rstd2,
    zn_buf,
    act,
    d_act,
    d_norm,
    edge_g,
    edge_d,
    halo_g,
    halo_d,
    dout4,
    dpre4,
    dout_r,
    dpre_r,
    n_t,
    a_t,
    gk,
    gg1,
    ebuf,
    tbuf,
    pa,
    pb,
    ya_in,
    yb_in,
    ya,
    yb,
    qa,
    qb,
    za,
    zb,
    fs,
    fr,
    sem_w,
    sem_h,
    sem_out,
    sem_grad,
    sem_x,
    sem_y,
    sem_z,
    sem_f,
):
    frames, model = inp.shape
    width = w2.shape[0]
    dy = lax.axis_index("dp")
    seg = lax.axis_index("segment")
    t = lax.axis_index("tm")
    c = t % 2
    xl = (t // 2) % 2
    z = t // 4
    j = t % 4
    base = z * 4
    group = [base + xl * 2 + (1 - c), base + (1 - xl) * 2 + c, base + (1 - xl) * 2 + (1 - c)]
    right = (t + 1) % n_tm
    left = (t + n_tm - 1) % n_tm
    first_seg = seg == 0
    last_seg = seg == 1

    def remote(src, dst, sems, index, axis, peer):
        return pltpu.make_async_remote_copy(
            src_ref=src,
            dst_ref=dst,
            send_sem=sems.at[0, index],
            recv_sem=sems.at[1, index],
            device_id={axis: peer},
            device_id_type=MESH,
        )

    load_w1 = pltpu.make_async_copy(w1_hbm, w1, sem_w.at[0])
    load_w2 = pltpu.make_async_copy(w2_hbm, w2, sem_w.at[1])
    store_out = pltpu.make_async_copy(out_ref, out_hbm, sem_w.at[2])
    store_grad = pltpu.make_async_copy(grad_ref, grad_hbm, sem_w.at[3])
    barrier = pltpu.get_barrier_semaphore()
    greet = [("tm", left), ("tm", right), ("segment", 1 - seg)]
    greet += [("tm", g) for g in group]
    greet += [("dp", (dy + d) % n_y) for d in range(1, n_y)]
    greet += [("tm", ((z + d) % n_z) * 4 + j) for d in range(1, n_z)]
    for axis, peer in greet:
        pl.semaphore_signal(barrier, inc=1, device_id={axis: peer}, device_id_type=MESH)

    @pl.when(first_seg)
    def _():
        load_w1.start()
        load_w2.start()

    @pl.when(last_seg)
    def _():
        load_w2.start()
        load_w1.start()

    length = len_ref[0]

    def mask_of(start, rows):
        ids = t * frames + start + lax.broadcasted_iota(jnp.int32, (rows, 1), 0)
        return (ids < length).astype(F32)

    def over_rows(work):
        def step(i, carry):
            start = pl.multiple_of(i * ROWS, ROWS)
            work(start, pl.ds(start, ROWS))
            return carry

        lax.fori_loop(0, frames // ROWS, step, 0)

    def out_copies():
        return [
            remote(
                out_ref.at[pl.ds(64 * i, 64)], cur.at[pl.ds(64 * i, 64)], sem_out, i, "segment", 1 - seg
            )
            for i in range(2)
        ]

    def grad_copies():
        return [
            remote(
                grad_ref.at[pl.ds(64 * i, 64)], e.at[pl.ds(64 * i, 64)], sem_grad, i, "segment", 1 - seg
            )
            for i in range(2)
        ]

    def halo_copies(edge, halo, offset):
        return [
            remote(edge.at[0], halo.at[1], sem_h, offset, "tm", left),
            remote(edge.at[1], halo.at[0], sem_h, offset + 1, "tm", right),
        ]

    def peer_j(d):
        return group[d] % 4

    def dout_copies():
        return [
            remote(dout4.at[peer_j(d)], dout_r.at[d], sem_x, d, "tm", group[d]) for d in range(3)
        ]

    def dpre_copies():
        return [
            remote(dpre4.at[peer_j(d)], dpre_r.at[d], sem_x, 3 + d, "tm", group[d]) for d in range(3)
        ]

    mid = model // 2

    def turned_copies(part, forward=False):
        buf = a_t if part == 2 else n_t
        rows = pl.ds(mid * part if part < 2 else 0, mid)

        def one(src, dst, d):
            return remote(
                buf.at[src, rows], buf.at[dst, rows], sem_x, 6 + 3 * part + d, "tm", group[d % 2]
            )

        return [one(2, 3, 2)] if forward else [one(0, 1, 0), one(0, 2, 1)]

    def forward_turned():
        for part in range(3):
            turned_copies(part)[1].wait_recv()
            turned_copies(part, True)[0].start()

    def start_all(copies):
        for copy in copies:
            copy.start()

    def upper():
        def mask_rows(start, rows):
            d_out = (e[rows, :].astype(F32) * mask_of(start, ROWS)).astype(BF16)
            for i in range(4):
                dout4[i, rows, :] = d_out[:, 384 * i : 384 * (i + 1)]

        over_rows(mask_rows)
        d_out = jnp.concatenate([dout4[i] for i in range(4)], axis=1)
        for n in range(width // 256):
            d_act[:, 256 * n : 256 * (n + 1)] = dot_t(d_out, w2[256 * n : 256 * (n + 1), :])

    def taps_over(src, block, flip):
        cols = pl.ds(pl.multiple_of(block * LANE, LANE), LANE)
        whole = src[:, cols]
        total = jnp.zeros((frames, LANE), F32)
        for r in range(8):
            moved = whole if r == 0 else pltpu.roll(whole, whole.shape[0] - r, 0)
            for k in range(TAPS):
                if (k + 1) % 8 == r:
                    at = k + 1 - r
                    tap = TAPS - 1 - k if flip else k
                    total = total + kern[tap, :, cols] * moved[at : at + frames]
        return cols, total

    def turn_normed():
        for i in range(model // LANE):
            cols = slice(LANE * i, LANE * (i + 1))
            n_t[0, cols, :] = normed[:, cols].astype(F32).T.astype(BF16)

    def turn_act():
        for i in range(width // LANE):
            cols = slice(LANE * i, LANE * (i + 1))
            a_t[0, cols, :] = act[:, cols].astype(F32).T.astype(BF16)

    @pl.when(last_seg)
    def _():
        e[...] = gout[...]
        load_w2.wait()
        upper()

    pl.semaphore_wait(barrier, len(greet))

    @pl.when(last_seg)
    def _():
        start_all(dout_copies())
        for copy in out_copies():
            copy.wait_recv()

    @pl.when(first_seg)
    def _():
        cur[...] = inp[...]

    def norm_rows(start, rows):
        x = cur[rows, :].astype(F32)
        centred = x - jnp.mean(x, axis=-1, keepdims=True)
        rstd = lax.rsqrt(jnp.mean(centred * centred, axis=-1, keepdims=True) + EPS)
        hat = centred * rstd
        xhat[rows, :] = hat
        rstd1[rows, :] = jnp.broadcast_to(rstd, (ROWS, LANE))
        normed[rows, :] = (hat * gain1[...]).astype(BF16)

    over_rows(norm_rows)
    load_w1.wait()
    maskf = mask_of(0, frames)
    for n in range(width // 256):
        cols = slice(256 * n, 256 * (n + 1))
        q_cols = slice(width + 256 * n, width + 256 * (n + 1))
        p = dot(normed[...], w1[:, cols])
        sig = jax.nn.sigmoid(dot(normed[...], w1[:, q_cols]))
        p_buf[:, cols] = p
        sig_buf[:, cols] = sig
        gated = (p * sig * maskf).astype(BF16)
        gpad[HALO : HALO + frames, cols] = gated.astype(F32)
        edge_g[0, :, cols] = gated[:HALO]
        edge_g[1, :, cols] = gated[frames - HALO :]
    copies = halo_copies(edge_g, halo_g, 0)
    start_all(copies)
    turn_normed()
    start_all(turned_copies(0))
    for copy in copies:
        copy.wait()
    has_left = (t > 0).astype(F32)
    has_right = (t < n_tm - 1).astype(F32)
    gpad[0:HALO, :] = halo_g[0].astype(F32) * has_left
    gpad[HALO + frames :, :] = halo_g[1].astype(F32) * has_right

    def conv_block(block, carry):
        cols, total = taps_over(gpad, block, False)
        conv[:, cols] = total
        return carry

    lax.fori_loop(0, width // LANE, conv_block, 0)

    def act_rows(start, rows):
        x = conv[rows, :]
        centred = x - jnp.mean(x, axis=-1, keepdims=True)
        rstd = lax.rsqrt(jnp.mean(centred * centred, axis=-1, keepdims=True) + EPS)
        hat = centred * rstd
        zn = hat * gain2[...]
        zhat[rows, :] = hat
        zn_buf[rows, :] = zn
        rstd2[rows, :] = jnp.broadcast_to(rstd, (ROWS, LANE))
        act[rows, :] = (zn * jax.nn.sigmoid(zn)).astype(BF16)

    over_rows(act_rows)

    @pl.when(first_seg)
    def _():
        load_w2.wait()

    for n in range(model // 512):
        cols = slice(512 * n, 512 * (n + 1))
        out = dot(act[...], w2[:, cols])
        out_ref[:, cols] = (cur[:, cols].astype(F32) + maskf * out).astype(BF16)

    @pl.when(first_seg)
    def _():
        copies = out_copies()
        start_all(copies)
        store_out.start()
        turn_act()
        for copy in copies:
            copy.wait_send()
        start_all(turned_copies(1))
        start_all(turned_copies(2))
        forward_turned()
        for copy in grad_copies():
            copy.wait_recv()
        upper()

    gg1[...] = jnp.zeros_like(gg1)
    gk[...] = jnp.zeros_like(gk)

    def conv_grad_rows(start, rows):
        zn = zn_buf[rows, :]
        hat = zhat[rows, :]
        sg = jax.nn.sigmoid(zn)
        d_zn = d_act[rows, :] * (sg + zn * sg * (1.0 - sg))
        gk[TAPS : TAPS + 1, :] += jnp.sum(d_zn * hat, axis=0, keepdims=True)
        d_hat = d_zn * gain2[...]
        m_one = jnp.mean(d_hat, axis=-1, keepdims=True)
        m_two = jnp.mean(d_hat * hat, axis=-1, keepdims=True)
        d_conv = rstd2[rows, 0:1] * (d_hat - m_one - hat * m_two)
        dpad[pl.ds(HALO + start, ROWS), :] = d_conv

    over_rows(conv_grad_rows)
    edge_d[0] = dpad[HALO : 2 * HALO, :].astype(BF16)
    edge_d[1] = dpad[frames : HALO + frames, :].astype(BF16)
    copies = halo_copies(edge_d, halo_d, 2)
    start_all(copies)

    @pl.when(first_seg)
    def _():
        start_all(dout_copies())

    @pl.when(last_seg)
    def _():
        store_out.start()
        start_all(turned_copies(1))
        turn_act()
        start_all(turned_copies(2))

    def tap_grads(block, carry):
        cols = pl.ds(pl.multiple_of(block * LANE, LANE), LANE)
        whole = gpad[:, cols]
        d_conv = dpad[HALO : HALO + frames, cols]
        for r in range(8):
            moved = whole if r == 0 else pltpu.roll(whole, whole.shape[0] - r, 0)
            for k in range(TAPS):
                if (k + 1) % 8 == r:
                    at = k + 1 - r
                    gk[k : k + 1, cols] = jnp.sum(
                        moved[at : at + frames] * d_conv, axis=0, keepdims=True
                    )
        return carry

    lax.fori_loop(0, width // LANE, tap_grads, 0)
    for copy in copies:
        copy.wait()
    dpad[0:HALO, :] = halo_d[0].astype(F32) * has_left
    dpad[HALO + frames :, :] = halo_d[1].astype(F32) * has_right

    for half in range(2):

        def pre_block(block, carry):
            cols, total = taps_over(dpad, half * 3 + block, True)
            d_gated = total * maskf
            sig = sig_buf[:, cols]
            d_p = d_gated * sig
            d_q = d_p * p_buf[:, cols] * (1.0 - sig)
            part = pl.ds(pl.multiple_of(block * LANE, LANE), LANE)
            dpre4[half, :, part] = d_p.astype(BF16)
            dpre4[2 + half, :, part] = d_q.astype(BF16)
            return carry

        lax.fori_loop(0, 3, pre_block, 0)

    @pl.when(first_seg)
    def _():
        start_all(dpre_copies())

    d_pre = jnp.concatenate([dpre4[i] for i in range(4)], axis=1)
    for n in range(model // 512):
        rows = slice(512 * n, 512 * (n + 1))
        d_norm[:, rows] = dot_t(d_pre, w1[rows, :])

    def grad_rows(start, rows):
        d_normed = d_norm[rows, :]
        hat = xhat[rows, :]
        gg1[0:1, :] += jnp.sum(d_normed * hat, axis=0, keepdims=True)
        d_hat = d_normed * gain1[...]
        m_one = jnp.mean(d_hat, axis=-1, keepdims=True)
        m_two = jnp.mean(d_hat * hat, axis=-1, keepdims=True)
        d_h = rstd1[rows, 0:1] * (d_hat - m_one - hat * m_two)
        grad_ref[rows, :] = (e[rows, :].astype(F32) + d_h).astype(BF16)

    over_rows(grad_rows)

    @pl.when(last_seg)
    def _():
        copies = grad_copies()
        start_all(copies)
        forward_turned()
        for copy in copies:
            copy.wait_send()
        start_all(dpre_copies())

    store_grad.start()
    for i in range(width // LANE):
        cols = slice(LANE * i, LANE * (i + 1))
        ebuf[cols, :] = gk[:, cols].T
    for i in range(model // LANE):
        cols = slice(LANE * i, LANE * (i + 1))
        tbuf[cols, :] = jnp.broadcast_to(gg1[0:1, cols], (LANE, LANE)).T

    low, high = pl.ds(0, n_z // 2), pl.ds(n_z // 2, n_z // 2)
    up, down, far = (dy + 1) % n_y, (dy + n_y - 1) % n_y, (dy + 2) % n_y

    def y_far(buf, inner, base_sem):
        return [
            remote(buf.at[far, low], inner.at[0], sem_y, base_sem, "dp", up),
            remote(buf.at[far, high], inner.at[1], sem_y, base_sem + 1, "dp", down),
        ]

    def y_direct(buf, got, base_sem):
        return [
            remote(buf.at[up, high], got.at[0, high], sem_y, base_sem + 2, "dp", up),
            remote(buf.at[down, low], got.at[1, low], sem_y, base_sem + 3, "dp", down),
        ]

    def y_summed(buf, got, base_sem):
        return [
            remote(buf.at[up, low], got.at[0, low], sem_y, base_sem + 4, "dp", up),
            remote(buf.at[down, high], got.at[1, high], sem_y, base_sem + 5, "dp", down),
        ]

    def z_copy(buf, got, d, offset):
        peer = (z + d) % n_z
        return remote(buf.at[peer], got.at[d - 1], sem_z, offset + d - 1, "tm", peer * 4 + j)

    rows_one = model // n_y
    rows_two = width // n_y

    for copy in dout_copies() + [c for part in range(3) for c in turned_copies(part)[:1]]:
        copy.wait()
    for part in range(3):
        turned_copies(part)[1].wait_send()
        turned_copies(part, True)[0].wait()
    rhs_two = jnp.concatenate([dout4[j]] + [dout_r[d] for d in range(3)], axis=0)
    lane = lax.broadcasted_iota(jnp.int32, (24, LANE), 1)

    def part_two(peer):
        start = pl.multiple_of(peer * rows_two, rows_two)
        lhs = jnp.concatenate([a_t[i, pl.ds(start, rows_two), :] for i in range(4)], axis=1)
        part = dot(lhs, rhs_two)
        for i in range(n_z):
            at = pl.multiple_of(peer * rows_two + 24 * i, 8)
            at_t = pl.multiple_of(peer * rows_one + 48 * i, 8)
            extra = ebuf[pl.ds(at, 24), :]
            extra = jnp.where(lane == 32, tbuf[pl.ds(at_t, 24), :], extra)
            extra = jnp.where(lane == 33, tbuf[pl.ds(at_t + 24, 24), :], extra)
            mine = part[24 * i : 24 * (i + 1)]
            lower = jnp.concatenate([mine[:, 256:], extra], axis=1)
            pb[peer, i] = jnp.concatenate([mine[:, :256], lower], axis=0).astype(BF16)

    part_two(far)
    start_all(y_far(pb, yb_in, 6))
    part_two(up)
    part_two(down)
    start_all(y_direct(pb, yb, 6))
    part_two(dy)

    for copy in dpre_copies():
        copy.wait()
    rhs_one = jnp.concatenate([dpre4[j]] + [dpre_r[d] for d in range(3)], axis=0)

    def part_one(peer):
        start = pl.multiple_of(peer * rows_one, rows_one)
        lhs = jnp.concatenate([n_t[i, pl.ds(start, rows_one), :] for i in range(4)], axis=1)
        part = dot(lhs, rhs_one)
        for i in range(n_z):
            pa[peer, i] = part[48 * i : 48 * (i + 1)].astype(BF16)

    def y_relay(buf, inner, got, base_sem):
        for copy in y_far(buf, inner, base_sem):
            copy.wait()
        for i in range(n_z // 2):
            k = n_z // 2 + i
            buf[up, i] = (buf[up, i].astype(F32) + inner[0, i].astype(F32)).astype(BF16)
            buf[down, k] = (buf[down, k].astype(F32) + inner[1, i].astype(F32)).astype(BF16)
        start_all(y_summed(buf, got, base_sem))

    def y_finish(buf, got, q_buf, z_got, base_sem, z_sem):
        for copy in y_direct(buf, got, base_sem) + y_summed(buf, got, base_sem):
            copy.wait()
        for i in range(n_z):
            total = buf[dy, i].astype(F32) + got[0, i].astype(F32) + got[1, i].astype(F32)
            q_buf[i] = total.astype(BF16)
        for d in range(1, n_z):
            z_copy(q_buf, z_got, d, z_sem).start()

    part_one(far)
    start_all(y_far(pa, ya_in, 0))
    part_one(up)
    part_one(down)
    start_all(y_direct(pa, ya, 0))
    y_relay(pb, yb_in, yb, 6)
    part_one(dy)
    y_relay(pa, ya_in, ya, 0)
    y_finish(pb, yb, qb, zb, 6, n_z - 1)
    y_finish(pa, ya, qa, za, 0, 0)

    fs[...] = jnp.zeros_like(fs)
    for d in range(1, n_z):
        z_copy(qa, za, d, 0).wait()
    total = qa[z].astype(F32)
    for d in range(n_z - 1):
        total = total + za[d].astype(F32)
    for i in range(4):
        fs[i, 0:12, :] = total[12 * i : 12 * (i + 1)]
    for d in range(1, n_z):
        z_copy(qb, zb, d, n_z - 1).wait()
    total = qb[z].astype(F32)
    for d in range(n_z - 1):
        total = total + zb[d].astype(F32)
    two = jnp.concatenate([total[:24], total[24:, :LANE]], axis=1)
    extra = total[24:, LANE:]
    for i in range(4):
        fs[i, 16:22, :] = two[6 * i : 6 * (i + 1)]
        fs[i, 24:30, 0:LANE] = extra[6 * i : 6 * (i + 1)]
        for m in range(2):
            at = 12 * (i % 2) + 6 * m
            fs[i, 24:30, LANE * (m + 1) : LANE * (m + 2)] = extra[at : at + 6]
    copies = [remote(fs.at[peer_j(d)], fr.at[j], sem_f, d, "tm", group[d]) for d in range(3)]
    start_all(copies)
    fr[j] = fs[j]
    for copy in copies:
        copy.wait()
    small = jnp.zeros((8, 3 * LANE), F32)
    for i in range(4):
        cols = slice(384 * i, 384 * (i + 1))
        for row in range(12):
            o_one[row, :, cols] = fr[i, row : row + 1, :]
        for row in range(6):
            o_two[row, :, cols] = fr[i, 16 + row : 17 + row, :]
        small = small + fr[i, 24:32, :]
    for i in range(6):
        o_kern[i] = small[i : i + 1, :TAPS]
    fill = jnp.zeros((LANE - 8, LANE), F32)
    turned = [
        jnp.concatenate([small[:, LANE * m : LANE * (m + 1)], fill], axis=0).T for m in range(3)
    ]
    o_gain2[...] = turned[0][TAPS : TAPS + 1, :6]
    for m in range(2):
        pair = turned[m + 1][32:34, :6]
        o_gain1[:, 6 * m : 6 * (m + 1)] = jnp.where(j < 2, pair[0:1], pair[1:2])
    store_out.wait()
    store_grad.wait()


def hand_over(*refs):
    n = len(refs) // 2
    for i in range(n):
        refs[n + i][...] = refs[i][...]


def per_device(inputs, lengths, w_first, kernel_w, gain_first, gain_second, w_second, grad_output):
    n_y = lax.axis_size("dp")
    n_tm = lax.axis_size("tm")
    n_z = n_tm // 4
    frames, model = inputs.shape[1:]
    width = w_second.shape[1]
    groups = n_y * n_tm
    vmem = pl.BlockSpec(memory_space=pltpu.VMEM)

    def buf(shape, dtype):
        return pltpu.VMEM(shape, dtype)

    wide = (frames, model)
    thin = (frames, width)
    padded = (frames + 2 * HALO, width)
    third = (4, frames, 384)
    scratch = [
        buf((model, 2 * width), BF16),
        buf((width, model), BF16),
        buf(wide, BF16),
        buf(wide, BF16),
        buf(wide, BF16),
        buf(wide, BF16),
        buf(wide, F32),
        buf((frames, LANE), F32),
        buf(wide, BF16),
        buf(thin, F32),
        buf(thin, F32),
        buf(padded, F32),
        buf(padded, F32),
        buf(thin, F32),
        buf(thin, F32),
        buf((frames, LANE), F32),
        buf(thin, F32),
        buf(thin, BF16),
        buf(thin, F32),
        buf(wide, F32),
        buf((2, HALO, width), BF16),
        buf((2, HALO, width), BF16),
        buf((2, HALO, width), BF16),
        buf((2, HALO, width), BF16),
        buf(third, BF16),
        buf(third, BF16),
        buf((3, frames, 384), BF16),
        buf((3, frames, 384), BF16),
        buf((4, model, LANE), BF16),
        buf((4, width, LANE), BF16),
        buf((LANE, width), F32),
        buf((8, model), F32),
        buf((width, LANE), F32),
        buf((model, LANE), F32),
        buf((n_y, n_z, 48, 384), BF16),
        buf((n_y, n_z, 48, 256), BF16),
        buf((2, n_z // 2, 48, 384), BF16),
        buf((2, n_z // 2, 48, 256), BF16),
        buf((2, n_z, 48, 384), BF16),
        buf((2, n_z, 48, 256), BF16),
        buf((n_z, 48, 384), BF16),
        buf((n_z, 48, 256), BF16),
        buf((n_z - 1, 48, 384), BF16),
        buf((n_z - 1, 48, 256), BF16),
        buf((4, 32, 384), F32),
        buf((4, 32, 384), F32),
        pltpu.SemaphoreType.DMA((4,)),
        pltpu.SemaphoreType.DMA((2, 4)),
        pltpu.SemaphoreType.DMA((2, 2)),
        pltpu.SemaphoreType.DMA((2, 2)),
        pltpu.SemaphoreType.DMA((2, 15)),
        pltpu.SemaphoreType.DMA((2, 12)),
        pltpu.SemaphoreType.DMA((2, 2 * (n_z - 1))),
        pltpu.SemaphoreType.DMA((2, 3)),
    ]
    hbm = pl.BlockSpec(memory_space=pl.ANY)
    shapes = (
        jax.ShapeDtypeStruct(wide, BF16),
        jax.ShapeDtypeStruct(wide, BF16),
        jax.ShapeDtypeStruct((model // groups, 1, model), F32),
        jax.ShapeDtypeStruct((width // groups, 1, model), F32),
        jax.ShapeDtypeStruct((width // groups, 1, TAPS), F32),
        jax.ShapeDtypeStruct((1, model // groups), F32),
        jax.ShapeDtypeStruct((1, width // groups), F32),
    )
    results = pl.pallas_call(
        functools.partial(kernel, n_y, n_z, n_tm),
        out_shape=shapes,
        in_specs=[pl.BlockSpec(memory_space=pltpu.SMEM), vmem, vmem, hbm, hbm, vmem, vmem, vmem],
        out_specs=(hbm, hbm) + (vmem,) * 5,
        scratch_shapes=scratch,
        compiler_params=pltpu.CompilerParams(
            collective_id=0, has_side_effects=True, vmem_limit_bytes=60 * 1024 * 1024
        ),
        cost_estimate=pl.CostEstimate(
            flops=2 * 3 * frames * model * 3 * width, bytes_accessed=12_000_000, transcendentals=0
        ),
    )(
        lengths,
        inputs[0],
        grad_output[0],
        w_first[0],
        w_second[0],
        kernel_w.transpose(1, 0, 2),
        gain_first,
        gain_second,
    )
    out, grad, one, two, taps, g_one, g_two = pl.pallas_call(
        hand_over,
        out_shape=shapes,
        in_specs=[vmem] * 7,
        out_specs=(vmem,) * 7,
        compiler_params=pltpu.CompilerParams(vmem_limit_bytes=60 * 1024 * 1024),
    )(*results)
    return (
        out[None, None],
        grad[None, None],
        one.transpose(1, 0, 2),
        taps.transpose(1, 2, 0),
        g_one,
        g_two,
        two.transpose(1, 0, 2),
    )


def solution(mesh):
    in_specs = (
        P("dp", "tm", None),
        P("dp"),
        P("segment", None, None),
        P("segment", None, None),
        P("segment", None),
        P("segment", None),
        P("segment", None, None),
        P("dp", "tm", None),
    )
    out_specs = (
        P("segment", "dp", "tm", None),
        P("segment", "dp", "tm", None),
        P("segment", ("dp", "tm"), None),
        P("segment", None, ("dp", "tm")),
        P("segment", ("dp", "tm")),
        P("segment", ("dp", "tm")),
        P("segment", ("dp", "tm"), None),
    )
    return jax.shard_map(
        per_device, mesh=mesh, in_specs=in_specs, out_specs=out_specs, check_vma=False
    )
```

```python
import functools

import jax
import jax.numpy as jnp
from jax import lax
from jax.experimental import pallas as pl
from jax.experimental.pallas import tpu as pltpu
from jax.sharding import PartitionSpec as P

EPS = 1e-05
F32 = jnp.float32
BF16 = jnp.bfloat16
MESH = pl.DeviceIdType.MESH
NT = (((1,), (1,)), ((), ()))
HALO = 16
TAPS = 31
LANE = 128
ROWS = 32
EDGES = ((0, 16), (112, 16))
MIDDLE = ((16, 48), (64, 48))
EVERY = EDGES + MIDDLE


def chunk_rows(chunk):
    return [(EVERY.index(part), pl.ds(*part)) for part in chunk]


def dot(a, b):
    return jnp.dot(a, b, preferred_element_type=F32)


def dot_t(a, b):
    return lax.dot_general(a, b, NT, preferred_element_type=F32)


def kernel(
    n_y,
    n_z,
    n_tm,
    len_ref,
    inp,
    gout,
    w1_hbm,
    w2_hbm,
    kern,
    gain1,
    gain2,
    out_hbm,
    grad_hbm,
    o_one,
    o_two,
    o_kern,
    o_gain1,
    o_gain2,
    w1,
    w2,
    out_ref,
    grad_ref,
    cur,
    e,
    xhat,
    rstd1,
    normed,
    p_buf,
    sig_buf,
    gpad,
    dpad,
    conv,
    zhat,
    rstd2,
    zn_buf,
    act,
    d_act,
    d_norm,
    edge_g,
    edge_d,
    halo_g,
    halo_d,
    dout4,
    dpre4,
    dout_r,
    dpre_r,
    n_raw,
    a_raw,
    n_t,
    a_t,
    gk,
    gg1,
    ebuf,
    tbuf,
    item_a,
    item_b,
    item_c,
    qy,
    y_got,
    fs,
    fr,
    sem_w,
    sem_h,
    sem_out,
    sem_grad,
    sem_x,
    sem_y,
    sem_z,
    sem_f,
):
    frames, model = inp.shape
    width = w2.shape[0]
    dy = lax.axis_index("dp")
    seg = lax.axis_index("segment")
    t = lax.axis_index("tm")
    c = t % 2
    xl = (t // 2) % 2
    z = t // 4
    j = t % 4
    base = z * 4
    group = [base + xl * 2 + (1 - c), base + (1 - xl) * 2 + c, base + (1 - xl) * 2 + (1 - c)]
    right = (t + 1) % n_tm
    left = (t + n_tm - 1) % n_tm
    first_seg = seg == 0
    last_seg = seg == 1

    def remote(src, dst, sems, index, axis, peer):
        return pltpu.make_async_remote_copy(
            src_ref=src,
            dst_ref=dst,
            send_sem=sems.at[0, index],
            recv_sem=sems.at[1, index],
            device_id={axis: peer},
            device_id_type=MESH,
        )

    load_w1 = pltpu.make_async_copy(w1_hbm, w1, sem_w.at[0])
    load_w2 = pltpu.make_async_copy(w2_hbm, w2, sem_w.at[1])
    store_out = pltpu.make_async_copy(out_ref, out_hbm, sem_w.at[2])
    store_grad = pltpu.make_async_copy(grad_ref, grad_hbm, sem_w.at[3])
    barrier = pltpu.get_barrier_semaphore()
    greet = [("tm", left), ("tm", right), ("segment", 1 - seg)]
    greet += [("tm", g) for g in group]
    greet += [("dp", (dy + d) % n_y) for d in range(1, n_y)]
    greet += [("tm", ((z + d) % n_z) * 4 + j) for d in (1, 2, n_z - 1, n_z - 2)]
    for axis, peer in greet:
        pl.semaphore_signal(barrier, inc=1, device_id={axis: peer}, device_id_type=MESH)

    @pl.when(first_seg)
    def _():
        load_w1.start()
        load_w2.start()

    @pl.when(last_seg)
    def _():
        load_w2.start()
        load_w1.start()

    length = len_ref[0]

    def mask_of(start, rows):
        ids = t * frames + start + lax.broadcasted_iota(jnp.int32, (rows, 1), 0)
        return (ids < length).astype(F32)

    def out_copies(chunk):
        return [
            remote(out_ref.at[rows], cur.at[rows], sem_out, i, "segment", 1 - seg)
            for i, rows in chunk_rows(chunk)
        ]

    def grad_copies(chunk):
        return [
            remote(grad_ref.at[rows], e.at[rows], sem_grad, i, "segment", 1 - seg)
            for i, rows in chunk_rows(chunk)
        ]

    def halo_copies(edge, halo, offset):
        return [
            remote(edge.at[0], halo.at[1], sem_h, offset, "tm", left),
            remote(edge.at[1], halo.at[0], sem_h, offset + 1, "tm", right),
        ]

    def peer_j(d):
        return group[d] % 4

    def dout_copies(chunk):
        return [
            remote(
                dout4.at[peer_j(d), rows], dout_r.at[d, rows], sem_x, 3 * i + d, "tm", group[d]
            )
            for i, rows in chunk_rows(chunk)
            for d in range(3)
        ]

    def dpre_copies():
        return [
            remote(dpre4.at[peer_j(d)], dpre_r.at[d], sem_x, 12 + d, "tm", group[d]) for d in range(3)
        ]

    def turned_copies(part, forward=False):
        own, got = (act, a_raw) if part == 2 else (normed, n_raw)
        rows = pl.ds(0, frames) if part == 2 else pl.ds(frames // 2 * part, frames // 2)

        def one(src, dst, d):
            return remote(
                src.at[rows], got.at[dst, rows], sem_x, 15 + 3 * part + d, "tm", group[d % 2]
            )

        return [one(got.at[1], 2, 2)] if forward else [one(own, 0, 0), one(own, 1, 1)]

    def forward_turned(parts):
        for part in parts:
            turned_copies(part)[1].wait_recv()
            turned_copies(part, True)[0].start()

    def wait_turned(parts):
        for part in parts:
            copies = turned_copies(part)
            copies[0].wait()
            copies[1].wait_send()
            turned_copies(part, True)[0].wait()

    def start_all(copies):
        for copy in copies:
            copy.start()

    def stacked(ref, chunk):
        return jnp.concatenate([ref[start : start + size] for start, size in chunk], axis=0)

    def spread(value, chunk):
        at = 0
        for start, size in chunk:
            yield slice(start, start + size), value[at : at + size]
            at += size

    def pieces(chunk):
        return [(at, min(ROWS, start + size - at)) for start, size in chunk for at in range(start, start + size, ROWS)]

    def upper(chunk):
        for start, size in pieces(chunk):
            rows = slice(start, start + size)
            d_out = (e[rows, :].astype(F32) * mask_of(start, size)).astype(BF16)
            for i in range(4):
                dout4[i, rows, :] = d_out[:, 384 * i : 384 * (i + 1)]
        d_out = jnp.concatenate([stacked(dout4.at[i], chunk) for i in range(4)], axis=1)
        for n in range(width // 256):
            cols = slice(256 * n, 256 * (n + 1))
            for rows, value in spread(dot_t(d_out, w2[cols, :]), chunk):
                d_act[rows, cols] = value

    def taps_over(src, block, flip):
        cols = pl.ds(pl.multiple_of(block * LANE, LANE), LANE)
        whole = src[:, cols]
        total = jnp.zeros((frames, LANE), F32)
        for r in range(8):
            moved = whole if r == 0 else pltpu.roll(whole, whole.shape[0] - r, 0)
            for k in range(TAPS):
                if (k + 1) % 8 == r:
                    at = k + 1 - r
                    tap = TAPS - 1 - k if flip else k
                    total = total + kern[tap, :, cols] * moved[at : at + frames]
        return cols, total

    def turn(slots):
        for slot in slots:
            n_src = normed if slot == 0 else n_raw.at[slot - 1]
            a_src = act if slot == 0 else a_raw.at[slot - 1]
            for i in range(model // LANE):
                cols = slice(LANE * i, LANE * (i + 1))
                n_t[slot, cols, :] = n_src[:, cols].T
            for i in range(width // LANE):
                cols = slice(LANE * i, LANE * (i + 1))
                a_t[slot, cols, :] = a_src[:, cols].T

    gg1[...] = jnp.zeros_like(gg1)
    gk[...] = jnp.zeros_like(gk)

    @pl.when(last_seg)
    def _():
        e[...] = gout[...]
        load_w2.wait()
        upper(EVERY)

    @pl.when(first_seg)
    def _():
        cur[...] = inp[...]

    pl.semaphore_wait(barrier, len(greet))

    @pl.when(last_seg)
    def _():
        start_all(dout_copies(EVERY))

    def front(chunk, edge):
        for start, size in pieces(chunk):
            rows = slice(start, start + size)
            x = cur[rows, :].astype(F32)
            centred = x - jnp.mean(x, axis=-1, keepdims=True)
            rstd = lax.rsqrt(jnp.mean(centred * centred, axis=-1, keepdims=True) + EPS)
            hat = centred * rstd
            xhat[rows, :] = hat
            rstd1[rows, :] = jnp.broadcast_to(rstd, (size, LANE))
            normed[rows, :] = (hat * gain1[...]).astype(BF16)
        x = stacked(normed, chunk)
        mask = jnp.concatenate([mask_of(start, size) for start, size in chunk], axis=0)
        for n in range(width // 256):
            cols = slice(256 * n, 256 * (n + 1))
            q_cols = slice(width + 256 * n, width + 256 * (n + 1))
            p = dot(x, w1[:, cols])
            sig = jax.nn.sigmoid(dot(x, w1[:, q_cols]))
            gated = (p * sig * mask).astype(BF16)
            for rows, value in spread(p, chunk):
                p_buf[rows, cols] = value
            for rows, value in spread(sig, chunk):
                sig_buf[rows, cols] = value
            for rows, value in spread(gated.astype(F32), chunk):
                gpad[HALO + rows.start : HALO + rows.stop, cols] = value
            if edge:
                edge_g[0, :, cols] = gated[:HALO]
                edge_g[1, :, cols] = gated[HALO:]

    @pl.when(last_seg)
    def _():
        for copy in out_copies(EDGES):
            copy.wait_recv()

    @pl.when(first_seg)
    def _():
        load_w1.wait()

    @pl.when(last_seg)
    def _():
        load_w1.wait()

    front(EDGES, True)
    copies = halo_copies(edge_g, halo_g, 0)
    start_all(copies)

    @pl.when(last_seg)
    def _():
        for copy in out_copies(MIDDLE):
            copy.wait_recv()

    front(MIDDLE, False)

    @pl.when(last_seg)
    def _():
        start_all(turned_copies(0))

    maskf = mask_of(0, frames)
    for copy in copies:
        copy.wait()
    has_left = (t > 0).astype(F32)
    has_right = (t < n_tm - 1).astype(F32)
    gpad[0:HALO, :] = halo_g[0].astype(F32) * has_left
    gpad[HALO + frames :, :] = halo_g[1].astype(F32) * has_right

    def conv_block(block, carry):
        cols, total = taps_over(gpad, block, False)
        conv[:, cols] = total
        return carry

    lax.fori_loop(0, width // LANE, conv_block, 0)

    def act_rows(chunk):
        for start, size in pieces(chunk):
            rows = slice(start, start + size)
            x = conv[rows, :]
            centred = x - jnp.mean(x, axis=-1, keepdims=True)
            rstd = lax.rsqrt(jnp.mean(centred * centred, axis=-1, keepdims=True) + EPS)
            hat = centred * rstd
            zn = hat * gain2[...]
            zhat[rows, :] = hat
            zn_buf[rows, :] = zn
            rstd2[rows, :] = jnp.broadcast_to(rstd, (size, LANE))
            act[rows, :] = (zn * jax.nn.sigmoid(zn)).astype(BF16)

    def out_rows(chunk):
        x = stacked(act, chunk)
        for n in range(model // 512):
            cols = slice(512 * n, 512 * (n + 1))
            for rows, value in spread(dot(x, w2[:, cols]), chunk):
                mask = mask_of(rows.start, rows.stop - rows.start)
                out_ref[rows, cols] = (cur[rows, cols].astype(F32) + mask * value).astype(BF16)

    @pl.when(first_seg)
    def _():
        load_w2.wait()
        for chunk in (EDGES, MIDDLE):
            act_rows(chunk)
            out_rows(chunk)
            start_all(out_copies(chunk))
        store_out.start()
        turn((0,))
        for copy in out_copies(EVERY):
            copy.wait_send()
        for part in range(3):
            start_all(turned_copies(part))
        forward_turned((0, 1, 2))
        wait_turned((0, 1, 2))
        turn((1, 2, 3))

    @pl.when(last_seg)
    def _():
        act_rows(EVERY)

    def conv_grad(chunk):
        for start, size in pieces(chunk):
            rows = slice(start, start + size)
            zn = zn_buf[rows, :]
            hat = zhat[rows, :]
            sg = jax.nn.sigmoid(zn)
            d_zn = d_act[rows, :] * (sg + zn * sg * (1.0 - sg))
            gk[TAPS : TAPS + 1, :] += jnp.sum(d_zn * hat, axis=0, keepdims=True)
            d_hat = d_zn * gain2[...]
            m_one = jnp.mean(d_hat, axis=-1, keepdims=True)
            m_two = jnp.mean(d_hat * hat, axis=-1, keepdims=True)
            d_conv = rstd2[rows, 0:1] * (d_hat - m_one - hat * m_two)
            dpad[HALO + start : HALO + start + size, :] = d_conv

    halos = halo_copies(edge_d, halo_d, 2)

    def send_edges():
        edge_d[0] = dpad[HALO : 2 * HALO, :].astype(BF16)
        edge_d[1] = dpad[frames : HALO + frames, :].astype(BF16)
        start_all(halos)

    @pl.when(first_seg)
    def _():
        for chunk in (EDGES, MIDDLE[:1], MIDDLE[1:]):
            for copy in grad_copies(chunk):
                copy.wait_recv()
            upper(chunk)
            conv_grad(chunk)
            if chunk is EDGES:
                send_edges()
            start_all(dout_copies(chunk))

    @pl.when(last_seg)
    def _():
        conv_grad(EDGES)
        send_edges()
        start_all(turned_copies(1))
        start_all(turned_copies(2))
        conv_grad(MIDDLE)

    for copy in halos:
        copy.wait()
    dpad[0:HALO, :] = halo_d[0].astype(F32) * has_left
    dpad[HALO + frames :, :] = halo_d[1].astype(F32) * has_right

    for half in range(2):

        def pre_block(block, carry):
            cols, total = taps_over(dpad, half * 3 + block, True)
            d_gated = total * maskf
            sig = sig_buf[:, cols]
            d_p = d_gated * sig
            d_q = d_p * p_buf[:, cols] * (1.0 - sig)
            part = pl.ds(pl.multiple_of(block * LANE, LANE), LANE)
            dpre4[half, :, part] = d_p.astype(BF16)
            dpre4[2 + half, :, part] = d_q.astype(BF16)
            return carry

        lax.fori_loop(0, 3, pre_block, 0)

    @pl.when(first_seg)
    def _():
        start_all(dpre_copies())

    def grad_rows(chunk):
        d_pre = jnp.concatenate([stacked(dpre4.at[i], chunk) for i in range(4)], axis=1)
        for n in range(model // 512):
            cols = slice(512 * n, 512 * (n + 1))
            for rows, value in spread(dot_t(d_pre, w1[cols, :]), chunk):
                d_norm[rows, cols] = value
        for start, size in pieces(chunk):
            rows = slice(start, start + size)
            d_normed = d_norm[rows, :]
            hat = xhat[rows, :]
            gg1[0:1, :] += jnp.sum(d_normed * hat, axis=0, keepdims=True)
            d_hat = d_normed * gain1[...]
            m_one = jnp.mean(d_hat, axis=-1, keepdims=True)
            m_two = jnp.mean(d_hat * hat, axis=-1, keepdims=True)
            d_h = rstd1[rows, 0:1] * (d_hat - m_one - hat * m_two)
            grad_ref[rows, :] = (e[rows, :].astype(F32) + d_h).astype(BF16)

    @pl.when(first_seg)
    def _():
        grad_rows(EVERY)
        store_grad.start()

    @pl.when(last_seg)
    def _():
        for chunk in (EDGES, MIDDLE):
            grad_rows(chunk)
            start_all(grad_copies(chunk))
        start_all(dpre_copies())
        store_grad.start()
        out_rows(EVERY)
        store_out.start()
        turn((0,))
        forward_turned((2, 0, 1))
        wait_turned((2, 0, 1))
        turn((1, 2, 3))
        for copy in grad_copies(EVERY):
            copy.wait_send()

    def tap_grads(block, carry):
        cols = pl.ds(pl.multiple_of(block * LANE, LANE), LANE)
        whole = gpad[:, cols]
        d_conv = dpad[HALO : HALO + frames, cols]
        for r in range(8):
            moved = whole if r == 0 else pltpu.roll(whole, whole.shape[0] - r, 0)
            for k in range(TAPS):
                if (k + 1) % 8 == r:
                    at = k + 1 - r
                    gk[k : k + 1, cols] = jnp.sum(
                        moved[at : at + frames] * d_conv, axis=0, keepdims=True
                    )
        return carry

    low, high = pl.ds(0, n_z // 2), pl.ds(n_z // 2, n_z // 2)
    up, down, far = (dy + 1) % n_y, (dy + n_y - 1) % n_y, (dy + 2) % n_y

    def y_far(buf, inner, base_sem):
        return [
            remote(buf.at[far, low], inner.at[0], sem_y, base_sem, "dp", up),
            remote(buf.at[far, high], inner.at[1], sem_y, base_sem + 1, "dp", down),
        ]

    def y_direct(buf, got, base_sem):
        return [
            remote(buf.at[up, high], got.at[0, high], sem_y, base_sem + 2, "dp", up),
            remote(buf.at[down, low], got.at[1, low], sem_y, base_sem + 3, "dp", down),
        ]

    def y_summed(buf, got, base_sem):
        return [
            remote(buf.at[up, low], got.at[0, low], sem_y, base_sem + 4, "dp", up),
            remote(buf.at[down, high], got.at[1, high], sem_y, base_sem + 5, "dp", down),
        ]

    def z_peer(d):
        return ((z + d + n_z) % n_z) * 4 + j

    def z_far(item):
        q_buf, in_three, in_four, _, base_sem = item[3:]
        parts = q_buf.shape[1] // 2
        copies = []
        for i, d in enumerate((1, -1)):
            over = pl.ds(parts * i, parts)
            three, four = (z + 3 * d + n_z) % n_z, (z + 4) % n_z
            to = z_peer(2 * d)
            at = base_sem + 2 * i
            copies.append(remote(q_buf.at[three], in_three.at[i], sem_z, at, "tm", to))
            copies.append(remote(q_buf.at[four, over], in_four.at[i], sem_z, at + 1, "tm", to))
        return copies

    def z_near(item):
        q_buf, _, _, got, base_sem = item[3:]
        copies = []
        for i, d in enumerate((2, -2, 1, -1)):
            peer = (z + d + n_z) % n_z
            at = base_sem + 4 + i
            copies.append(remote(q_buf.at[peer], got.at[i], sem_z, at, "tm", z_peer(d)))
        return copies

    def z_relay(item):
        q_buf, in_three, in_four, _, _ = item[3:]
        parts = q_buf.shape[1] // 2
        for copy in z_far(item):
            copy.wait()
        copies = z_near(item)
        for i, d in enumerate((2, -2)):
            peer = (z + d + n_z) % n_z
            for m in range(parts):
                k = parts * i + m
                q_buf[peer, k] = (q_buf[peer, k].astype(F32) + in_four[i, m].astype(F32)).astype(BF16)
            copies[i].start()
        for i, d in enumerate((1, -1)):
            peer = (z + d + n_z) % n_z
            q_buf[peer] = (q_buf[peer].astype(F32) + in_three[i].astype(F32)).astype(BF16)
            copies[2 + i].start()

    def z_total(item):
        q_buf, _, _, got, _ = item[3:]
        for copy in z_near(item):
            copy.wait()
        total = q_buf[z].astype(F32)
        for i in range(4):
            total = total + got[i].astype(F32)
        return total

    def b_copies():
        return [
            remote(qy.at[(dy + d) % n_y], y_got.at[d - 1], sem_y, 11 + d, "dp", (dy + d) % n_y)
            for d in range(1, n_y)
        ]

    rows_one = model // n_y
    rows_two = width // n_y

    for copy in dout_copies(EVERY):
        copy.wait()
    rhs_two = jnp.concatenate([dout4[j]] + [dout_r[d] for d in range(3)], axis=0)
    item_a = tuple(item_a) + (0,)
    item_b = (None,) * 3 + tuple(item_b) + (8,)
    item_c = tuple(item_c) + (16,)

    def product(turned, peer, rows, rhs):
        start = pl.multiple_of(peer * rows, rows)
        lhs = jnp.concatenate([turned[i, pl.ds(start, rows), :] for i in range(4)], axis=1)
        return dot(lhs, rhs)

    def part_two(peer):
        part = product(a_t, peer, rows_two, rhs_two)
        fill = jnp.zeros((8, LANE), F32)
        for i in range(n_z):
            mine = part[24 * i : 24 * (i + 1)]
            blocks = [mine[:, LANE * m : LANE * (m + 1)] for m in range(3)]
            item_b[3][i, peer] = jnp.concatenate(blocks + [fill], axis=0).astype(BF16)

    def part_one(peer):
        part = product(n_t, peer, rows_one, rhs_one[:, :256])
        for i in range(n_z):
            for m in range(2):
                mine = part[48 * i : 48 * (i + 1), LANE * m : LANE * (m + 1)]
                item_a[0][peer, i, m] = mine.astype(BF16)

    def part_last(peer):
        part = product(n_t, peer, rows_one, rhs_one[:, 256:])
        lane = lax.broadcasted_iota(jnp.int32, (24, LANE), 1)
        for i in range(n_z):
            at = pl.multiple_of(peer * rows_two + 24 * i, 8)
            at_t = pl.multiple_of(peer * rows_one + 48 * i, 8)
            extra = ebuf[pl.ds(at, 24), :]
            extra = jnp.where(lane == 32, tbuf[pl.ds(at_t, 24), :], extra)
            extra = jnp.where(lane == 33, tbuf[pl.ds(at_t + 24, 24), :], extra)
            top = extra[:8] + pltpu.roll(extra[8:16], 64, 1)
            item_c[0][peer, i, 0] = part[48 * i : 48 * i + 32].astype(BF16)
            blocks = [part[48 * i + 32 : 48 * (i + 1)], top, extra[16:]]
            item_c[0][peer, i, 1] = jnp.concatenate(blocks, axis=0).astype(BF16)

    def y_begin(item, fill, base_sem):
        buf, inner, got = item[:3]
        fill(far)
        start_all(y_far(buf, inner, base_sem))
        fill(up)
        fill(down)
        start_all(y_direct(buf, got, base_sem))
        fill(dy)

    def y_relay(item, base_sem):
        buf, inner, got = item[:3]
        for copy in y_far(buf, inner, base_sem):
            copy.wait()
        for i in range(n_z // 2):
            k = n_z // 2 + i
            buf[up, i] = (buf[up, i].astype(F32) + inner[0, i].astype(F32)).astype(BF16)
            buf[down, k] = (buf[down, k].astype(F32) + inner[1, i].astype(F32)).astype(BF16)
        start_all(y_summed(buf, got, base_sem))

    def y_finish(item, base_sem):
        buf, _, got, q_buf = item[:4]
        for copy in y_direct(buf, got, base_sem) + y_summed(buf, got, base_sem):
            copy.wait()

        def total(d):
            at = (z + d) % n_z
            mine = buf[dy, at].astype(F32) + got[0, at].astype(F32) + got[1, at].astype(F32)
            q_buf[at] = mine.astype(BF16)

        for d in (3, 5, 4):
            total(d)
        start_all(z_far(item))
        for d in (2, 6, 1, 7, 0):
            total(d)

    for yy in range(n_y):
        part_two(yy)
    start_all(z_far(item_b))
    lax.fori_loop(0, width // LANE, tap_grads, 0)
    for i in range(width // LANE):
        cols = slice(LANE * i, LANE * (i + 1))
        ebuf[cols, :] = gk[:, cols].T
    for i in range(model // LANE):
        cols = slice(LANE * i, LANE * (i + 1))
        tbuf[cols, :] = jnp.broadcast_to(gg1[0:1, cols], (LANE, LANE)).T


    for copy in dpre_copies():
        copy.wait()
    rhs_one = jnp.concatenate([dpre4[j]] + [dpre_r[d] for d in range(3)], axis=0)
    y_begin(item_a, part_one, 0)
    z_relay(item_b)
    y_begin(item_c, part_last, 6)
    y_relay(item_a, 0)
    y_relay(item_c, 6)
    qy[...] = z_total(item_b).astype(BF16)
    start_all(b_copies())
    y_finish(item_a, 0)
    y_finish(item_c, 6)
    z_relay(item_a)

    fs[...] = jnp.zeros_like(fs)
    for copy in b_copies():
        copy.wait()
    total = qy[dy].astype(F32)
    for d in range(n_y - 1):
        total = total + y_got[d].astype(F32)
    for i in range(4):
        for m in range(3):
            at = 24 * m + 6 * i
            fs[i, 16:22, LANE * m : LANE * (m + 1)] = total[at : at + 6]
    z_relay(item_c)
    total = z_total(item_a)
    for i in range(4):
        for m in range(2):
            fs[i, 0:12, LANE * m : LANE * (m + 1)] = total[m, 12 * i : 12 * (i + 1)]
    total = z_total(item_c)
    whole = jnp.concatenate([total[0], total[1, :16]], axis=0)
    top = total[1, 16:24]
    extra = jnp.concatenate([top, pltpu.roll(top, 64, 1), total[1, 24:]], axis=0)
    for i in range(4):
        fs[i, 0:12, 256:] = whole[12 * i : 12 * (i + 1)]
        fs[i, 24:30, 0:LANE] = extra[6 * i : 6 * (i + 1)]
        for m in range(2):
            at = 12 * (i % 2) + 6 * m
            fs[i, 24:30, LANE * (m + 1) : LANE * (m + 2)] = extra[at : at + 6]
    copies = [remote(fs.at[peer_j(d)], fr.at[j], sem_f, d, "tm", group[d]) for d in range(3)]
    start_all(copies)
    fr[j] = fs[j]
    for copy in copies:
        copy.wait()
    small = jnp.zeros((8, 3 * LANE), F32)
    for i in range(4):
        cols = slice(384 * i, 384 * (i + 1))
        for row in range(12):
            o_one[row, :, cols] = fr[i, row : row + 1, :]
        for row in range(6):
            o_two[row, :, cols] = fr[i, 16 + row : 17 + row, :]
        small = small + fr[i, 24:32, :]
    for i in range(6):
        o_kern[i] = small[i : i + 1, :TAPS]
    fill = jnp.zeros((LANE - 8, LANE), F32)
    turned = [
        jnp.concatenate([small[:, LANE * m : LANE * (m + 1)], fill], axis=0).T for m in range(3)
    ]
    o_gain2[...] = turned[0][TAPS : TAPS + 1, :6]
    for m in range(2):
        pair = turned[m + 1][32:34, :6]
        o_gain1[:, 6 * m : 6 * (m + 1)] = jnp.where(j < 2, pair[0:1], pair[1:2])
    store_out.wait()
    store_grad.wait()


def hand_over(*refs):
    n = len(refs) // 2
    for i in range(n):
        refs[n + i][...] = refs[i][...]


def per_device(inputs, lengths, w_first, kernel_w, gain_first, gain_second, w_second, grad_output):
    n_y = lax.axis_size("dp")
    n_tm = lax.axis_size("tm")
    n_z = n_tm // 4
    frames, model = inputs.shape[1:]
    width = w_second.shape[1]
    groups = n_y * n_tm
    vmem = pl.BlockSpec(memory_space=pltpu.VMEM)

    def buf(shape, dtype):
        return pltpu.VMEM(shape, dtype)

    def second(parts, rows):
        return (
            buf((n_z, parts, rows, LANE), BF16),
            buf((2, parts, rows, LANE), BF16),
            buf((2, parts // 2, rows, LANE), BF16),
            buf((4, parts, rows, LANE), BF16),
        )

    def reduced(rows):
        return (
            buf((n_y, n_z, 2, rows, LANE), BF16),
            buf((2, n_z // 2, 2, rows, LANE), BF16),
            buf((2, n_z, 2, rows, LANE), BF16),
        ) + second(2, rows)

    wide = (frames, model)
    thin = (frames, width)
    padded = (frames + 2 * HALO, width)
    third = (4, frames, 384)
    scratch = [
        buf((model, 2 * width), BF16),
        buf((width, model), BF16),
        buf(wide, BF16),
        buf(wide, BF16),
        buf(wide, BF16),
        buf(wide, BF16),
        buf(wide, F32),
        buf((frames, LANE), F32),
        buf(wide, BF16),
        buf(thin, F32),
        buf(thin, F32),
        buf(padded, F32),
        buf(padded, F32),
        buf(thin, F32),
        buf(thin, F32),
        buf((frames, LANE), F32),
        buf(thin, F32),
        buf(thin, BF16),
        buf(thin, F32),
        buf(wide, F32),
        buf((2, HALO, width), BF16),
        buf((2, HALO, width), BF16),
        buf((2, HALO, width), BF16),
        buf((2, HALO, width), BF16),
        buf(third, BF16),
        buf(third, BF16),
        buf((3, frames, 384), BF16),
        buf((3, frames, 384), BF16),
        buf((3,) + wide, BF16),
        buf((3,) + thin, BF16),
        buf((4, model, LANE), BF16),
        buf((4, width, LANE), BF16),
        buf((LANE, width), F32),
        buf((8, model), F32),
        buf((width, LANE), F32),
        buf((model, LANE), F32),
        reduced(48),
        second(4, 80),
        reduced(32),
        buf((n_y, 80, LANE), BF16),
        buf((n_y - 1, 80, LANE), BF16),
        buf((4, 32, 384), F32),
        buf((4, 32, 384), F32),
        pltpu.SemaphoreType.DMA((4,)),
        pltpu.SemaphoreType.DMA((2, 4)),
        pltpu.SemaphoreType.DMA((2, 4)),
        pltpu.SemaphoreType.DMA((2, 4)),
        pltpu.SemaphoreType.DMA((2, 24)),
        pltpu.SemaphoreType.DMA((2, 15)),
        pltpu.SemaphoreType.DMA((2, 24)),
        pltpu.SemaphoreType.DMA((2, 3)),
    ]
    hbm = pl.BlockSpec(memory_space=pl.ANY)
    shapes = (
        jax.ShapeDtypeStruct(wide, BF16),
        jax.ShapeDtypeStruct(wide, BF16),
        jax.ShapeDtypeStruct((model // groups, 1, model), F32),
        jax.ShapeDtypeStruct((width // groups, 1, model), F32),
        jax.ShapeDtypeStruct((width // groups, 1, TAPS), F32),
        jax.ShapeDtypeStruct((1, model // groups), F32),
        jax.ShapeDtypeStruct((1, width // groups), F32),
    )
    results = pl.pallas_call(
        functools.partial(kernel, n_y, n_z, n_tm),
        out_shape=shapes,
        in_specs=[pl.BlockSpec(memory_space=pltpu.SMEM), vmem, vmem, hbm, hbm, vmem, vmem, vmem],
        out_specs=(hbm, hbm) + (vmem,) * 5,
        scratch_shapes=scratch,
        compiler_params=pltpu.CompilerParams(
            collective_id=0, has_side_effects=True, vmem_limit_bytes=60 * 1024 * 1024
        ),
        cost_estimate=pl.CostEstimate(
            flops=2 * 3 * frames * model * 3 * width, bytes_accessed=12_000_000, transcendentals=0
        ),
    )(
        lengths,
        inputs[0],
        grad_output[0],
        w_first[0],
        w_second[0],
        kernel_w.transpose(1, 0, 2),
        gain_first,
        gain_second,
    )
    out, grad, one, two, taps, g_one, g_two = pl.pallas_call(
        hand_over,
        out_shape=shapes,
        in_specs=[vmem] * 7,
        out_specs=(vmem,) * 7,
        compiler_params=pltpu.CompilerParams(vmem_limit_bytes=60 * 1024 * 1024),
    )(*results)
    return (
        out[None, None],
        grad[None, None],
        one.transpose(1, 0, 2),
        taps.transpose(1, 2, 0),
        g_one,
        g_two,
        two.transpose(1, 0, 2),
    )


def solution(mesh):
    in_specs = (
        P("dp", "tm", None),
        P("dp"),
        P("segment", None, None),
        P("segment", None, None),
        P("segment", None),
        P("segment", None),
        P("segment", None, None),
        P("dp", "tm", None),
    )
    out_specs = (
        P("segment", "dp", "tm", None),
        P("segment", "dp", "tm", None),
        P("segment", ("dp", "tm"), None),
        P("segment", None, ("dp", "tm")),
        P("segment", ("dp", "tm")),
        P("segment", ("dp", "tm")),
        P("segment", ("dp", "tm"), None),
    )
    return jax.shard_map(
        per_device, mesh=mesh, in_specs=in_specs, out_specs=out_specs, check_vma=False
    )
```

```python
import functools

import jax
import jax.numpy as jnp
from jax import lax
from jax.experimental import pallas as pl
from jax.experimental.pallas import tpu as pltpu
from jax.sharding import PartitionSpec as P

EPS = 1e-05
F32 = jnp.float32
BF16 = jnp.bfloat16
MESH = pl.DeviceIdType.MESH
NT = (((1,), (1,)), ((), ()))
HALO = 16
TAPS = 31
LANE = 128
ROWS = 32
EDGES = ((0, 16), (112, 16))
MIDDLE = ((16, 48), (64, 48))
EVERY = EDGES + MIDDLE


def chunk_rows(chunk):
    return [(EVERY.index(part), pl.ds(*part)) for part in chunk]


def dot(a, b):
    return jnp.dot(a, b, preferred_element_type=F32)


def dot_t(a, b):
    return lax.dot_general(a, b, NT, preferred_element_type=F32)


def kernel(
    n_y,
    n_z,
    n_tm,
    len_ref,
    inp,
    gout,
    w1_hbm,
    w2_hbm,
    kern,
    gain1,
    gain2,
    out_hbm,
    grad_hbm,
    o_one,
    o_two,
    o_kern,
    o_gain1,
    o_gain2,
    w1,
    w2,
    out_ref,
    grad_ref,
    cur,
    e,
    xhat,
    rstd1,
    normed,
    p_buf,
    sig_buf,
    gpad,
    dpad,
    conv,
    zhat,
    rstd2,
    zn_buf,
    act,
    d_act,
    d_norm,
    edge_g,
    edge_d,
    halo_g,
    halo_d,
    dout4,
    dpre4,
    dout_r,
    dpre_r,
    n_raw,
    a_raw,
    n_t,
    a_t,
    gk,
    gg1,
    ebuf,
    tbuf,
    item_a,
    item_b,
    item_c,
    item_d,
    qy,
    y_got,
    dqy,
    d_got,
    fs,
    f_out,
    f_in,
    sem_w,
    sem_h,
    sem_out,
    sem_grad,
    sem_x,
    sem_y,
    sem_z,
    sem_f,
):
    frames, model = inp.shape
    width = w2.shape[0]
    dy = lax.axis_index("dp")
    seg = lax.axis_index("segment")
    t = lax.axis_index("tm")
    c = t % 2
    xl = (t // 2) % 2
    z = t // 4
    j = t % 4
    base = z * 4
    group = [base + xl * 2 + (1 - c), base + (1 - xl) * 2 + c, base + (1 - xl) * 2 + (1 - c)]
    right = (t + 1) % n_tm
    left = (t + n_tm - 1) % n_tm
    first_seg = seg == 0
    last_seg = seg == 1

    def remote(src, dst, sems, index, axis, peer):
        return pltpu.make_async_remote_copy(
            src_ref=src,
            dst_ref=dst,
            send_sem=sems.at[0, index],
            recv_sem=sems.at[1, index],
            device_id={axis: peer},
            device_id_type=MESH,
        )

    load_w1 = pltpu.make_async_copy(w1_hbm, w1, sem_w.at[0])
    load_w2 = pltpu.make_async_copy(w2_hbm, w2, sem_w.at[1])
    store_out = pltpu.make_async_copy(out_ref, out_hbm, sem_w.at[2])
    store_grad = pltpu.make_async_copy(grad_ref, grad_hbm, sem_w.at[3])
    barrier = pltpu.get_barrier_semaphore()
    greet = [("tm", left), ("tm", right), ("segment", 1 - seg)]
    greet += [("tm", g) for g in group]
    greet += [("dp", (dy + d) % n_y) for d in range(1, n_y)]
    greet += [("tm", ((z + d) % n_z) * 4 + j) for d in (1, 2, n_z - 1, n_z - 2)]
    for axis, peer in greet:
        pl.semaphore_signal(barrier, inc=1, device_id={axis: peer}, device_id_type=MESH)

    @pl.when(first_seg)
    def _():
        load_w1.start()
        load_w2.start()

    @pl.when(last_seg)
    def _():
        load_w2.start()
        load_w1.start()

    length = len_ref[0]

    def mask_of(start, rows):
        ids = t * frames + start + lax.broadcasted_iota(jnp.int32, (rows, 1), 0)
        return (ids < length).astype(F32)

    def out_copies(chunk):
        return [
            remote(out_ref.at[rows], cur.at[rows], sem_out, i, "segment", 1 - seg)
            for i, rows in chunk_rows(chunk)
        ]

    def grad_copies(chunk):
        return [
            remote(grad_ref.at[rows], e.at[rows], sem_grad, i, "segment", 1 - seg)
            for i, rows in chunk_rows(chunk)
        ]

    def halo_copies(edge, halo, offset):
        return [
            remote(edge.at[0], halo.at[1], sem_h, offset, "tm", left),
            remote(edge.at[1], halo.at[0], sem_h, offset + 1, "tm", right),
        ]

    def peer_j(d):
        return group[d] % 4

    def dout_copies(chunk):
        return [
            remote(
                dout4.at[peer_j(d), rows], dout_r.at[d, rows], sem_x, 3 * i + d, "tm", group[d]
            )
            for i, rows in chunk_rows(chunk)
            for d in range(3)
        ]

    def dpre_copies(last):
        cols = pl.ds(256, LANE) if last else pl.ds(0, 256)
        return [
            remote(
                dpre4.at[peer_j(d), :, cols],
                dpre_r.at[d, :, cols],
                sem_x,
                12 + 3 * last + d,
                "tm",
                group[d],
            )
            for d in range(3)
        ]

    def turned_copies(part, forward=False):
        own, got = (act, a_raw) if part > 3 else (normed, n_raw)
        rows = pl.ds(64 * (part - 4), 64) if part > 3 else pl.ds(32 * part, 32)

        def one(src, dst, d):
            return remote(
                src.at[rows], got.at[dst, rows], sem_x, 18 + 3 * part + d, "tm", group[d % 2]
            )

        return [one(got.at[1], 2, 2)] if forward else [one(own, 0, 0), one(own, 1, 1)]

    def forward_turned(parts):
        for part in parts:
            turned_copies(part)[1].wait_recv()
            turned_copies(part, True)[0].start()

    def wait_turned(parts):
        for part in parts:
            copies = turned_copies(part)
            copies[0].wait()
            copies[1].wait_send()
            turned_copies(part, True)[0].wait()

    def start_all(copies):
        for copy in copies:
            copy.start()

    def stacked(ref, chunk):
        return jnp.concatenate([ref[start : start + size] for start, size in chunk], axis=0)

    def spread(value, chunk):
        at = 0
        for start, size in chunk:
            yield slice(start, start + size), value[at : at + size]
            at += size

    def pieces(chunk):
        return [(at, min(ROWS, start + size - at)) for start, size in chunk for at in range(start, start + size, ROWS)]

    def upper(chunk):
        for start, size in pieces(chunk):
            rows = slice(start, start + size)
            d_out = (e[rows, :].astype(F32) * mask_of(start, size)).astype(BF16)
            for i in range(4):
                dout4[i, rows, :] = d_out[:, 384 * i : 384 * (i + 1)]
        d_out = jnp.concatenate([stacked(dout4.at[i], chunk) for i in range(4)], axis=1)
        for n in range(width // 256):
            cols = slice(256 * n, 256 * (n + 1))
            for rows, value in spread(dot_t(d_out, w2[cols, :]), chunk):
                d_act[rows, cols] = value

    def taps_over(src, block, flip):
        cols = pl.ds(pl.multiple_of(block * LANE, LANE), LANE)
        whole = src[:, cols]
        total = jnp.zeros((frames, LANE), F32)
        for r in range(8):
            moved = whole if r == 0 else pltpu.roll(whole, whole.shape[0] - r, 0)
            for k in range(TAPS):
                if (k + 1) % 8 == r:
                    at = k + 1 - r
                    tap = TAPS - 1 - k if flip else k
                    total = total + kern[tap, :, cols] * moved[at : at + frames]
        return cols, total

    def turn_normed(slots):
        for slot in slots:
            src = normed if slot == 0 else n_raw.at[slot - 1]
            for i in range(model // LANE):
                cols = slice(LANE * i, LANE * (i + 1))
                n_t[slot, cols, :] = src[:, cols].T

    def turn_act(slots):
        for slot in slots:
            src = act if slot == 0 else a_raw.at[slot - 1]
            for i in range(width // LANE):
                cols = slice(LANE * i, LANE * (i + 1))
                a_t[slot, cols, :] = src[:, cols].T

    gg1[...] = jnp.zeros_like(gg1)
    gk[...] = jnp.zeros_like(gk)

    @pl.when(last_seg)
    def _():
        e[...] = gout[...]
        load_w2.wait()
        upper(EVERY)

    @pl.when(first_seg)
    def _():
        cur[...] = inp[...]

    pl.semaphore_wait(barrier, len(greet))

    @pl.when(last_seg)
    def _():
        start_all(dout_copies(EVERY))

    def front(chunk, edge):
        for start, size in pieces(chunk):
            rows = slice(start, start + size)
            x = cur[rows, :].astype(F32)
            centred = x - jnp.mean(x, axis=-1, keepdims=True)
            rstd = lax.rsqrt(jnp.mean(centred * centred, axis=-1, keepdims=True) + EPS)
            hat = centred * rstd
            xhat[rows, :] = hat
            rstd1[rows, :] = jnp.broadcast_to(rstd, (size, LANE))
            normed[rows, :] = (hat * gain1[...]).astype(BF16)
        x = stacked(normed, chunk)
        mask = jnp.concatenate([mask_of(start, size) for start, size in chunk], axis=0)
        for n in range(width // 256):
            cols = slice(256 * n, 256 * (n + 1))
            q_cols = slice(width + 256 * n, width + 256 * (n + 1))
            p = dot(x, w1[:, cols])
            sig = jax.nn.sigmoid(dot(x, w1[:, q_cols]))
            gated = (p * sig * mask).astype(BF16)
            for rows, value in spread(p, chunk):
                p_buf[rows, cols] = value
            for rows, value in spread(sig, chunk):
                sig_buf[rows, cols] = value
            for rows, value in spread(gated.astype(F32), chunk):
                gpad[HALO + rows.start : HALO + rows.stop, cols] = value
            if edge:
                edge_g[0, :, cols] = gated[:HALO]
                edge_g[1, :, cols] = gated[HALO:]

    @pl.when(last_seg)
    def _():
        for copy in out_copies(EDGES):
            copy.wait_recv()

    @pl.when(first_seg)
    def _():
        load_w1.wait()

    @pl.when(last_seg)
    def _():
        load_w1.wait()

    front(EDGES, True)
    copies = halo_copies(edge_g, halo_g, 0)
    start_all(copies)

    @pl.when(last_seg)
    def _():
        for copy in out_copies(MIDDLE):
            copy.wait_recv()

    front(MIDDLE, False)

    @pl.when(last_seg)
    def _():
        start_all(turned_copies(0))

    maskf = mask_of(0, frames)
    for copy in copies:
        copy.wait()
    has_left = (t > 0).astype(F32)
    has_right = (t < n_tm - 1).astype(F32)
    gpad[0:HALO, :] = halo_g[0].astype(F32) * has_left
    gpad[HALO + frames :, :] = halo_g[1].astype(F32) * has_right

    def conv_block(block, carry):
        cols, total = taps_over(gpad, block, False)
        conv[:, cols] = total
        return carry

    lax.fori_loop(0, width // LANE, conv_block, 0)

    def act_rows(chunk):
        for start, size in pieces(chunk):
            rows = slice(start, start + size)
            x = conv[rows, :]
            centred = x - jnp.mean(x, axis=-1, keepdims=True)
            rstd = lax.rsqrt(jnp.mean(centred * centred, axis=-1, keepdims=True) + EPS)
            hat = centred * rstd
            zn = hat * gain2[...]
            zhat[rows, :] = hat
            zn_buf[rows, :] = zn
            rstd2[rows, :] = jnp.broadcast_to(rstd, (size, LANE))
            act[rows, :] = (zn * jax.nn.sigmoid(zn)).astype(BF16)

    def out_rows(chunk):
        x = stacked(act, chunk)
        for n in range(model // 512):
            cols = slice(512 * n, 512 * (n + 1))
            for rows, value in spread(dot(x, w2[:, cols]), chunk):
                mask = mask_of(rows.start, rows.stop - rows.start)
                out_ref[rows, cols] = (cur[rows, cols].astype(F32) + mask * value).astype(BF16)

    @pl.when(first_seg)
    def _():
        load_w2.wait()
        for chunk in (EDGES, MIDDLE):
            act_rows(chunk)
            out_rows(chunk)
            start_all(out_copies(chunk))
        store_out.start()
        turn_normed((0,))
        turn_act((0,))
        for copy in out_copies(EVERY):
            copy.wait_send()
        for part in range(6):
            start_all(turned_copies(part))
        forward_turned(range(6))
        wait_turned(range(6))
        turn_normed((1, 2, 3))
        turn_act((1, 2, 3))

    @pl.when(last_seg)
    def _():
        start_all(turned_copies(1))
        act_rows(EVERY)

    def conv_grad(chunk):
        for start, size in pieces(chunk):
            rows = slice(start, start + size)
            zn = zn_buf[rows, :]
            hat = zhat[rows, :]
            sg = jax.nn.sigmoid(zn)
            d_zn = d_act[rows, :] * (sg + zn * sg * (1.0 - sg))
            gk[TAPS : TAPS + 1, :] += jnp.sum(d_zn * hat, axis=0, keepdims=True)
            d_hat = d_zn * gain2[...]
            m_one = jnp.mean(d_hat, axis=-1, keepdims=True)
            m_two = jnp.mean(d_hat * hat, axis=-1, keepdims=True)
            d_conv = rstd2[rows, 0:1] * (d_hat - m_one - hat * m_two)
            dpad[HALO + start : HALO + start + size, :] = d_conv

    halos = halo_copies(edge_d, halo_d, 2)

    def send_edges():
        edge_d[0] = dpad[HALO : 2 * HALO, :].astype(BF16)
        edge_d[1] = dpad[frames : HALO + frames, :].astype(BF16)
        start_all(halos)

    @pl.when(first_seg)
    def _():
        for chunk in (EDGES, MIDDLE[:1], MIDDLE[1:]):
            for copy in grad_copies(chunk):
                copy.wait_recv()
            upper(chunk)
            conv_grad(chunk)
            if chunk is EDGES:
                send_edges()
            start_all(dout_copies(chunk))

    @pl.when(last_seg)
    def _():
        conv_grad(EDGES)
        send_edges()
        conv_grad(MIDDLE)

    for copy in halos:
        copy.wait()

    @pl.when(last_seg)
    def _():
        start_all(turned_copies(2))

    dpad[0:HALO, :] = halo_d[0].astype(F32) * has_left
    dpad[HALO + frames :, :] = halo_d[1].astype(F32) * has_right

    for half in range(2):

        def pre_block(block, carry):
            cols, total = taps_over(dpad, half * 3 + block, True)
            d_gated = total * maskf
            sig = sig_buf[:, cols]
            d_p = d_gated * sig
            d_q = d_p * p_buf[:, cols] * (1.0 - sig)
            part = pl.ds(pl.multiple_of(block * LANE, LANE), LANE)
            dpre4[half, :, part] = d_p.astype(BF16)
            dpre4[2 + half, :, part] = d_q.astype(BF16)
            return carry

        lax.fori_loop(0, 3, pre_block, 0)

    @pl.when(first_seg)
    def _():
        start_all(dpre_copies(0) + dpre_copies(1))

    def grad_rows(chunk):
        d_pre = jnp.concatenate([stacked(dpre4.at[i], chunk) for i in range(4)], axis=1)
        for n in range(model // 512):
            cols = slice(512 * n, 512 * (n + 1))
            for rows, value in spread(dot_t(d_pre, w1[cols, :]), chunk):
                d_norm[rows, cols] = value
        for start, size in pieces(chunk):
            rows = slice(start, start + size)
            d_normed = d_norm[rows, :]
            hat = xhat[rows, :]
            gg1[0:1, :] += jnp.sum(d_normed * hat, axis=0, keepdims=True)
            d_hat = d_normed * gain1[...]
            m_one = jnp.mean(d_hat, axis=-1, keepdims=True)
            m_two = jnp.mean(d_hat * hat, axis=-1, keepdims=True)
            d_h = rstd1[rows, 0:1] * (d_hat - m_one - hat * m_two)
            grad_ref[rows, :] = (e[rows, :].astype(F32) + d_h).astype(BF16)

    @pl.when(last_seg)
    def _():
        for chunk in (EDGES, MIDDLE):
            grad_rows(chunk)
            start_all(grad_copies(chunk))
        for part in (4, 5, 3):
            start_all(turned_copies(part))
        start_all(dpre_copies(0) + dpre_copies(1))
        store_grad.start()
        out_rows(EVERY)
        store_out.start()
        turn_act((0,))
        turn_normed((0,))
        forward_turned((0, 1, 2, 4, 5))
        wait_turned((0, 1, 2, 4, 5))
        turn_act((1, 2, 3))
        for copy in grad_copies(EVERY):
            copy.wait_send()

    def tap_grads(block, carry):
        cols = pl.ds(pl.multiple_of(block * LANE, LANE), LANE)
        whole = gpad[:, cols]
        d_conv = dpad[HALO : HALO + frames, cols]
        for r in range(8):
            moved = whole if r == 0 else pltpu.roll(whole, whole.shape[0] - r, 0)
            for k in range(TAPS):
                if (k + 1) % 8 == r:
                    at = k + 1 - r
                    gk[k : k + 1, cols] = jnp.sum(
                        moved[at : at + frames] * d_conv, axis=0, keepdims=True
                    )
        return carry

    low, high = pl.ds(0, n_z // 2), pl.ds(n_z // 2, n_z // 2)
    up, down, far = (dy + 1) % n_y, (dy + n_y - 1) % n_y, (dy + 2) % n_y

    def y_far(buf, inner, base_sem):
        return [
            remote(buf.at[far, low], inner.at[0], sem_y, base_sem, "dp", up),
            remote(buf.at[far, high], inner.at[1], sem_y, base_sem + 1, "dp", down),
        ]

    def y_direct(buf, got, base_sem):
        return [
            remote(buf.at[up, high], got.at[0, high], sem_y, base_sem + 2, "dp", up),
            remote(buf.at[down, low], got.at[1, low], sem_y, base_sem + 3, "dp", down),
        ]

    def y_summed(buf, got, base_sem):
        return [
            remote(buf.at[up, low], got.at[0, low], sem_y, base_sem + 4, "dp", up),
            remote(buf.at[down, high], got.at[1, high], sem_y, base_sem + 5, "dp", down),
        ]

    def z_peer(d):
        return ((z + d + n_z) % n_z) * 4 + j

    def z_far(item):
        q_buf, in_three, in_four, _, base_sem = item[3:]
        parts = q_buf.shape[1] // 2
        copies = []
        for i, d in enumerate((1, -1)):
            over = pl.ds(parts * i, parts if i == 0 else q_buf.shape[1] - parts)
            three, four = (z + 3 * d + n_z) % n_z, (z + 4) % n_z
            to = z_peer(2 * d)
            at = base_sem + 2 * i
            copies.append(remote(q_buf.at[three], in_three.at[i], sem_z, at, "tm", to))
            into = in_four.at[i, pl.ds(0, over.size)]
            copies.append(remote(q_buf.at[four, over], into, sem_z, at + 1, "tm", to))
        return copies

    def z_near(item):
        q_buf, _, _, got, base_sem = item[3:]
        copies = []
        for i, d in enumerate((2, -2, 1, -1)):
            peer = (z + d + n_z) % n_z
            at = base_sem + 4 + i
            copies.append(remote(q_buf.at[peer], got.at[i], sem_z, at, "tm", z_peer(d)))
        return copies

    def z_relay(item):
        q_buf, in_three, in_four, _, _ = item[3:]
        parts = q_buf.shape[1] // 2
        for copy in z_far(item):
            copy.wait()
        copies = z_near(item)
        for i, d in enumerate((2, -2)):
            peer = (z + d + n_z) % n_z
            for m in range(parts if i == 0 else q_buf.shape[1] - parts):
                k = parts * i + m
                q_buf[peer, k] = (q_buf[peer, k].astype(F32) + in_four[i, m].astype(F32)).astype(BF16)
            copies[i].start()
        for i, d in enumerate((1, -1)):
            peer = (z + d + n_z) % n_z
            q_buf[peer] = (q_buf[peer].astype(F32) + in_three[i].astype(F32)).astype(BF16)
            copies[2 + i].start()

    def z_total(item):
        q_buf, _, _, got, _ = item[3:]
        for copy in z_near(item):
            copy.wait()
        total = q_buf[z].astype(F32)
        for i in range(4):
            total = total + got[i].astype(F32)
        return total

    def last_copies(buf, got, base_sem):
        return [
            remote(buf.at[(dy + d) % n_y], got.at[d - 1], sem_y, base_sem + d, "dp", (dy + d) % n_y)
            for d in range(1, n_y)
        ]

    def last_total(buf, got, base_sem):
        for copy in last_copies(buf, got, base_sem):
            copy.wait()
        total = buf[dy].astype(F32)
        for d in range(n_y - 1):
            total = total + got[d].astype(F32)
        return total

    rows_one = model // n_y
    rows_two = width // n_y

    for copy in dout_copies(EVERY):
        copy.wait()
    rhs_two = jnp.concatenate([dout4[j]] + [dout_r[d] for d in range(3)], axis=0)
    item_a = tuple(item_a) + (0,)
    item_b = tuple(item_b) + (8,)
    item_c = (None,) * 3 + tuple(item_c) + (16,)
    item_d = (None,) * 3 + tuple(item_d) + (24,)
    qy_c = (qy, y_got, 11)
    qy_d = (dqy, d_got, 14)

    def product(turned, peer, rows, rhs):
        start = pl.multiple_of(peer * rows, rows)
        lhs = jnp.concatenate([turned[i, pl.ds(start, rows), :] for i in range(4)], axis=1)
        return dot(lhs, rhs)

    def part_two(peer):
        part = product(a_t, peer, rows_two, rhs_two)
        fill = jnp.zeros((8, LANE), F32)
        for i in range(n_z):
            mine = part[24 * i : 24 * (i + 1)]
            blocks = [mine[:, LANE * m : LANE * (m + 1)] for m in range(3)]
            whole = jnp.concatenate(blocks + [fill], axis=0).astype(BF16)
            for m in range(5):
                item_b[0][peer, i, m] = whole[16 * m : 16 * (m + 1)]

    def part_one(peer):
        part = product(n_t, peer, rows_one, rhs_one)
        for i in range(n_z):
            for m in range(2):
                mine = part[48 * i : 48 * (i + 1), LANE * m : LANE * (m + 1)]
                item_a[0][peer, i, m] = mine.astype(BF16)

    def part_last(d):
        peer = (z + d + n_z) % n_z
        starts = [pl.multiple_of(rows_one * yy + 48 * peer, 16) for yy in range(n_y)]
        lhs = jnp.concatenate(
            [
                jnp.concatenate([n_t[i, pl.ds(start, 48), :] for i in range(4)], axis=1)
                for start in starts
            ],
            axis=0,
        )
        part = dot(lhs, rhs_last)
        for yy in range(n_y):
            item_c[3][peer, yy] = part[48 * yy : 48 * (yy + 1)].astype(BF16)

    def part_small():
        for i in range(width // LANE):
            cols = slice(LANE * i, LANE * (i + 1))
            ebuf[cols, :] = gk[:, cols].T
        for i in range(model // LANE):
            cols = slice(LANE * i, LANE * (i + 1))
            tbuf[cols, :] = jnp.broadcast_to(gg1[0:1, cols], (LANE, LANE)).T
        lane = lax.broadcasted_iota(jnp.int32, (24, LANE), 1)
        for peer in range(n_y):
            for i in range(n_z):
                at = peer * rows_two + 24 * i
                at_t = peer * rows_one + 48 * i
                extra = ebuf[at : at + 24, :]
                extra = jnp.where(lane == 32, tbuf[at_t : at_t + 24, :], extra)
                extra = jnp.where(lane == 33, tbuf[at_t + 24 : at_t + 48, :], extra)
                top = extra[:8] + pltpu.roll(extra[8:16], 64, 1)
                item_d[3][i, peer] = jnp.concatenate([top, extra[16:]], axis=0).astype(BF16)

    def y_begin(item, fill, base_sem):
        buf, inner, got = item[:3]
        fill(far)
        start_all(y_far(buf, inner, base_sem))
        fill(up)
        fill(down)
        start_all(y_direct(buf, got, base_sem))
        fill(dy)

    def y_relay(item, base_sem):
        buf, inner, got = item[:3]
        for copy in y_far(buf, inner, base_sem):
            copy.wait()
        for i in range(n_z // 2):
            k = n_z // 2 + i
            buf[up, i] = (buf[up, i].astype(F32) + inner[0, i].astype(F32)).astype(BF16)
            buf[down, k] = (buf[down, k].astype(F32) + inner[1, i].astype(F32)).astype(BF16)
        start_all(y_summed(buf, got, base_sem))

    def y_finish(item, base_sem):
        buf, _, got, q_buf = item[:4]
        for copy in y_direct(buf, got, base_sem) + y_summed(buf, got, base_sem):
            copy.wait()

        def total(d):
            at = (z + d) % n_z
            mine = buf[dy, at].astype(F32) + got[0, at].astype(F32) + got[1, at].astype(F32)
            q_buf[at] = mine.astype(BF16)

        for d in (3, 5, 4):
            total(d)
        start_all(z_far(item))
        for d in (2, 6, 1, 7, 0):
            total(d)

    y_begin(item_b, part_two, 6)

    @pl.when(last_seg)
    def _():
        forward_turned((3,))
        wait_turned((3,))
        turn_normed((1, 2, 3))

    for copy in dpre_copies(0):
        copy.wait()
    rhs_one = jnp.concatenate([dpre4[j, :, :256]] + [dpre_r[d, :, :256] for d in range(3)], axis=0)
    part_one(far)
    start_all(y_far(item_a[0], item_a[1], 0))
    for copy in dpre_copies(1):
        copy.wait()
    rhs_last = jnp.concatenate([dpre4[j, :, 256:]] + [dpre_r[d, :, 256:] for d in range(3)], axis=0)
    for d in (3, -3, 4):
        part_last(d)
    start_all(z_far(item_c))
    part_one(up)
    part_one(down)
    y_relay(item_b, 6)
    start_all(y_direct(item_a[0], item_a[2], 0))
    part_one(dy)
    for d in (1, -1, 2, -2, 0):
        part_last(d)
    lax.fori_loop(0, width // LANE, tap_grads, 0)

    @pl.when(first_seg)
    def _():
        grad_rows(EVERY)
        store_grad.start()

    y_relay(item_a, 0)
    z_relay(item_c)
    y_finish(item_b, 6)
    part_small()
    start_all(z_far(item_d))
    y_finish(item_a, 0)
    qy[...] = z_total(item_c).astype(BF16)
    start_all(last_copies(*qy_c))
    z_relay(item_b)
    z_relay(item_d)
    z_relay(item_a)
    dqy[...] = z_total(item_d).astype(BF16)
    start_all(last_copies(*qy_d))

    fs[...] = jnp.zeros_like(fs)
    total = z_total(item_b)
    total = jnp.concatenate([total[m] for m in range(5)], axis=0)
    for i in range(4):
        for m in range(3):
            at = 24 * m + 6 * i
            fs[i, 16:22, LANE * m : LANE * (m + 1)] = total[at : at + 6]
    total = z_total(item_a)
    for i in range(4):
        for m in range(2):
            fs[i, 0:12, LANE * m : LANE * (m + 1)] = total[m, 12 * i : 12 * (i + 1)]
    small = last_total(*qy_d)
    top = small[:8]
    extra = jnp.concatenate([top, pltpu.roll(top, 64, 1), small[8:]], axis=0)
    total = last_total(*qy_c)
    for i in range(4):
        fs[i, 0:12, 256:] = total[12 * i : 12 * (i + 1)]
        fs[i, 24:30, 0:LANE] = extra[6 * i : 6 * (i + 1)]
        for m in range(2):
            at = 12 * (i % 2) + 6 * m
            fs[i, 24:30, LANE * (m + 1) : LANE * (m + 2)] = extra[at : at + 6]
    f_out[...] = fs[...].astype(BF16)
    copies = [remote(f_out.at[peer_j(d)], f_in.at[j], sem_f, d, "tm", group[d]) for d in range(3)]
    start_all(copies)
    f_in[j] = f_out[j]
    for copy in copies:
        copy.wait()
    fs[...] = f_in[...].astype(F32)
    small = jnp.zeros((8, 3 * LANE), F32)
    for i in range(4):
        cols = slice(384 * i, 384 * (i + 1))
        for row in range(12):
            o_one[row, :, cols] = fs[i, row : row + 1, :]
        for row in range(6):
            o_two[row, :, cols] = fs[i, 16 + row : 17 + row, :]
        small = small + fs[i, 24:32, :]
    for i in range(6):
        o_kern[i] = small[i : i + 1, :TAPS]
    fill = jnp.zeros((LANE - 8, LANE), F32)
    turned = [
        jnp.concatenate([small[:, LANE * m : LANE * (m + 1)], fill], axis=0).T for m in range(3)
    ]
    o_gain2[...] = turned[0][TAPS : TAPS + 1, :6]
    for m in range(2):
        pair = turned[m + 1][32:34, :6]
        o_gain1[:, 6 * m : 6 * (m + 1)] = jnp.where(j < 2, pair[0:1], pair[1:2])
    store_out.wait()
    store_grad.wait()


def hand_over(*refs):
    n = len(refs) // 2
    for i in range(n):
        refs[n + i][...] = refs[i][...]


def per_device(inputs, lengths, w_first, kernel_w, gain_first, gain_second, w_second, grad_output):
    n_y = lax.axis_size("dp")
    n_tm = lax.axis_size("tm")
    n_z = n_tm // 4
    frames, model = inputs.shape[1:]
    width = w_second.shape[1]
    groups = n_y * n_tm
    vmem = pl.BlockSpec(memory_space=pltpu.VMEM)

    def buf(shape, dtype):
        return pltpu.VMEM(shape, dtype)

    def second(parts, rows):
        return (
            buf((n_z, parts, rows, LANE), BF16),
            buf((2, parts, rows, LANE), BF16),
            buf((2, parts - parts // 2, rows, LANE), BF16),
            buf((4, parts, rows, LANE), BF16),
        )

    def reduced(parts, rows):
        return (
            buf((n_y, n_z, parts, rows, LANE), BF16),
            buf((2, n_z // 2, parts, rows, LANE), BF16),
            buf((2, n_z, parts, rows, LANE), BF16),
        ) + second(parts, rows)

    wide = (frames, model)
    thin = (frames, width)
    padded = (frames + 2 * HALO, width)
    third = (4, frames, 384)
    scratch = [
        buf((model, 2 * width), BF16),
        buf((width, model), BF16),
        buf(wide, BF16),
        buf(wide, BF16),
        buf(wide, BF16),
        buf(wide, BF16),
        buf(wide, F32),
        buf((frames, LANE), F32),
        buf(wide, BF16),
        buf(thin, F32),
        buf(thin, F32),
        buf(padded, F32),
        buf(padded, F32),
        buf(thin, F32),
        buf(thin, F32),
        buf((frames, LANE), F32),
        buf(thin, F32),
        buf(thin, BF16),
        buf(thin, F32),
        buf(wide, F32),
        buf((2, HALO, width), BF16),
        buf((2, HALO, width), BF16),
        buf((2, HALO, width), BF16),
        buf((2, HALO, width), BF16),
        buf(third, BF16),
        buf(third, BF16),
        buf((3, frames, 384), BF16),
        buf((3, frames, 384), BF16),
        buf((3,) + wide, BF16),
        buf((3,) + thin, BF16),
        buf((4, model, LANE), BF16),
        buf((4, width, LANE), BF16),
        buf((LANE, width), F32),
        buf((8, model), F32),
        buf((width, LANE), F32),
        buf((model, LANE), F32),
        reduced(2, 48),
        reduced(5, 16),
        second(4, 48),
        second(4, 16),
        buf((n_y, 48, LANE), BF16),
        buf((n_y - 1, 48, LANE), BF16),
        buf((n_y, 16, LANE), BF16),
        buf((n_y - 1, 16, LANE), BF16),
        buf((4, 32, 384), F32),
        buf((4, 32, 384), BF16),
        buf((4, 32, 384), BF16),
        pltpu.SemaphoreType.DMA((4,)),
        pltpu.SemaphoreType.DMA((2, 4)),
        pltpu.SemaphoreType.DMA((2, 4)),
        pltpu.SemaphoreType.DMA((2, 4)),
        pltpu.SemaphoreType.DMA((2, 36)),
        pltpu.SemaphoreType.DMA((2, 18)),
        pltpu.SemaphoreType.DMA((2, 32)),
        pltpu.SemaphoreType.DMA((2, 3)),
    ]
    hbm = pl.BlockSpec(memory_space=pl.ANY)
    shapes = (
        jax.ShapeDtypeStruct(wide, BF16),
        jax.ShapeDtypeStruct(wide, BF16),
        jax.ShapeDtypeStruct((model // groups, 1, model), F32),
        jax.ShapeDtypeStruct((width // groups, 1, model), F32),
        jax.ShapeDtypeStruct((width // groups, 1, TAPS), F32),
        jax.ShapeDtypeStruct((1, model // groups), F32),
        jax.ShapeDtypeStruct((1, width // groups), F32),
    )
    results = pl.pallas_call(
        functools.partial(kernel, n_y, n_z, n_tm),
        out_shape=shapes,
        in_specs=[pl.BlockSpec(memory_space=pltpu.SMEM), vmem, vmem, hbm, hbm, vmem, vmem, vmem],
        out_specs=(hbm, hbm) + (vmem,) * 5,
        scratch_shapes=scratch,
        compiler_params=pltpu.CompilerParams(
            collective_id=0, has_side_effects=True, vmem_limit_bytes=60 * 1024 * 1024
        ),
        cost_estimate=pl.CostEstimate(
            flops=2 * 3 * frames * model * 3 * width, bytes_accessed=12_000_000, transcendentals=0
        ),
    )(
        lengths,
        inputs[0],
        grad_output[0],
        w_first[0],
        w_second[0],
        kernel_w.transpose(1, 0, 2),
        gain_first,
        gain_second,
    )
    out, grad, one, two, taps, g_one, g_two = pl.pallas_call(
        hand_over,
        out_shape=shapes,
        in_specs=[vmem] * 7,
        out_specs=(vmem,) * 7,
        compiler_params=pltpu.CompilerParams(vmem_limit_bytes=60 * 1024 * 1024),
    )(*results)
    return (
        out[None, None],
        grad[None, None],
        one.transpose(1, 0, 2),
        taps.transpose(1, 2, 0),
        g_one,
        g_two,
        two.transpose(1, 0, 2),
    )


def solution(mesh):
    in_specs = (
        P("dp", "tm", None),
        P("dp"),
        P("segment", None, None),
        P("segment", None, None),
        P("segment", None),
        P("segment", None),
        P("segment", None, None),
        P("dp", "tm", None),
    )
    out_specs = (
        P("segment", "dp", "tm", None),
        P("segment", "dp", "tm", None),
        P("segment", ("dp", "tm"), None),
        P("segment", None, ("dp", "tm")),
        P("segment", ("dp", "tm")),
        P("segment", ("dp", "tm")),
        P("segment", ("dp", "tm"), None),
    )
    return jax.shard_map(
        per_device, mesh=mesh, in_specs=in_specs, out_specs=out_specs, check_vma=False
    )
```

```python
import functools

import jax
import jax.numpy as jnp
from jax import lax
from jax.experimental import pallas as pl
from jax.experimental.pallas import tpu as pltpu
from jax.sharding import PartitionSpec as P

EPS = 1e-05
F32 = jnp.float32
BF16 = jnp.bfloat16
MESH = pl.DeviceIdType.MESH
NT = (((1,), (1,)), ((), ()))
HALO = 16
TAPS = 31
LANE = 128
ROWS = 32
EDGES = ((0, 16), (112, 16))
MIDDLE = ((16, 48), (64, 48))
EVERY = EDGES + MIDDLE


def chunk_rows(chunk):
    return [(EVERY.index(part), pl.ds(*part)) for part in chunk]


def dot(a, b):
    return jnp.dot(a, b, preferred_element_type=F32)


def dot_t(a, b):
    return lax.dot_general(a, b, NT, preferred_element_type=F32)


def kernel(
    n_y,
    n_z,
    n_tm,
    len_ref,
    inp,
    gout,
    w1_hbm,
    w2_hbm,
    kern,
    gain1,
    gain2,
    out_hbm,
    grad_hbm,
    o_one,
    o_two,
    o_kern,
    o_gain1,
    o_gain2,
    w1,
    w2,
    out_ref,
    grad_ref,
    cur,
    e,
    xhat,
    rstd1,
    normed,
    p_buf,
    sig_buf,
    gpad,
    dpad,
    conv,
    zhat,
    rstd2,
    zn_buf,
    act,
    d_act,
    d_norm,
    edge_g,
    edge_d,
    halo_g,
    halo_d,
    dout4,
    dpre4,
    dout_r,
    dpre_r,
    n_raw,
    a_raw,
    n_t,
    a_t,
    gk,
    ebuf,
    tbuf,
    item_a,
    item_b,
    item_c,
    qy,
    y_got,
    fs,
    f_out,
    f_in,
    sem_w,
    sem_h,
    sem_out,
    sem_grad,
    sem_x,
    sem_y,
    sem_z,
    sem_f,
):
    frames, model = inp.shape
    width = w2.shape[0]
    dy = lax.axis_index("dp")
    seg = lax.axis_index("segment")
    t = lax.axis_index("tm")
    c = t % 2
    xl = (t // 2) % 2
    z = t // 4
    j = t % 4
    base = z * 4
    group = [base + xl * 2 + (1 - c), base + (1 - xl) * 2 + c, base + (1 - xl) * 2 + (1 - c)]
    right = (t + 1) % n_tm
    left = (t + n_tm - 1) % n_tm
    first_seg = seg == 0
    last_seg = seg == 1

    def remote(src, dst, sems, index, axis, peer):
        return pltpu.make_async_remote_copy(
            src_ref=src,
            dst_ref=dst,
            send_sem=sems.at[0, index],
            recv_sem=sems.at[1, index],
            device_id={axis: peer},
            device_id_type=MESH,
        )

    load_w1 = pltpu.make_async_copy(w1_hbm, w1, sem_w.at[0])
    load_w2 = pltpu.make_async_copy(w2_hbm, w2, sem_w.at[1])
    store_out = pltpu.make_async_copy(out_ref, out_hbm, sem_w.at[2])
    store_grad = pltpu.make_async_copy(grad_ref, grad_hbm, sem_w.at[3])
    barrier = pltpu.get_barrier_semaphore()
    greet = [("tm", left), ("tm", right), ("segment", 1 - seg)]
    greet += [("tm", g) for g in group]
    greet += [("dp", (dy + d) % n_y) for d in range(1, n_y)]
    greet += [("tm", ((z + d) % n_z) * 4 + j) for d in (1, 2, n_z - 1, n_z - 2)]
    for axis, peer in greet:
        pl.semaphore_signal(barrier, inc=1, device_id={axis: peer}, device_id_type=MESH)

    @pl.when(first_seg)
    def _():
        load_w1.start()
        load_w2.start()

    @pl.when(last_seg)
    def _():
        load_w2.start()
        load_w1.start()

    length = len_ref[0]

    def mask_of(start, rows):
        ids = t * frames + start + lax.broadcasted_iota(jnp.int32, (rows, 1), 0)
        return (ids < length).astype(F32)

    def out_copies(chunk):
        return [
            remote(out_ref.at[rows], cur.at[rows], sem_out, i, "segment", 1 - seg)
            for i, rows in chunk_rows(chunk)
        ]

    def grad_copies(chunk):
        return [
            remote(grad_ref.at[rows], e.at[rows], sem_grad, i, "segment", 1 - seg)
            for i, rows in chunk_rows(chunk)
        ]

    def halo_copies(edge, halo, offset):
        return [
            remote(edge.at[0], halo.at[1], sem_h, offset, "tm", left),
            remote(edge.at[1], halo.at[0], sem_h, offset + 1, "tm", right),
        ]

    def peer_j(d):
        return group[d] % 4

    def dout_copies(chunk):
        return [
            remote(
                dout4.at[peer_j(d), rows], dout_r.at[d, rows], sem_x, 3 * i + d, "tm", group[d]
            )
            for i, rows in chunk_rows(chunk)
            for d in range(3)
        ]

    def dpre_copies(last):
        cols = pl.ds(256, LANE) if last else pl.ds(0, 256)
        return [
            remote(
                dpre4.at[peer_j(d), :, cols],
                dpre_r.at[d, :, cols],
                sem_x,
                12 + 3 * last + d,
                "tm",
                group[d],
            )
            for d in range(3)
        ]

    def turned_copies(part, forward=False):
        own, got = (act, a_raw) if part > 3 else (normed, n_raw)
        rows = pl.ds(64 * (part - 4), 64) if part > 3 else pl.ds(32 * part, 32)

        def one(src, dst, d):
            return remote(
                src.at[rows], got.at[dst, rows], sem_x, 18 + 3 * part + d, "tm", group[d % 2]
            )

        return [one(got.at[1], 2, 2)] if forward else [one(own, 0, 0), one(own, 1, 1)]

    def forward_turned(parts):
        for part in parts:
            turned_copies(part)[1].wait_recv()
            turned_copies(part, True)[0].start()

    def wait_turned(parts):
        for part in parts:
            copies = turned_copies(part)
            copies[0].wait()
            copies[1].wait_send()
            turned_copies(part, True)[0].wait()

    def start_all(copies):
        for copy in copies:
            copy.start()

    def stacked(ref, chunk):
        return jnp.concatenate([ref[start : start + size] for start, size in chunk], axis=0)

    def spread(value, chunk):
        at = 0
        for start, size in chunk:
            yield slice(start, start + size), value[at : at + size]
            at += size

    def pieces(chunk):
        return [(at, min(ROWS, start + size - at)) for start, size in chunk for at in range(start, start + size, ROWS)]

    def upper(chunk):
        for start, size in pieces(chunk):
            rows = slice(start, start + size)
            d_out = (e[rows, :].astype(F32) * mask_of(start, size)).astype(BF16)
            for i in range(4):
                dout4[i, rows, :] = d_out[:, 384 * i : 384 * (i + 1)]
        d_out = jnp.concatenate([stacked(dout4.at[i], chunk) for i in range(4)], axis=1)
        for n in range(width // 256):
            cols = slice(256 * n, 256 * (n + 1))
            for rows, value in spread(dot_t(d_out, w2[cols, :]), chunk):
                d_act[rows, cols] = value

    def taps_over(src, block, flip):
        cols = pl.ds(pl.multiple_of(block * LANE, LANE), LANE)
        whole = src[:, cols]
        total = jnp.zeros((frames, LANE), F32)
        for r in range(8):
            moved = whole if r == 0 else pltpu.roll(whole, whole.shape[0] - r, 0)
            for k in range(TAPS):
                if (k + 1) % 8 == r:
                    at = k + 1 - r
                    tap = TAPS - 1 - k if flip else k
                    total = total + kern[tap, :, cols] * moved[at : at + frames]
        return cols, total

    def turn_normed(slots):
        for slot in slots:
            src = normed if slot == 0 else n_raw.at[slot - 1]
            for i in range(model // LANE):
                cols = slice(LANE * i, LANE * (i + 1))
                n_t[slot, cols, :] = src[:, cols].T

    def turn_act(slots):
        for slot in slots:
            src = act if slot == 0 else a_raw.at[slot - 1]
            for i in range(width // LANE):
                cols = slice(LANE * i, LANE * (i + 1))
                a_t[slot, cols, :] = src[:, cols].T

    for i in range(model // LANE):
        cols = slice(LANE * i, LANE * (i + 1))
        tbuf[cols, :] = jnp.broadcast_to(1.0 / gain1[:, cols], (LANE, LANE)).T
    gk[...] = jnp.zeros_like(gk)

    @pl.when(last_seg)
    def _():
        e[...] = gout[...]
        load_w2.wait()
        upper(EVERY)

    @pl.when(first_seg)
    def _():
        cur[...] = inp[...]

    pl.semaphore_wait(barrier, len(greet))

    @pl.when(last_seg)
    def _():
        start_all(dout_copies(EVERY))

    def front(chunk, edge):
        for start, size in pieces(chunk):
            rows = slice(start, start + size)
            x = cur[rows, :].astype(F32)
            centred = x - jnp.mean(x, axis=-1, keepdims=True)
            rstd = lax.rsqrt(jnp.mean(centred * centred, axis=-1, keepdims=True) + EPS)
            hat = centred * rstd
            xhat[rows, :] = hat
            rstd1[rows, :] = jnp.broadcast_to(rstd, (size, LANE))
            normed[rows, :] = (hat * gain1[...]).astype(BF16)
        x = stacked(normed, chunk)
        mask = jnp.concatenate([mask_of(start, size) for start, size in chunk], axis=0)
        for n in range(width // 256):
            cols = slice(256 * n, 256 * (n + 1))
            q_cols = slice(width + 256 * n, width + 256 * (n + 1))
            p = dot(x, w1[:, cols])
            sig = jax.nn.sigmoid(dot(x, w1[:, q_cols]))
            gated = (p * sig * mask).astype(BF16)
            for rows, value in spread(p, chunk):
                p_buf[rows, cols] = value
            for rows, value in spread(sig, chunk):
                sig_buf[rows, cols] = value
            for rows, value in spread(gated.astype(F32), chunk):
                gpad[HALO + rows.start : HALO + rows.stop, cols] = value
            if edge:
                edge_g[0, :, cols] = gated[:HALO]
                edge_g[1, :, cols] = gated[HALO:]

    @pl.when(last_seg)
    def _():
        for copy in out_copies(EDGES):
            copy.wait_recv()

    @pl.when(first_seg)
    def _():
        load_w1.wait()

    @pl.when(last_seg)
    def _():
        load_w1.wait()

    front(EDGES, True)
    copies = halo_copies(edge_g, halo_g, 0)
    start_all(copies)

    @pl.when(last_seg)
    def _():
        for copy in out_copies(MIDDLE):
            copy.wait_recv()

    front(MIDDLE, False)

    @pl.when(last_seg)
    def _():
        start_all(turned_copies(0))

    maskf = mask_of(0, frames)
    for copy in copies:
        copy.wait()
    has_left = (t > 0).astype(F32)
    has_right = (t < n_tm - 1).astype(F32)
    gpad[0:HALO, :] = halo_g[0].astype(F32) * has_left
    gpad[HALO + frames :, :] = halo_g[1].astype(F32) * has_right

    def conv_block(block, carry):
        cols, total = taps_over(gpad, block, False)
        conv[:, cols] = total
        return carry

    lax.fori_loop(0, width // LANE, conv_block, 0)

    def act_rows(chunk):
        for start, size in pieces(chunk):
            rows = slice(start, start + size)
            x = conv[rows, :]
            centred = x - jnp.mean(x, axis=-1, keepdims=True)
            rstd = lax.rsqrt(jnp.mean(centred * centred, axis=-1, keepdims=True) + EPS)
            hat = centred * rstd
            zn = hat * gain2[...]
            zhat[rows, :] = hat
            zn_buf[rows, :] = zn
            rstd2[rows, :] = jnp.broadcast_to(rstd, (size, LANE))
            act[rows, :] = (zn * jax.nn.sigmoid(zn)).astype(BF16)

    def out_rows(chunk):
        x = stacked(act, chunk)
        for n in range(model // 512):
            cols = slice(512 * n, 512 * (n + 1))
            for rows, value in spread(dot(x, w2[:, cols]), chunk):
                mask = mask_of(rows.start, rows.stop - rows.start)
                out_ref[rows, cols] = (cur[rows, cols].astype(F32) + mask * value).astype(BF16)

    @pl.when(first_seg)
    def _():
        load_w2.wait()
        for chunk in (EDGES, MIDDLE):
            act_rows(chunk)
            out_rows(chunk)
            start_all(out_copies(chunk))
        store_out.start()
        turn_normed((0,))
        turn_act((0,))
        for copy in out_copies(EVERY):
            copy.wait_send()
        for part in range(6):
            start_all(turned_copies(part))
        forward_turned(range(6))
        wait_turned(range(6))
        turn_normed((1, 2, 3))
        turn_act((1, 2, 3))

    @pl.when(last_seg)
    def _():
        start_all(turned_copies(1))
        act_rows(EVERY)

    def conv_grad(chunk):
        for start, size in pieces(chunk):
            rows = slice(start, start + size)
            zn = zn_buf[rows, :]
            hat = zhat[rows, :]
            sg = jax.nn.sigmoid(zn)
            d_zn = d_act[rows, :] * (sg + zn * sg * (1.0 - sg))
            gk[TAPS : TAPS + 1, :] += jnp.sum(d_zn * hat, axis=0, keepdims=True)
            d_hat = d_zn * gain2[...]
            m_one = jnp.mean(d_hat, axis=-1, keepdims=True)
            m_two = jnp.mean(d_hat * hat, axis=-1, keepdims=True)
            d_conv = rstd2[rows, 0:1] * (d_hat - m_one - hat * m_two)
            dpad[HALO + start : HALO + start + size, :] = d_conv

    halos = halo_copies(edge_d, halo_d, 2)

    def send_edges():
        edge_d[0] = dpad[HALO : 2 * HALO, :].astype(BF16)
        edge_d[1] = dpad[frames : HALO + frames, :].astype(BF16)
        start_all(halos)

    @pl.when(first_seg)
    def _():
        for chunk in (EDGES, MIDDLE[:1], MIDDLE[1:]):
            for copy in grad_copies(chunk):
                copy.wait_recv()
            upper(chunk)
            conv_grad(chunk)
            if chunk is EDGES:
                send_edges()
            start_all(dout_copies(chunk))

    @pl.when(last_seg)
    def _():
        conv_grad(EDGES)
        send_edges()
        conv_grad(MIDDLE)

    for copy in halos:
        copy.wait()

    @pl.when(last_seg)
    def _():
        start_all(turned_copies(2))

    dpad[0:HALO, :] = halo_d[0].astype(F32) * has_left
    dpad[HALO + frames :, :] = halo_d[1].astype(F32) * has_right

    for half in range(2):

        def pre_block(block, carry):
            cols, total = taps_over(dpad, half * 3 + block, True)
            d_gated = total * maskf
            sig = sig_buf[:, cols]
            d_p = d_gated * sig
            d_q = d_p * p_buf[:, cols] * (1.0 - sig)
            part = pl.ds(pl.multiple_of(block * LANE, LANE), LANE)
            dpre4[half, :, part] = d_p.astype(BF16)
            dpre4[2 + half, :, part] = d_q.astype(BF16)
            return carry

        lax.fori_loop(0, 3, pre_block, 0)

    @pl.when(first_seg)
    def _():
        start_all(dpre_copies(0) + dpre_copies(1))

    def grad_rows(chunk):
        d_pre = jnp.concatenate([stacked(dpre4.at[i], chunk) for i in range(4)], axis=1)
        for n in range(model // 512):
            cols = slice(512 * n, 512 * (n + 1))
            for rows, value in spread(dot_t(d_pre, w1[cols, :]), chunk):
                d_norm[rows, cols] = value
        for start, size in pieces(chunk):
            rows = slice(start, start + size)
            d_normed = d_norm[rows, :]
            hat = xhat[rows, :]
            d_hat = d_normed * gain1[...]
            m_one = jnp.mean(d_hat, axis=-1, keepdims=True)
            m_two = jnp.mean(d_hat * hat, axis=-1, keepdims=True)
            d_h = rstd1[rows, 0:1] * (d_hat - m_one - hat * m_two)
            grad_ref[rows, :] = (e[rows, :].astype(F32) + d_h).astype(BF16)

    @pl.when(last_seg)
    def _():
        for chunk in (EDGES, MIDDLE):
            grad_rows(chunk)
            start_all(grad_copies(chunk))
        for part in (4, 5, 3):
            start_all(turned_copies(part))
        start_all(dpre_copies(0) + dpre_copies(1))
        store_grad.start()
        out_rows(EVERY)
        store_out.start()
        turn_act((0,))
        turn_normed((0,))
        forward_turned((0, 1, 2, 4, 5))
        wait_turned((0, 1, 2, 4, 5))
        turn_act((1, 2, 3))
        for copy in grad_copies(EVERY):
            copy.wait_send()

    def tap_grads(block, carry):
        cols = pl.ds(pl.multiple_of(block * LANE, LANE), LANE)
        whole = gpad[:, cols]
        d_conv = dpad[HALO : HALO + frames, cols]
        for r in range(8):
            moved = whole if r == 0 else pltpu.roll(whole, whole.shape[0] - r, 0)
            for k in range(TAPS):
                if (k + 1) % 8 == r:
                    at = k + 1 - r
                    gk[k : k + 1, cols] = jnp.sum(
                        moved[at : at + frames] * d_conv, axis=0, keepdims=True
                    )
        return carry

    low, high = pl.ds(0, n_z // 2), pl.ds(n_z // 2, n_z // 2)
    up, down, far = (dy + 1) % n_y, (dy + n_y - 1) % n_y, (dy + 2) % n_y

    def y_far(buf, inner, base_sem):
        return [
            remote(buf.at[far, low], inner.at[0], sem_y, base_sem, "dp", up),
            remote(buf.at[far, high], inner.at[1], sem_y, base_sem + 1, "dp", down),
        ]

    def y_direct(buf, got, base_sem):
        return [
            remote(buf.at[up, high], got.at[0, high], sem_y, base_sem + 2, "dp", up),
            remote(buf.at[down, low], got.at[1, low], sem_y, base_sem + 3, "dp", down),
        ]

    def y_summed(buf, got, base_sem):
        return [
            remote(buf.at[up, low], got.at[0, low], sem_y, base_sem + 4, "dp", up),
            remote(buf.at[down, high], got.at[1, high], sem_y, base_sem + 5, "dp", down),
        ]

    def z_peer(d):
        return ((z + d + n_z) % n_z) * 4 + j

    def z_far(item):
        q_buf, in_three, in_four, _, base_sem = item[3:]
        parts = q_buf.shape[1] // 2
        copies = []
        for i, d in enumerate((1, -1)):
            over = pl.ds(parts * i, parts if i == 0 else q_buf.shape[1] - parts)
            three, four = (z + 3 * d + n_z) % n_z, (z + 4) % n_z
            to = z_peer(2 * d)
            at = base_sem + 2 * i
            copies.append(remote(q_buf.at[three], in_three.at[i], sem_z, at, "tm", to))
            into = in_four.at[i, pl.ds(0, over.size)]
            copies.append(remote(q_buf.at[four, over], into, sem_z, at + 1, "tm", to))
        return copies

    def z_near(item):
        q_buf, _, _, got, base_sem = item[3:]
        copies = []
        for i, d in enumerate((2, -2, 1, -1)):
            peer = (z + d + n_z) % n_z
            at = base_sem + 4 + i
            copies.append(remote(q_buf.at[peer], got.at[i], sem_z, at, "tm", z_peer(d)))
        return copies

    def z_relay(item):
        q_buf, in_three, in_four, _, _ = item[3:]
        parts = q_buf.shape[1] // 2
        for copy in z_far(item):
            copy.wait()
        copies = z_near(item)
        for i, d in enumerate((2, -2)):
            peer = (z + d + n_z) % n_z
            for m in range(parts if i == 0 else q_buf.shape[1] - parts):
                k = parts * i + m
                q_buf[peer, k] = (q_buf[peer, k].astype(F32) + in_four[i, m].astype(F32)).astype(BF16)
            copies[i].start()
        for i, d in enumerate((1, -1)):
            peer = (z + d + n_z) % n_z
            q_buf[peer] = (q_buf[peer].astype(F32) + in_three[i].astype(F32)).astype(BF16)
            copies[2 + i].start()

    def z_total(item):
        q_buf, _, _, got, _ = item[3:]
        for copy in z_near(item):
            copy.wait()
        total = q_buf[z].astype(F32)
        for i in range(4):
            total = total + got[i].astype(F32)
        return total

    def last_copies(buf, got, base_sem):
        return [
            remote(buf.at[(dy + d) % n_y], got.at[d - 1], sem_y, base_sem + d, "dp", (dy + d) % n_y)
            for d in range(1, n_y)
        ]

    def last_total(buf, got, base_sem):
        for copy in last_copies(buf, got, base_sem):
            copy.wait()
        total = buf[dy].astype(F32)
        for d in range(n_y - 1):
            total = total + got[d].astype(F32)
        return total

    rows_one = model // n_y
    rows_two = width // n_y

    for copy in dout_copies(EVERY):
        copy.wait()
    rhs_two = jnp.concatenate([dout4[j]] + [dout_r[d] for d in range(3)], axis=0)
    item_a = tuple(item_a) + (0,)
    item_b = tuple(item_b) + (8,)
    item_c = (None,) * 3 + tuple(item_c) + (16,)
    qy_c = (qy, y_got, 11)

    def product(turned, peer, rows, rhs):
        start = pl.multiple_of(peer * rows, rows)
        lhs = jnp.concatenate([turned[i, pl.ds(start, rows), :] for i in range(4)], axis=1)
        return dot(lhs, rhs)

    def part_two(peer):
        part = product(a_t, peer, rows_two, rhs_two)
        for i in range(n_z):
            mine = part[24 * i : 24 * (i + 1)]
            blocks = [mine[:, LANE * m : LANE * (m + 1)] for m in range(3)]
            at = pl.multiple_of(peer * rows_two + 24 * i, 8)
            extra = ebuf[pl.ds(at, 24), :]
            fill = extra[:8] + pltpu.roll(extra[8:16], 32, 1) + pltpu.roll(extra[16:], 64, 1)
            whole = jnp.concatenate(blocks + [fill], axis=0).astype(BF16)
            for m in range(5):
                item_b[0][peer, i, m] = whole[16 * m : 16 * (m + 1)]

    def part_one(peer):
        part = product(n_t, peer, rows_one, rhs_one)
        for i in range(n_z):
            for m in range(2):
                mine = part[48 * i : 48 * (i + 1), LANE * m : LANE * (m + 1)]
                item_a[0][peer, i, m] = mine.astype(BF16)

    def part_last(d):
        peer = (z + d + n_z) % n_z
        starts = [pl.multiple_of(rows_one * yy + 48 * peer, 16) for yy in range(n_y)]
        lhs = jnp.concatenate(
            [
                jnp.concatenate([n_t[i, pl.ds(start, 48), :] for i in range(4)], axis=1)
                for start in starts
            ],
            axis=0,
        )
        part = dot(lhs, rhs_last)
        for yy in range(n_y):
            item_c[3][peer, yy] = part[48 * yy : 48 * (yy + 1)].astype(BF16)

    def y_begin(item, fill, base_sem):
        buf, inner, got = item[:3]
        fill(far)
        start_all(y_far(buf, inner, base_sem))
        fill(up)
        fill(down)
        start_all(y_direct(buf, got, base_sem))
        fill(dy)

    def y_relay(item, base_sem):
        buf, inner, got = item[:3]
        for copy in y_far(buf, inner, base_sem):
            copy.wait()
        for i in range(n_z // 2):
            k = n_z // 2 + i
            buf[up, i] = (buf[up, i].astype(F32) + inner[0, i].astype(F32)).astype(BF16)
            buf[down, k] = (buf[down, k].astype(F32) + inner[1, i].astype(F32)).astype(BF16)
        start_all(y_summed(buf, got, base_sem))

    def y_finish(item, base_sem):
        buf, _, got, q_buf = item[:4]
        for copy in y_direct(buf, got, base_sem) + y_summed(buf, got, base_sem):
            copy.wait()

        def total(d):
            at = (z + d) % n_z
            mine = buf[dy, at].astype(F32) + got[0, at].astype(F32) + got[1, at].astype(F32)
            q_buf[at] = mine.astype(BF16)

        for d in (3, 5, 4):
            total(d)
        start_all(z_far(item))
        for d in (2, 6, 1, 7, 0):
            total(d)

    lax.fori_loop(0, width // LANE, tap_grads, 0)
    for i in range(width // LANE):
        cols = slice(LANE * i, LANE * (i + 1))
        ebuf[cols, :] = gk[:, cols].T
    y_begin(item_b, part_two, 6)

    @pl.when(last_seg)
    def _():
        forward_turned((3,))
        wait_turned((3,))
        turn_normed((1, 2, 3))

    for copy in dpre_copies(0):
        copy.wait()
    rhs_one = jnp.concatenate([dpre4[j, :, :256]] + [dpre_r[d, :, :256] for d in range(3)], axis=0)
    part_one(far)
    start_all(y_far(item_a[0], item_a[1], 0))
    for copy in dpre_copies(1):
        copy.wait()
    rhs_last = jnp.concatenate([dpre4[j, :, 256:]] + [dpre_r[d, :, 256:] for d in range(3)], axis=0)
    for d in (3, -3, 4):
        part_last(d)
    start_all(z_far(item_c))
    part_one(up)
    part_one(down)
    y_relay(item_b, 6)
    start_all(y_direct(item_a[0], item_a[2], 0))
    part_one(dy)
    for d in (1, -1, 2, -2, 0):
        part_last(d)

    @pl.when(first_seg)
    def _():
        grad_rows(EVERY)
        store_grad.start()

    y_relay(item_a, 0)
    z_relay(item_c)
    y_finish(item_b, 6)
    y_finish(item_a, 0)
    qy[...] = z_total(item_c).astype(BF16)
    start_all(last_copies(*qy_c))
    z_relay(item_b)
    z_relay(item_a)

    fs[...] = jnp.zeros_like(fs)
    total = z_total(item_b)
    total = jnp.concatenate([total[m] for m in range(5)], axis=0)
    for i in range(4):
        for m in range(3):
            at = 24 * m + 6 * i
            fs[i, 16:22, LANE * m : LANE * (m + 1)] = total[at : at + 6]
    fill = total[72:]
    extra = jnp.concatenate([fill, pltpu.roll(fill, 96, 1), pltpu.roll(fill, 64, 1)], axis=0)
    for i in range(4):
        fs[i, 24:30, 0:LANE] = extra[6 * i : 6 * (i + 1)]
    total = z_total(item_a)
    for i in range(4):
        for m in range(2):
            fs[i, 0:12, LANE * m : LANE * (m + 1)] = total[m, 12 * i : 12 * (i + 1)]
    final = last_total(*qy_c)
    mine = jnp.concatenate([total[0], total[1], final], axis=1)
    place = pl.ds(pl.multiple_of((dy * n_z + z) * 48, 16), 48)
    weights = w1[place, pl.ds(pl.multiple_of(j * 384, LANE), 384)].astype(F32)
    gains = jnp.sum(mine * weights, axis=-1, keepdims=True) * tbuf[place, :]
    for i in range(4):
        fs[i, 0:12, 256:] = final[12 * i : 12 * (i + 1)]
        for m in range(2):
            at = 12 * i + 6 * m
            fs[i, 24:30, LANE * (m + 1) : LANE * (m + 2)] = gains[at : at + 6]
    f_out[...] = fs[...].astype(BF16)
    copies = [remote(f_out.at[peer_j(d)], f_in.at[j], sem_f, d, "tm", group[d]) for d in range(3)]
    start_all(copies)
    f_in[j] = f_out[j]
    for copy in copies:
        copy.wait()
    fs[...] = f_in[...].astype(F32)
    small = jnp.zeros((8, 3 * LANE), F32)
    for i in range(4):
        cols = slice(384 * i, 384 * (i + 1))
        for row in range(12):
            o_one[row, :, cols] = fs[i, row : row + 1, :]
        for row in range(6):
            o_two[row, :, cols] = fs[i, 16 + row : 17 + row, :]
        small = small + fs[i, 24:32, :]
    for i in range(6):
        o_kern[i] = small[i : i + 1, :TAPS]
    fill = jnp.zeros((LANE - 8, LANE), F32)
    turned = [
        jnp.concatenate([small[:, LANE * m : LANE * (m + 1)], fill], axis=0).T for m in range(3)
    ]
    o_gain2[...] = turned[0][TAPS : TAPS + 1, :6]
    for m in range(2):
        o_gain1[:, 6 * m : 6 * (m + 1)] = turned[m + 1][0:1, :6]
    store_out.wait()
    store_grad.wait()


def hand_over(*refs):
    n = len(refs) // 2
    for i in range(n):
        refs[n + i][...] = refs[i][...]


def per_device(inputs, lengths, w_first, kernel_w, gain_first, gain_second, w_second, grad_output):
    n_y = lax.axis_size("dp")
    n_tm = lax.axis_size("tm")
    n_z = n_tm // 4
    frames, model = inputs.shape[1:]
    width = w_second.shape[1]
    groups = n_y * n_tm
    vmem = pl.BlockSpec(memory_space=pltpu.VMEM)

    def buf(shape, dtype):
        return pltpu.VMEM(shape, dtype)

    def second(parts, rows):
        return (
            buf((n_z, parts, rows, LANE), BF16),
            buf((2, parts, rows, LANE), BF16),
            buf((2, parts - parts // 2, rows, LANE), BF16),
            buf((4, parts, rows, LANE), BF16),
        )

    def reduced(parts, rows):
        return (
            buf((n_y, n_z, parts, rows, LANE), BF16),
            buf((2, n_z // 2, parts, rows, LANE), BF16),
            buf((2, n_z, parts, rows, LANE), BF16),
        ) + second(parts, rows)

    wide = (frames, model)
    thin = (frames, width)
    padded = (frames + 2 * HALO, width)
    third = (4, frames, 384)
    scratch = [
        buf((model, 2 * width), BF16),
        buf((width, model), BF16),
        buf(wide, BF16),
        buf(wide, BF16),
        buf(wide, BF16),
        buf(wide, BF16),
        buf(wide, F32),
        buf((frames, LANE), F32),
        buf(wide, BF16),
        buf(thin, F32),
        buf(thin, F32),
        buf(padded, F32),
        buf(padded, F32),
        buf(thin, F32),
        buf(thin, F32),
        buf((frames, LANE), F32),
        buf(thin, F32),
        buf(thin, BF16),
        buf(thin, F32),
        buf(wide, F32),
        buf((2, HALO, width), BF16),
        buf((2, HALO, width), BF16),
        buf((2, HALO, width), BF16),
        buf((2, HALO, width), BF16),
        buf(third, BF16),
        buf(third, BF16),
        buf((3, frames, 384), BF16),
        buf((3, frames, 384), BF16),
        buf((3,) + wide, BF16),
        buf((3,) + thin, BF16),
        buf((4, model, LANE), BF16),
        buf((4, width, LANE), BF16),
        buf((LANE, width), F32),
        buf((width, LANE), F32),
        buf((model, LANE), F32),
        reduced(2, 48),
        reduced(5, 16),
        second(4, 48),
        buf((n_y, 48, LANE), BF16),
        buf((n_y - 1, 48, LANE), BF16),
        buf((4, 32, 384), F32),
        buf((4, 32, 384), BF16),
        buf((4, 32, 384), BF16),
        pltpu.SemaphoreType.DMA((4,)),
        pltpu.SemaphoreType.DMA((2, 4)),
        pltpu.SemaphoreType.DMA((2, 4)),
        pltpu.SemaphoreType.DMA((2, 4)),
        pltpu.SemaphoreType.DMA((2, 36)),
        pltpu.SemaphoreType.DMA((2, 15)),
        pltpu.SemaphoreType.DMA((2, 24)),
        pltpu.SemaphoreType.DMA((2, 3)),
    ]
    hbm = pl.BlockSpec(memory_space=pl.ANY)
    shapes = (
        jax.ShapeDtypeStruct(wide, BF16),
        jax.ShapeDtypeStruct(wide, BF16),
        jax.ShapeDtypeStruct((model // groups, 1, model), F32),
        jax.ShapeDtypeStruct((width // groups, 1, model), F32),
        jax.ShapeDtypeStruct((width // groups, 1, TAPS), F32),
        jax.ShapeDtypeStruct((1, model // groups), F32),
        jax.ShapeDtypeStruct((1, width // groups), F32),
    )
    results = pl.pallas_call(
        functools.partial(kernel, n_y, n_z, n_tm),
        out_shape=shapes,
        in_specs=[pl.BlockSpec(memory_space=pltpu.SMEM), vmem, vmem, hbm, hbm, vmem, vmem, vmem],
        out_specs=(hbm, hbm) + (vmem,) * 5,
        scratch_shapes=scratch,
        compiler_params=pltpu.CompilerParams(
            collective_id=0, has_side_effects=True, vmem_limit_bytes=60 * 1024 * 1024
        ),
        cost_estimate=pl.CostEstimate(
            flops=2 * 3 * frames * model * 3 * width, bytes_accessed=12_000_000, transcendentals=0
        ),
    )(
        lengths,
        inputs[0],
        grad_output[0],
        w_first[0],
        w_second[0],
        kernel_w.transpose(1, 0, 2),
        gain_first,
        gain_second,
    )
    out, grad, one, two, taps, g_one, g_two = pl.pallas_call(
        hand_over,
        out_shape=shapes,
        in_specs=[vmem] * 7,
        out_specs=(vmem,) * 7,
        compiler_params=pltpu.CompilerParams(vmem_limit_bytes=60 * 1024 * 1024),
    )(*results)
    return (
        out[None, None],
        grad[None, None],
        one.transpose(1, 0, 2),
        taps.transpose(1, 2, 0),
        g_one,
        g_two,
        two.transpose(1, 0, 2),
    )


def solution(mesh):
    in_specs = (
        P("dp", "tm", None),
        P("dp"),
        P("segment", None, None),
        P("segment", None, None),
        P("segment", None),
        P("segment", None),
        P("segment", None, None),
        P("dp", "tm", None),
    )
    out_specs = (
        P("segment", "dp", "tm", None),
        P("segment", "dp", "tm", None),
        P("segment", ("dp", "tm"), None),
        P("segment", None, ("dp", "tm")),
        P("segment", ("dp", "tm")),
        P("segment", ("dp", "tm")),
        P("segment", ("dp", "tm"), None),
    )
    return jax.shard_map(
        per_device, mesh=mesh, in_specs=in_specs, out_specs=out_specs, check_vma=False
    )
```

```python
import functools

import jax
import jax.numpy as jnp
from jax import lax
from jax.experimental import pallas as pl
from jax.experimental.pallas import tpu as pltpu
from jax.sharding import PartitionSpec as P

EPS = 1e-05
F32 = jnp.float32
BF16 = jnp.bfloat16
MESH = pl.DeviceIdType.MESH
NT = (((1,), (1,)), ((), ()))
HALO = 16
TAPS = 31
LANE = 128
ROWS = 32
EDGES = ((0, 16), (112, 16))
MIDDLE = ((16, 48), (64, 48))
EVERY = EDGES + MIDDLE


def chunk_rows(chunk):
    return [(EVERY.index(part), pl.ds(*part)) for part in chunk]


def dot(a, b):
    return jnp.dot(a, b, preferred_element_type=F32)


def dot_t(a, b):
    return lax.dot_general(a, b, NT, preferred_element_type=F32)


def kernel(
    n_y,
    n_z,
    n_tm,
    len_ref,
    inp,
    gout,
    w1_hbm,
    w2_hbm,
    kern,
    gain1,
    gain2,
    out_hbm,
    grad_hbm,
    o_one,
    o_two,
    o_kern,
    o_gain1,
    o_gain2,
    w1,
    w2,
    out_ref,
    grad_ref,
    cur,
    e,
    xhat,
    rstd1,
    normed,
    p_buf,
    sig_buf,
    gpad,
    dpad,
    conv,
    zhat,
    rstd2,
    zn_buf,
    act,
    d_act,
    d_norm,
    edge_g,
    edge_d,
    halo_g,
    halo_d,
    dout4,
    dpre4,
    dout_r,
    dpre_r,
    n_raw,
    a_raw,
    n_t,
    a_t,
    gk,
    ebuf,
    tbuf,
    item_a,
    item_b,
    item_c,
    qy,
    y_got,
    fs,
    f_out,
    f_in,
    sem_w,
    sem_h,
    sem_out,
    sem_grad,
    sem_x,
    sem_y,
    sem_z,
    sem_f,
):
    frames, model = inp.shape
    width = w2.shape[0]
    dy = lax.axis_index("dp")
    seg = lax.axis_index("segment")
    t = lax.axis_index("tm")
    c = t % 2
    xl = (t // 2) % 2
    z = t // 4
    j = t % 4
    base = z * 4
    group = [base + xl * 2 + (1 - c), base + (1 - xl) * 2 + c, base + (1 - xl) * 2 + (1 - c)]
    right = (t + 1) % n_tm
    left = (t + n_tm - 1) % n_tm
    first_seg = seg == 0
    last_seg = seg == 1

    def remote(src, dst, sems, index, axis, peer):
        return pltpu.make_async_remote_copy(
            src_ref=src,
            dst_ref=dst,
            send_sem=sems.at[0, index],
            recv_sem=sems.at[1, index],
            device_id={axis: peer},
            device_id_type=MESH,
        )

    load_w1 = pltpu.make_async_copy(w1_hbm, w1, sem_w.at[0])
    load_w2 = pltpu.make_async_copy(w2_hbm, w2, sem_w.at[1])
    store_out = pltpu.make_async_copy(out_ref, out_hbm, sem_w.at[2])
    store_grad = pltpu.make_async_copy(grad_ref, grad_hbm, sem_w.at[3])
    barrier = pltpu.get_barrier_semaphore()
    greet = [("tm", left), ("tm", right), ("segment", 1 - seg)]
    greet += [("tm", g) for g in group]
    greet += [("dp", (dy + d) % n_y) for d in range(1, n_y)]
    greet += [("tm", ((z + d) % n_z) * 4 + j) for d in (1, 2, n_z - 1, n_z - 2)]
    for axis, peer in greet:
        pl.semaphore_signal(barrier, inc=1, device_id={axis: peer}, device_id_type=MESH)

    @pl.when(first_seg)
    def _():
        load_w1.start()
        load_w2.start()

    @pl.when(last_seg)
    def _():
        load_w2.start()
        load_w1.start()

    length = len_ref[0]

    def mask_of(start, rows):
        ids = t * frames + start + lax.broadcasted_iota(jnp.int32, (rows, 1), 0)
        return (ids < length).astype(F32)

    def out_copies(chunk):
        return [
            remote(out_ref.at[rows], cur.at[rows], sem_out, i, "segment", 1 - seg)
            for i, rows in chunk_rows(chunk)
        ]

    def grad_copies(chunk):
        return [
            remote(grad_ref.at[rows], e.at[rows], sem_grad, i, "segment", 1 - seg)
            for i, rows in chunk_rows(chunk)
        ]

    def halo_copies(edge, halo, offset):
        return [
            remote(edge.at[0], halo.at[1], sem_h, offset, "tm", left),
            remote(edge.at[1], halo.at[0], sem_h, offset + 1, "tm", right),
        ]

    def peer_j(d):
        return group[d] % 4

    def dout_copies(chunk):
        return [
            remote(
                dout4.at[peer_j(d), rows], dout_r.at[d, rows], sem_x, 3 * i + d, "tm", group[d]
            )
            for i, rows in chunk_rows(chunk)
            for d in range(3)
        ]

    def dpre_copies(last):
        cols = pl.ds(256, LANE) if last else pl.ds(0, 256)
        return [
            remote(
                dpre4.at[peer_j(d), :, cols],
                dpre_r.at[d, :, cols],
                sem_x,
                12 + 3 * last + d,
                "tm",
                group[d],
            )
            for d in range(3)
        ]

    def turned_copies(part, forward=False):
        own, got = (act, a_raw) if part > 3 else (normed, n_raw)
        rows = pl.ds(64 * (part - 4), 64) if part > 3 else pl.ds(32 * part, 32)

        def one(src, dst, d):
            return remote(
                src.at[rows], got.at[dst, rows], sem_x, 18 + 3 * part + d, "tm", group[d % 2]
            )

        return [one(got.at[1], 2, 2)] if forward else [one(own, 0, 0), one(own, 1, 1)]

    def forward_turned(parts):
        for part in parts:
            turned_copies(part)[1].wait_recv()
            turned_copies(part, True)[0].start()

    def wait_turned(parts):
        for part in parts:
            copies = turned_copies(part)
            copies[0].wait()
            copies[1].wait_send()
            turned_copies(part, True)[0].wait()

    def start_all(copies):
        for copy in copies:
            copy.start()

    def stacked(ref, chunk):
        return jnp.concatenate([ref[start : start + size] for start, size in chunk], axis=0)

    def spread(value, chunk):
        at = 0
        for start, size in chunk:
            yield slice(start, start + size), value[at : at + size]
            at += size

    def pieces(chunk):
        return [(at, min(ROWS, start + size - at)) for start, size in chunk for at in range(start, start + size, ROWS)]

    def upper(chunk):
        for start, size in pieces(chunk):
            rows = slice(start, start + size)
            d_out = (e[rows, :].astype(F32) * mask_of(start, size)).astype(BF16)
            for i in range(4):
                dout4[i, rows, :] = d_out[:, 384 * i : 384 * (i + 1)]
        d_out = jnp.concatenate([stacked(dout4.at[i], chunk) for i in range(4)], axis=1)
        for n in range(width // 256):
            cols = slice(256 * n, 256 * (n + 1))
            for rows, value in spread(dot_t(d_out, w2[cols, :]), chunk):
                d_act[rows, cols] = value

    def taps_over(src, block, flip):
        cols = pl.ds(pl.multiple_of(block * LANE, LANE), LANE)
        whole = src[:, cols]
        total = jnp.zeros((frames, LANE), F32)
        for r in range(8):
            moved = whole if r == 0 else pltpu.roll(whole, whole.shape[0] - r, 0)
            for k in range(TAPS):
                if (k + 1) % 8 == r:
                    at = k + 1 - r
                    tap = TAPS - 1 - k if flip else k
                    total = total + kern[tap, :, cols] * moved[at : at + frames]
        return cols, total

    def turn_normed(slots):
        for slot in slots:
            src = normed if slot == 0 else n_raw.at[slot - 1]
            for i in range(model // LANE):
                cols = slice(LANE * i, LANE * (i + 1))
                n_t[slot, cols, :] = src[:, cols].T

    def turn_act(slots):
        for slot in slots:
            src = act if slot == 0 else a_raw.at[slot - 1]
            for i in range(width // LANE):
                cols = slice(LANE * i, LANE * (i + 1))
                a_t[slot, cols, :] = src[:, cols].T

    for i in range(model // LANE):
        cols = slice(LANE * i, LANE * (i + 1))
        tbuf[cols, :] = jnp.broadcast_to(1.0 / gain1[:, cols], (LANE, LANE)).T
    gk[...] = jnp.zeros_like(gk)

    @pl.when(last_seg)
    def _():
        e[...] = gout[...]
        load_w2.wait()
        upper(EVERY)

    def front(chunk, edge):
        for start, size in pieces(chunk):
            rows = slice(start, start + size)
            x = cur[rows, :].astype(F32)
            centred = x - jnp.mean(x, axis=-1, keepdims=True)
            rstd = lax.rsqrt(jnp.mean(centred * centred, axis=-1, keepdims=True) + EPS)
            hat = centred * rstd
            xhat[rows, :] = hat
            rstd1[rows, :] = jnp.broadcast_to(rstd, (size, LANE))
            normed[rows, :] = (hat * gain1[...]).astype(BF16)
        x = stacked(normed, chunk)
        mask = jnp.concatenate([mask_of(start, size) for start, size in chunk], axis=0)
        for n in range(width // 256):
            cols = slice(256 * n, 256 * (n + 1))
            q_cols = slice(width + 256 * n, width + 256 * (n + 1))
            p = dot(x, w1[:, cols])
            sig = jax.nn.sigmoid(dot(x, w1[:, q_cols]))
            gated = (p * sig * mask).astype(BF16)
            for rows, value in spread(p, chunk):
                p_buf[rows, cols] = value
            for rows, value in spread(sig, chunk):
                sig_buf[rows, cols] = value
            for rows, value in spread(gated.astype(F32), chunk):
                gpad[HALO + rows.start : HALO + rows.stop, cols] = value
            if edge:
                edge_g[0, :, cols] = gated[:HALO]
                edge_g[1, :, cols] = gated[HALO:]

    @pl.when(first_seg)
    def _():
        cur[...] = inp[...]
        load_w1.wait()
        front(EDGES, True)

    pl.semaphore_wait(barrier, len(greet))

    @pl.when(last_seg)
    def _():
        start_all(dout_copies(EVERY))
        load_w1.wait()
        for copy in out_copies(EDGES):
            copy.wait_recv()
        front(EDGES, True)

    copies = halo_copies(edge_g, halo_g, 0)
    start_all(copies)

    @pl.when(first_seg)
    def _():
        front(MIDDLE, False)

    @pl.when(last_seg)
    def _():
        for chunk in (MIDDLE[:1], MIDDLE[1:]):
            for copy in out_copies(chunk):
                copy.wait_recv()
            front(chunk, False)
        start_all(turned_copies(0))

    maskf = mask_of(0, frames)
    for copy in copies:
        copy.wait()
    has_left = (t > 0).astype(F32)
    has_right = (t < n_tm - 1).astype(F32)
    gpad[0:HALO, :] = halo_g[0].astype(F32) * has_left
    gpad[HALO + frames :, :] = halo_g[1].astype(F32) * has_right

    def conv_block(block, carry):
        cols, total = taps_over(gpad, block, False)
        conv[:, cols] = total
        return carry

    lax.fori_loop(0, width // LANE, conv_block, 0)

    def act_rows(chunk):
        for start, size in pieces(chunk):
            rows = slice(start, start + size)
            x = conv[rows, :]
            centred = x - jnp.mean(x, axis=-1, keepdims=True)
            rstd = lax.rsqrt(jnp.mean(centred * centred, axis=-1, keepdims=True) + EPS)
            hat = centred * rstd
            zn = hat * gain2[...]
            zhat[rows, :] = hat
            zn_buf[rows, :] = zn
            rstd2[rows, :] = jnp.broadcast_to(rstd, (size, LANE))
            act[rows, :] = (zn * jax.nn.sigmoid(zn)).astype(BF16)

    def out_rows(chunk):
        x = stacked(act, chunk)
        for n in range(model // 512):
            cols = slice(512 * n, 512 * (n + 1))
            for rows, value in spread(dot(x, w2[:, cols]), chunk):
                mask = mask_of(rows.start, rows.stop - rows.start)
                out_ref[rows, cols] = (cur[rows, cols].astype(F32) + mask * value).astype(BF16)

    @pl.when(first_seg)
    def _():
        load_w2.wait()
        for chunk in (EDGES, MIDDLE):
            act_rows(chunk)
            out_rows(chunk)
            start_all(out_copies(chunk))
        store_out.start()
        turn_normed((0,))
        turn_act((0,))
        for copy in out_copies(EVERY):
            copy.wait_send()
        for part in range(6):
            start_all(turned_copies(part))
        forward_turned(range(6))
        wait_turned(range(6))
        turn_normed((1, 2, 3))
        turn_act((1, 2, 3))

    @pl.when(last_seg)
    def _():
        start_all(turned_copies(1))
        act_rows(EVERY)

    def conv_grad(chunk):
        for start, size in pieces(chunk):
            rows = slice(start, start + size)
            zn = zn_buf[rows, :]
            hat = zhat[rows, :]
            sg = jax.nn.sigmoid(zn)
            d_zn = d_act[rows, :] * (sg + zn * sg * (1.0 - sg))
            gk[TAPS : TAPS + 1, :] += jnp.sum(d_zn * hat, axis=0, keepdims=True)
            d_hat = d_zn * gain2[...]
            m_one = jnp.mean(d_hat, axis=-1, keepdims=True)
            m_two = jnp.mean(d_hat * hat, axis=-1, keepdims=True)
            d_conv = rstd2[rows, 0:1] * (d_hat - m_one - hat * m_two)
            dpad[HALO + start : HALO + start + size, :] = d_conv

    def tap_grads(block, carry):
        cols = pl.ds(pl.multiple_of(block * LANE, LANE), LANE)
        whole = gpad[:, cols]
        d_conv = dpad[HALO : HALO + frames, cols]
        for r in range(8):
            moved = whole if r == 0 else pltpu.roll(whole, whole.shape[0] - r, 0)
            for k in range(TAPS):
                if (k + 1) % 8 == r:
                    at = k + 1 - r
                    gk[k : k + 1, cols] = jnp.sum(
                        moved[at : at + frames] * d_conv, axis=0, keepdims=True
                    )
        return carry

    halos = halo_copies(edge_d, halo_d, 2)

    def send_edges():
        edge_d[0] = dpad[HALO : 2 * HALO, :].astype(BF16)
        edge_d[1] = dpad[frames : HALO + frames, :].astype(BF16)
        start_all(halos)

    @pl.when(first_seg)
    def _():
        for chunk in (EDGES, MIDDLE[:1], MIDDLE[1:]):
            for copy in grad_copies(chunk):
                copy.wait_recv()
            upper(chunk)
            conv_grad(chunk)
            if chunk is EDGES:
                send_edges()
            start_all(dout_copies(chunk))

    @pl.when(last_seg)
    def _():
        conv_grad(EDGES)
        send_edges()
        conv_grad(MIDDLE)
        lax.fori_loop(0, width // LANE, tap_grads, 0)

    for copy in halos:
        copy.wait()

    @pl.when(last_seg)
    def _():
        start_all(turned_copies(2))

    dpad[0:HALO, :] = halo_d[0].astype(F32) * has_left
    dpad[HALO + frames :, :] = halo_d[1].astype(F32) * has_right

    def pre_blocks(first, last):
        for half in range(2):

            def pre_block(block, carry):
                cols, total = taps_over(dpad, half * 3 + block, True)
                d_gated = total * maskf
                sig = sig_buf[:, cols]
                d_p = d_gated * sig
                d_q = d_p * p_buf[:, cols] * (1.0 - sig)
                part = pl.ds(pl.multiple_of(block * LANE, LANE), LANE)
                dpre4[half, :, part] = d_p.astype(BF16)
                dpre4[2 + half, :, part] = d_q.astype(BF16)
                return carry

            lax.fori_loop(first, last, pre_block, 0)

    pre_blocks(0, 2)

    @pl.when(first_seg)
    def _():
        start_all(dpre_copies(0))

    pre_blocks(2, 3)

    @pl.when(first_seg)
    def _():
        start_all(dpre_copies(1))

    def grad_rows(chunk):
        d_pre = jnp.concatenate([stacked(dpre4.at[i], chunk) for i in range(4)], axis=1)
        for n in range(model // 512):
            cols = slice(512 * n, 512 * (n + 1))
            for rows, value in spread(dot_t(d_pre, w1[cols, :]), chunk):
                d_norm[rows, cols] = value
        for start, size in pieces(chunk):
            rows = slice(start, start + size)
            d_normed = d_norm[rows, :]
            hat = xhat[rows, :]
            d_hat = d_normed * gain1[...]
            m_one = jnp.mean(d_hat, axis=-1, keepdims=True)
            m_two = jnp.mean(d_hat * hat, axis=-1, keepdims=True)
            d_h = rstd1[rows, 0:1] * (d_hat - m_one - hat * m_two)
            grad_ref[rows, :] = (e[rows, :].astype(F32) + d_h).astype(BF16)

    @pl.when(last_seg)
    def _():
        for chunk in (EDGES, MIDDLE):
            grad_rows(chunk)
            start_all(grad_copies(chunk))
        for part in (4, 5, 3):
            start_all(turned_copies(part))
        start_all(dpre_copies(0) + dpre_copies(1))
        store_grad.start()
        out_rows(EVERY)
        store_out.start()
        turn_act((0,))
        turn_normed((0,))
        forward_turned((0, 1, 2, 4, 5))
        wait_turned((0, 1, 2, 4, 5))
        turn_act((1, 2, 3))
        for copy in grad_copies(EVERY):
            copy.wait_send()

    low, high = pl.ds(0, n_z // 2), pl.ds(n_z // 2, n_z // 2)
    up, down, far = (dy + 1) % n_y, (dy + n_y - 1) % n_y, (dy + 2) % n_y

    def y_far(buf, inner, base_sem):
        return [
            remote(buf.at[far, low], inner.at[0], sem_y, base_sem, "dp", up),
            remote(buf.at[far, high], inner.at[1], sem_y, base_sem + 1, "dp", down),
        ]

    def y_direct(buf, got, base_sem):
        return [
            remote(buf.at[up, high], got.at[0, high], sem_y, base_sem + 2, "dp", up),
            remote(buf.at[down, low], got.at[1, low], sem_y, base_sem + 3, "dp", down),
        ]

    def y_summed(buf, got, base_sem):
        return [
            remote(buf.at[up, low], got.at[0, low], sem_y, base_sem + 4, "dp", up),
            remote(buf.at[down, high], got.at[1, high], sem_y, base_sem + 5, "dp", down),
        ]

    def z_peer(d):
        return ((z + d + n_z) % n_z) * 4 + j

    def z_far(item):
        q_buf, in_three, in_four, _, base_sem = item[3:]
        parts = q_buf.shape[1] // 2
        copies = []
        for i, d in enumerate((1, -1)):
            over = pl.ds(parts * i, parts if i == 0 else q_buf.shape[1] - parts)
            three, four = (z + 3 * d + n_z) % n_z, (z + 4) % n_z
            to = z_peer(2 * d)
            at = base_sem + 2 * i
            copies.append(remote(q_buf.at[three], in_three.at[i], sem_z, at, "tm", to))
            into = in_four.at[i, pl.ds(0, over.size)]
            copies.append(remote(q_buf.at[four, over], into, sem_z, at + 1, "tm", to))
        return copies

    def z_near(item):
        q_buf, _, _, got, base_sem = item[3:]
        copies = []
        for i, d in enumerate((2, -2, 1, -1)):
            peer = (z + d + n_z) % n_z
            at = base_sem + 4 + i
            copies.append(remote(q_buf.at[peer], got.at[i], sem_z, at, "tm", z_peer(d)))
        return copies

    def z_relay(item):
        q_buf, in_three, in_four, _, _ = item[3:]
        parts = q_buf.shape[1] // 2
        for copy in z_far(item):
            copy.wait()
        copies = z_near(item)
        for i, d in enumerate((2, -2)):
            peer = (z + d + n_z) % n_z
            for m in range(parts if i == 0 else q_buf.shape[1] - parts):
                k = parts * i + m
                q_buf[peer, k] = (q_buf[peer, k].astype(F32) + in_four[i, m].astype(F32)).astype(BF16)
            copies[i].start()
        for i, d in enumerate((1, -1)):
            peer = (z + d + n_z) % n_z
            q_buf[peer] = (q_buf[peer].astype(F32) + in_three[i].astype(F32)).astype(BF16)
            copies[2 + i].start()

    def z_total(item):
        q_buf, _, _, got, _ = item[3:]
        for copy in z_near(item):
            copy.wait()
        total = q_buf[z].astype(F32)
        for i in range(4):
            total = total + got[i].astype(F32)
        return total

    def last_copies(buf, got, base_sem):
        return [
            remote(buf.at[(dy + d) % n_y], got.at[d - 1], sem_y, base_sem + d, "dp", (dy + d) % n_y)
            for d in range(1, n_y)
        ]

    def last_total(buf, got, base_sem):
        for copy in last_copies(buf, got, base_sem):
            copy.wait()
        total = buf[dy].astype(F32)
        for d in range(n_y - 1):
            total = total + got[d].astype(F32)
        return total

    rows_one = model // n_y
    rows_two = width // n_y

    for copy in dout_copies(EVERY):
        copy.wait()
    rhs_two = jnp.concatenate([dout4[j]] + [dout_r[d] for d in range(3)], axis=0)
    item_a = tuple(item_a) + (0,)
    item_b = tuple(item_b) + (8,)
    item_c = (None,) * 3 + tuple(item_c) + (16,)
    qy_c = (qy, y_got, 11)

    def product(turned, peer, rows, rhs):
        start = pl.multiple_of(peer * rows, rows)
        lhs = jnp.concatenate([turned[i, pl.ds(start, rows), :] for i in range(4)], axis=1)
        return dot(lhs, rhs)

    def part_two(peer):
        part = product(a_t, peer, rows_two, rhs_two)
        for i in range(n_z):
            mine = part[24 * i : 24 * (i + 1)]
            blocks = [mine[:, LANE * m : LANE * (m + 1)] for m in range(3)]
            at = pl.multiple_of(peer * rows_two + 24 * i, 8)
            extra = ebuf[pl.ds(at, 24), :]
            fill = extra[:8] + pltpu.roll(extra[8:16], 32, 1) + pltpu.roll(extra[16:], 64, 1)
            whole = jnp.concatenate(blocks + [fill], axis=0).astype(BF16)
            for m in range(5):
                item_b[0][peer, i, m] = whole[16 * m : 16 * (m + 1)]

    def part_one(peer):
        part = product(n_t, peer, rows_one, rhs_one)
        for i in range(n_z):
            for m in range(2):
                mine = part[48 * i : 48 * (i + 1), LANE * m : LANE * (m + 1)]
                item_a[0][peer, i, m] = mine.astype(BF16)

    def part_last(d):
        peer = (z + d + n_z) % n_z
        starts = [pl.multiple_of(rows_one * yy + 48 * peer, 16) for yy in range(n_y)]
        lhs = jnp.concatenate(
            [
                jnp.concatenate([n_t[i, pl.ds(start, 48), :] for i in range(4)], axis=1)
                for start in starts
            ],
            axis=0,
        )
        part = dot(lhs, rhs_last)
        for yy in range(n_y):
            item_c[3][peer, yy] = part[48 * yy : 48 * (yy + 1)].astype(BF16)

    def y_begin(item, fill, base_sem):
        buf, inner, got = item[:3]
        fill(far)
        start_all(y_far(buf, inner, base_sem))
        fill(up)
        fill(down)
        start_all(y_direct(buf, got, base_sem))
        fill(dy)

    def y_relay(item, base_sem):
        buf, inner, got = item[:3]
        for copy in y_far(buf, inner, base_sem):
            copy.wait()
        for i in range(n_z // 2):
            k = n_z // 2 + i
            buf[up, i] = (buf[up, i].astype(F32) + inner[0, i].astype(F32)).astype(BF16)
            buf[down, k] = (buf[down, k].astype(F32) + inner[1, i].astype(F32)).astype(BF16)
        start_all(y_summed(buf, got, base_sem))

    def y_finish(item, base_sem):
        buf, _, got, q_buf = item[:4]
        for copy in y_direct(buf, got, base_sem) + y_summed(buf, got, base_sem):
            copy.wait()

        def total(d):
            at = (z + d) % n_z
            mine = buf[dy, at].astype(F32) + got[0, at].astype(F32) + got[1, at].astype(F32)
            q_buf[at] = mine.astype(BF16)

        for d in (3, 5, 4):
            total(d)
        start_all(z_far(item))
        for d in (2, 6, 1, 7, 0):
            total(d)

    @pl.when(first_seg)
    def _():
        lax.fori_loop(0, width // LANE, tap_grads, 0)

    for i in range(width // LANE):
        cols = slice(LANE * i, LANE * (i + 1))
        ebuf[cols, :] = gk[:, cols].T
    y_begin(item_b, part_two, 6)

    @pl.when(last_seg)
    def _():
        forward_turned((3,))
        wait_turned((3,))
        turn_normed((1, 2, 3))

    for copy in dpre_copies(0):
        copy.wait()
    rhs_one = jnp.concatenate([dpre4[j, :, :256]] + [dpre_r[d, :, :256] for d in range(3)], axis=0)
    part_one(far)
    start_all(y_far(item_a[0], item_a[1], 0))
    for copy in dpre_copies(1):
        copy.wait()
    rhs_last = jnp.concatenate([dpre4[j, :, 256:]] + [dpre_r[d, :, 256:] for d in range(3)], axis=0)
    for d in (3, -3, 4):
        part_last(d)
    start_all(z_far(item_c))
    part_one(up)
    part_one(down)
    y_relay(item_b, 6)
    start_all(y_direct(item_a[0], item_a[2], 0))
    part_one(dy)
    for d in (1, -1, 2, -2, 0):
        part_last(d)

    @pl.when(first_seg)
    def _():
        grad_rows(EVERY)
        store_grad.start()

    y_relay(item_a, 0)
    z_relay(item_c)
    y_finish(item_b, 6)
    y_finish(item_a, 0)
    qy[...] = z_total(item_c).astype(BF16)
    start_all(last_copies(*qy_c))
    z_relay(item_b)
    z_relay(item_a)

    fs[...] = jnp.zeros_like(fs)
    total = z_total(item_b)
    total = jnp.concatenate([total[m] for m in range(5)], axis=0)
    for i in range(4):
        for m in range(3):
            at = 24 * m + 6 * i
            fs[i, 16:22, LANE * m : LANE * (m + 1)] = total[at : at + 6]
    fill = total[72:]
    extra = jnp.concatenate([fill, pltpu.roll(fill, 96, 1), pltpu.roll(fill, 64, 1)], axis=0)
    for i in range(4):
        fs[i, 24:30, 0:LANE] = extra[6 * i : 6 * (i + 1)]
    total = z_total(item_a)
    for i in range(4):
        for m in range(2):
            fs[i, 0:12, LANE * m : LANE * (m + 1)] = total[m, 12 * i : 12 * (i + 1)]
    final = last_total(*qy_c)
    mine = jnp.concatenate([total[0], total[1], final], axis=1)
    place = pl.ds(pl.multiple_of((dy * n_z + z) * 48, 16), 48)
    weights = w1[place, pl.ds(pl.multiple_of(j * 384, LANE), 384)].astype(F32)
    gains = jnp.sum(mine * weights, axis=-1, keepdims=True) * tbuf[place, :]
    for i in range(4):
        fs[i, 0:12, 256:] = final[12 * i : 12 * (i + 1)]
        for m in range(2):
            at = 12 * i + 6 * m
            fs[i, 24:30, LANE * (m + 1) : LANE * (m + 2)] = gains[at : at + 6]
    f_out[...] = fs[...].astype(BF16)
    copies = [remote(f_out.at[peer_j(d)], f_in.at[j], sem_f, d, "tm", group[d]) for d in range(3)]
    start_all(copies)
    f_in[j] = f_out[j]
    for copy in copies:
        copy.wait()
    fs[...] = f_in[...].astype(F32)
    small = jnp.zeros((8, 3 * LANE), F32)
    for i in range(4):
        cols = slice(384 * i, 384 * (i + 1))
        for row in range(12):
            o_one[row, :, cols] = fs[i, row : row + 1, :]
        for row in range(6):
            o_two[row, :, cols] = fs[i, 16 + row : 17 + row, :]
        small = small + fs[i, 24:32, :]
    for i in range(6):
        o_kern[i] = small[i : i + 1, :TAPS]
    fill = jnp.zeros((LANE - 8, LANE), F32)
    turned = [
        jnp.concatenate([small[:, LANE * m : LANE * (m + 1)], fill], axis=0).T for m in range(3)
    ]
    o_gain2[...] = turned[0][TAPS : TAPS + 1, :6]
    for m in range(2):
        o_gain1[:, 6 * m : 6 * (m + 1)] = turned[m + 1][0:1, :6]
    store_out.wait()
    store_grad.wait()


def hand_over(*refs):
    n = len(refs) // 2
    for i in range(n):
        refs[n + i][...] = refs[i][...]


def per_device(inputs, lengths, w_first, kernel_w, gain_first, gain_second, w_second, grad_output):
    n_y = lax.axis_size("dp")
    n_tm = lax.axis_size("tm")
    n_z = n_tm // 4
    frames, model = inputs.shape[1:]
    width = w_second.shape[1]
    groups = n_y * n_tm
    vmem = pl.BlockSpec(memory_space=pltpu.VMEM)

    def buf(shape, dtype):
        return pltpu.VMEM(shape, dtype)

    def second(parts, rows):
        return (
            buf((n_z, parts, rows, LANE), BF16),
            buf((2, parts, rows, LANE), BF16),
            buf((2, parts - parts // 2, rows, LANE), BF16),
            buf((4, parts, rows, LANE), BF16),
        )

    def reduced(parts, rows):
        return (
            buf((n_y, n_z, parts, rows, LANE), BF16),
            buf((2, n_z // 2, parts, rows, LANE), BF16),
            buf((2, n_z, parts, rows, LANE), BF16),
        ) + second(parts, rows)

    wide = (frames, model)
    thin = (frames, width)
    padded = (frames + 2 * HALO, width)
    third = (4, frames, 384)
    scratch = [
        buf((model, 2 * width), BF16),
        buf((width, model), BF16),
        buf(wide, BF16),
        buf(wide, BF16),
        buf(wide, BF16),
        buf(wide, BF16),
        buf(wide, F32),
        buf((frames, LANE), F32),
        buf(wide, BF16),
        buf(thin, F32),
        buf(thin, F32),
        buf(padded, F32),
        buf(padded, F32),
        buf(thin, F32),
        buf(thin, F32),
        buf((frames, LANE), F32),
        buf(thin, F32),
        buf(thin, BF16),
        buf(thin, F32),
        buf(wide, F32),
        buf((2, HALO, width), BF16),
        buf((2, HALO, width), BF16),
        buf((2, HALO, width), BF16),
        buf((2, HALO, width), BF16),
        buf(third, BF16),
        buf(third, BF16),
        buf((3, frames, 384), BF16),
        buf((3, frames, 384), BF16),
        buf((3,) + wide, BF16),
        buf((3,) + thin, BF16),
        buf((4, model, LANE), BF16),
        buf((4, width, LANE), BF16),
        buf((LANE, width), F32),
        buf((width, LANE), F32),
        buf((model, LANE), F32),
        reduced(2, 48),
        reduced(5, 16),
        second(4, 48),
        buf((n_y, 48, LANE), BF16),
        buf((n_y - 1, 48, LANE), BF16),
        buf((4, 32, 384), F32),
        buf((4, 32, 384), BF16),
        buf((4, 32, 384), BF16),
        pltpu.SemaphoreType.DMA((4,)),
        pltpu.SemaphoreType.DMA((2, 4)),
        pltpu.SemaphoreType.DMA((2, 4)),
        pltpu.SemaphoreType.DMA((2, 4)),
        pltpu.SemaphoreType.DMA((2, 36)),
        pltpu.SemaphoreType.DMA((2, 15)),
        pltpu.SemaphoreType.DMA((2, 24)),
        pltpu.SemaphoreType.DMA((2, 3)),
    ]
    hbm = pl.BlockSpec(memory_space=pl.ANY)
    shapes = (
        jax.ShapeDtypeStruct(wide, BF16),
        jax.ShapeDtypeStruct(wide, BF16),
        jax.ShapeDtypeStruct((model // groups, 1, model), F32),
        jax.ShapeDtypeStruct((width // groups, 1, model), F32),
        jax.ShapeDtypeStruct((width // groups, 1, TAPS), F32),
        jax.ShapeDtypeStruct((1, model // groups), F32),
        jax.ShapeDtypeStruct((1, width // groups), F32),
    )
    results = pl.pallas_call(
        functools.partial(kernel, n_y, n_z, n_tm),
        out_shape=shapes,
        in_specs=[pl.BlockSpec(memory_space=pltpu.SMEM), vmem, vmem, hbm, hbm, vmem, vmem, vmem],
        out_specs=(hbm, hbm) + (vmem,) * 5,
        scratch_shapes=scratch,
        compiler_params=pltpu.CompilerParams(
            collective_id=0, has_side_effects=True, vmem_limit_bytes=60 * 1024 * 1024
        ),
        cost_estimate=pl.CostEstimate(
            flops=2 * 3 * frames * model * 3 * width, bytes_accessed=12_000_000, transcendentals=0
        ),
    )(
        lengths,
        inputs[0],
        grad_output[0],
        w_first[0],
        w_second[0],
        kernel_w.transpose(1, 0, 2),
        gain_first,
        gain_second,
    )
    out, grad, one, two, taps, g_one, g_two = pl.pallas_call(
        hand_over,
        out_shape=shapes,
        in_specs=[vmem] * 7,
        out_specs=(vmem,) * 7,
        compiler_params=pltpu.CompilerParams(vmem_limit_bytes=60 * 1024 * 1024),
    )(*results)
    return (
        out[None, None],
        grad[None, None],
        one.transpose(1, 0, 2),
        taps.transpose(1, 2, 0),
        g_one,
        g_two,
        two.transpose(1, 0, 2),
    )


def solution(mesh):
    in_specs = (
        P("dp", "tm", None),
        P("dp"),
        P("segment", None, None),
        P("segment", None, None),
        P("segment", None),
        P("segment", None),
        P("segment", None, None),
        P("dp", "tm", None),
    )
    out_specs = (
        P("segment", "dp", "tm", None),
        P("segment", "dp", "tm", None),
        P("segment", ("dp", "tm"), None),
        P("segment", None, ("dp", "tm")),
        P("segment", ("dp", "tm")),
        P("segment", ("dp", "tm")),
        P("segment", ("dp", "tm"), None),
    )
    return jax.shard_map(
        per_device, mesh=mesh, in_specs=in_specs, out_specs=out_specs, check_vma=False
    )
```

```python
import functools

import jax
import jax.numpy as jnp
from jax import lax
from jax.experimental import pallas as pl
from jax.experimental.pallas import tpu as pltpu
from jax.sharding import PartitionSpec as P

EPS = 1e-05
F32 = jnp.float32
BF16 = jnp.bfloat16
MESH = pl.DeviceIdType.MESH
NT = (((1,), (1,)), ((), ()))
HALO = 16
TAPS = 31
LANE = 128
ROWS = 32
EDGES = ((0, 16), (112, 16))
MIDDLE = ((16, 48), (64, 48))
EVERY = EDGES + MIDDLE


def chunk_rows(chunk):
    return [(EVERY.index(part), pl.ds(*part)) for part in chunk]


def dot(a, b):
    return jnp.dot(a, b, preferred_element_type=F32)


def dot_t(a, b):
    return lax.dot_general(a, b, NT, preferred_element_type=F32)


def kernel(
    n_y,
    n_z,
    n_tm,
    len_ref,
    inp,
    gout,
    w1_hbm,
    w2_hbm,
    kern,
    gain1,
    gain2,
    out_hbm,
    grad_hbm,
    o_one,
    o_two,
    o_kern,
    o_gain1,
    o_gain2,
    w1,
    w2,
    out_ref,
    grad_ref,
    cur,
    e,
    xhat,
    rstd1,
    normed,
    p_buf,
    sig_buf,
    gpad,
    dpad,
    conv,
    zhat,
    rstd2,
    zn_buf,
    act,
    d_act,
    d_norm,
    edge_g,
    edge_d,
    halo_g,
    halo_d,
    dout4,
    dpre4,
    dout_r,
    dpre_r,
    n_raw,
    a_raw,
    n_t,
    a_t,
    gk,
    ebuf,
    tbuf,
    item_a,
    item_b,
    item_c,
    qy,
    y_got,
    fs,
    f_out,
    f_in,
    sem_w,
    sem_h,
    sem_out,
    sem_grad,
    sem_x,
    sem_y,
    sem_z,
    sem_f,
):
    frames, model = inp.shape
    width = w2.shape[0]
    dy = lax.axis_index("dp")
    seg = lax.axis_index("segment")
    t = lax.axis_index("tm")
    c = t % 2
    xl = (t // 2) % 2
    z = t // 4
    j = t % 4
    base = z * 4
    group = [base + xl * 2 + (1 - c), base + (1 - xl) * 2 + c, base + (1 - xl) * 2 + (1 - c)]
    right = (t + 1) % n_tm
    left = (t + n_tm - 1) % n_tm
    first_seg = seg == 0
    last_seg = seg == 1

    def remote(src, dst, sems, index, axis, peer):
        return pltpu.make_async_remote_copy(
            src_ref=src,
            dst_ref=dst,
            send_sem=sems.at[0, index],
            recv_sem=sems.at[1, index],
            device_id={axis: peer},
            device_id_type=MESH,
        )

    load_w1 = pltpu.make_async_copy(w1_hbm, w1, sem_w.at[0])
    load_w2 = pltpu.make_async_copy(w2_hbm, w2, sem_w.at[1])
    store_out = pltpu.make_async_copy(out_ref, out_hbm, sem_w.at[2])
    store_grad = pltpu.make_async_copy(grad_ref, grad_hbm, sem_w.at[3])
    barrier = pltpu.get_barrier_semaphore()
    greet = [("tm", left), ("tm", right), ("segment", 1 - seg)]
    greet += [("tm", g) for g in group]
    greet += [("dp", (dy + d) % n_y) for d in range(1, n_y)]
    greet += [("tm", ((z + d) % n_z) * 4 + j) for d in (1, 2, n_z - 1, n_z - 2)]
    for axis, peer in greet:
        pl.semaphore_signal(barrier, inc=1, device_id={axis: peer}, device_id_type=MESH)

    @pl.when(first_seg)
    def _():
        load_w1.start()
        load_w2.start()

    @pl.when(last_seg)
    def _():
        load_w2.start()
        load_w1.start()

    length = len_ref[0]

    def mask_of(start, rows):
        ids = t * frames + start + lax.broadcasted_iota(jnp.int32, (rows, 1), 0)
        return (ids < length).astype(F32)

    def out_copies(chunk):
        return [
            remote(out_ref.at[rows], cur.at[rows], sem_out, i, "segment", 1 - seg)
            for i, rows in chunk_rows(chunk)
        ]

    def grad_copies(chunk):
        return [
            remote(grad_ref.at[rows], e.at[rows], sem_grad, i, "segment", 1 - seg)
            for i, rows in chunk_rows(chunk)
        ]

    def halo_copies(edge, halo, offset):
        return [
            remote(edge.at[0], halo.at[1], sem_h, offset, "tm", left),
            remote(edge.at[1], halo.at[0], sem_h, offset + 1, "tm", right),
        ]

    def peer_j(d):
        return group[d] % 4

    def dout_copies(chunk):
        return [
            remote(
                dout4.at[peer_j(d), rows], dout_r.at[d, rows], sem_x, 3 * i + d, "tm", group[d]
            )
            for i, rows in chunk_rows(chunk)
            for d in range(3)
        ]

    def dpre_copies(last):
        cols = pl.ds(256, LANE) if last else pl.ds(0, 256)
        return [
            remote(
                dpre4.at[peer_j(d), :, cols],
                dpre_r.at[d, :, cols],
                sem_x,
                12 + 3 * last + d,
                "tm",
                group[d],
            )
            for d in range(3)
        ]

    def turned_copies(part, forward=False):
        own, got = (act, a_raw) if part > 3 else (normed, n_raw)
        rows = pl.ds(64 * (part - 4), 64) if part > 3 else pl.ds(32 * part, 32)

        def one(src, dst, d):
            return remote(
                src.at[rows], got.at[dst, rows], sem_x, 18 + 3 * part + d, "tm", group[d % 2]
            )

        return [one(got.at[1], 2, 2)] if forward else [one(own, 0, 0), one(own, 1, 1)]

    def forward_turned(parts):
        for part in parts:
            turned_copies(part)[1].wait_recv()
            turned_copies(part, True)[0].start()

    def wait_turned(parts):
        for part in parts:
            copies = turned_copies(part)
            copies[0].wait()
            copies[1].wait_send()
            turned_copies(part, True)[0].wait()

    def start_all(copies):
        for copy in copies:
            copy.start()

    def stacked(ref, chunk):
        return jnp.concatenate([ref[start : start + size] for start, size in chunk], axis=0)

    def spread(value, chunk):
        at = 0
        for start, size in chunk:
            yield slice(start, start + size), value[at : at + size]
            at += size

    def pieces(chunk):
        return [(at, min(ROWS, start + size - at)) for start, size in chunk for at in range(start, start + size, ROWS)]

    def upper(chunk):
        for start, size in pieces(chunk):
            rows = slice(start, start + size)
            d_out = (e[rows, :].astype(F32) * mask_of(start, size)).astype(BF16)
            for i in range(4):
                dout4[i, rows, :] = d_out[:, 384 * i : 384 * (i + 1)]
        d_out = jnp.concatenate([stacked(dout4.at[i], chunk) for i in range(4)], axis=1)
        for n in range(width // 256):
            cols = slice(256 * n, 256 * (n + 1))
            for rows, value in spread(dot_t(d_out, w2[cols, :]), chunk):
                d_act[rows, cols] = value

    def taps_over(src, block, flip):
        cols = pl.ds(pl.multiple_of(block * LANE, LANE), LANE)
        whole = src[:, cols]
        total = jnp.zeros((frames, LANE), F32)
        for r in range(8):
            moved = whole if r == 0 else pltpu.roll(whole, whole.shape[0] - r, 0)
            for k in range(TAPS):
                if (k + 1) % 8 == r:
                    at = k + 1 - r
                    tap = TAPS - 1 - k if flip else k
                    total = total + kern[tap, :, cols] * moved[at : at + frames]
        return cols, total

    def turn_normed(slots):
        for slot in slots:
            src = normed if slot == 0 else n_raw.at[slot - 1]
            for i in range(model // LANE):
                cols = slice(LANE * i, LANE * (i + 1))
                n_t[slot, cols, :] = src[:, cols].T

    def turn_act(slots):
        for slot in slots:
            src = act if slot == 0 else a_raw.at[slot - 1]
            for i in range(width // LANE):
                cols = slice(LANE * i, LANE * (i + 1))
                a_t[slot, cols, :] = src[:, cols].T

    for i in range(model // LANE):
        cols = slice(LANE * i, LANE * (i + 1))
        tbuf[cols, :] = jnp.broadcast_to(1.0 / gain1[:, cols], (LANE, LANE)).T
    gk[...] = jnp.zeros_like(gk)

    @pl.when(last_seg)
    def _():
        e[...] = gout[...]
        load_w2.wait()
        upper(EVERY)

    def front(chunk, edge):
        for start, size in pieces(chunk):
            rows = slice(start, start + size)
            x = cur[rows, :].astype(F32)
            centred = x - jnp.mean(x, axis=-1, keepdims=True)
            rstd = lax.rsqrt(jnp.mean(centred * centred, axis=-1, keepdims=True) + EPS)
            hat = centred * rstd
            xhat[rows, :] = hat
            rstd1[rows, :] = jnp.broadcast_to(rstd, (size, LANE))
            normed[rows, :] = (hat * gain1[...]).astype(BF16)
        x = stacked(normed, chunk)
        mask = jnp.concatenate([mask_of(start, size) for start, size in chunk], axis=0)
        for n in range(width // 256):
            cols = slice(256 * n, 256 * (n + 1))
            q_cols = slice(width + 256 * n, width + 256 * (n + 1))
            p = dot(x, w1[:, cols])
            sig = jax.nn.sigmoid(dot(x, w1[:, q_cols]))
            gated = (p * sig * mask).astype(BF16)
            for rows, value in spread(p, chunk):
                p_buf[rows, cols] = value
            for rows, value in spread(sig, chunk):
                sig_buf[rows, cols] = value
            for rows, value in spread(gated.astype(F32), chunk):
                gpad[HALO + rows.start : HALO + rows.stop, cols] = value
            if edge:
                edge_g[0, :, cols] = gated[:HALO]
                edge_g[1, :, cols] = gated[HALO:]

    @pl.when(first_seg)
    def _():
        cur[...] = inp[...]
        load_w1.wait()
        front(EDGES, True)

    pl.semaphore_wait(barrier, len(greet))

    @pl.when(last_seg)
    def _():
        start_all(dout_copies(EVERY))
        load_w1.wait()
        for copy in out_copies(EDGES):
            copy.wait_recv()
        front(EDGES, True)

    copies = halo_copies(edge_g, halo_g, 0)
    start_all(copies)

    @pl.when(first_seg)
    def _():
        front(MIDDLE, False)

    @pl.when(last_seg)
    def _():
        for chunk in (MIDDLE[:1], MIDDLE[1:]):
            for copy in out_copies(chunk):
                copy.wait_recv()
            front(chunk, False)
        start_all(turned_copies(0))

    maskf = mask_of(0, frames)
    for copy in copies:
        copy.wait()
    has_left = (t > 0).astype(F32)
    has_right = (t < n_tm - 1).astype(F32)
    gpad[0:HALO, :] = halo_g[0].astype(F32) * has_left
    gpad[HALO + frames :, :] = halo_g[1].astype(F32) * has_right

    def conv_block(block, carry):
        cols, total = taps_over(gpad, block, False)
        conv[:, cols] = total
        return carry

    lax.fori_loop(0, width // LANE, conv_block, 0)

    def act_rows(chunk):
        for start, size in pieces(chunk):
            rows = slice(start, start + size)
            x = conv[rows, :]
            centred = x - jnp.mean(x, axis=-1, keepdims=True)
            rstd = lax.rsqrt(jnp.mean(centred * centred, axis=-1, keepdims=True) + EPS)
            hat = centred * rstd
            zn = hat * gain2[...]
            zhat[rows, :] = hat
            zn_buf[rows, :] = zn
            rstd2[rows, :] = jnp.broadcast_to(rstd, (size, LANE))
            act[rows, :] = (zn * jax.nn.sigmoid(zn)).astype(BF16)

    def out_rows(chunk):
        x = stacked(act, chunk)
        for n in range(model // 512):
            cols = slice(512 * n, 512 * (n + 1))
            for rows, value in spread(dot(x, w2[:, cols]), chunk):
                mask = mask_of(rows.start, rows.stop - rows.start)
                out_ref[rows, cols] = (cur[rows, cols].astype(F32) + mask * value).astype(BF16)

    @pl.when(first_seg)
    def _():
        load_w2.wait()
        for chunk in (EDGES, MIDDLE):
            act_rows(chunk)
            out_rows(chunk)
            start_all(out_copies(chunk))
        store_out.start()
        turn_normed((0,))
        turn_act((0,))
        for copy in out_copies(EVERY):
            copy.wait_send()
        for part in range(6):
            start_all(turned_copies(part))
        forward_turned(range(6))
        wait_turned(range(6))
        turn_normed((1, 2, 3))
        turn_act((1, 2, 3))

    @pl.when(last_seg)
    def _():
        start_all(turned_copies(1))
        act_rows(EVERY)

    def conv_grad(chunk):
        for start, size in pieces(chunk):
            rows = slice(start, start + size)
            zn = zn_buf[rows, :]
            hat = zhat[rows, :]
            sg = jax.nn.sigmoid(zn)
            d_zn = d_act[rows, :] * (sg + zn * sg * (1.0 - sg))
            gk[TAPS : TAPS + 1, :] += jnp.sum(d_zn * hat, axis=0, keepdims=True)
            d_hat = d_zn * gain2[...]
            m_one = jnp.mean(d_hat, axis=-1, keepdims=True)
            m_two = jnp.mean(d_hat * hat, axis=-1, keepdims=True)
            d_conv = rstd2[rows, 0:1] * (d_hat - m_one - hat * m_two)
            dpad[HALO + start : HALO + start + size, :] = d_conv

    def tap_grads(block, carry):
        cols = pl.ds(pl.multiple_of(block * LANE, LANE), LANE)
        whole = gpad[:, cols]
        d_conv = dpad[HALO : HALO + frames, cols]
        for r in range(8):
            moved = whole if r == 0 else pltpu.roll(whole, whole.shape[0] - r, 0)
            for k in range(TAPS):
                if (k + 1) % 8 == r:
                    at = k + 1 - r
                    gk[k : k + 1, cols] = jnp.sum(
                        moved[at : at + frames] * d_conv, axis=0, keepdims=True
                    )
        return carry

    halos = halo_copies(edge_d, halo_d, 2)

    def send_edges():
        edge_d[0] = dpad[HALO : 2 * HALO, :].astype(BF16)
        edge_d[1] = dpad[frames : HALO + frames, :].astype(BF16)
        start_all(halos)

    @pl.when(first_seg)
    def _():
        for chunk in (EDGES, MIDDLE[:1], MIDDLE[1:]):
            for copy in grad_copies(chunk):
                copy.wait_recv()
            upper(chunk)
            conv_grad(chunk)
            if chunk is EDGES:
                send_edges()
            start_all(dout_copies(chunk))

    @pl.when(last_seg)
    def _():
        conv_grad(EDGES)
        send_edges()
        conv_grad(MIDDLE)
        lax.fori_loop(0, width // LANE, tap_grads, 0)

    for copy in halos:
        copy.wait()

    @pl.when(last_seg)
    def _():
        start_all(turned_copies(2))

    dpad[0:HALO, :] = halo_d[0].astype(F32) * has_left
    dpad[HALO + frames :, :] = halo_d[1].astype(F32) * has_right

    def pre_blocks(first, last):
        for half in range(2):

            def pre_block(block, carry):
                cols, total = taps_over(dpad, half * 3 + block, True)
                d_gated = total * maskf
                sig = sig_buf[:, cols]
                d_p = d_gated * sig
                d_q = d_p * p_buf[:, cols] * (1.0 - sig)
                part = pl.ds(pl.multiple_of(block * LANE, LANE), LANE)
                dpre4[half, :, part] = d_p.astype(BF16)
                dpre4[2 + half, :, part] = d_q.astype(BF16)
                return carry

            lax.fori_loop(first, last, pre_block, 0)

    pre_blocks(0, 2)

    @pl.when(first_seg)
    def _():
        start_all(dpre_copies(0))

    pre_blocks(2, 3)

    @pl.when(first_seg)
    def _():
        start_all(dpre_copies(1))

    def grad_rows(chunk):
        d_pre = jnp.concatenate([stacked(dpre4.at[i], chunk) for i in range(4)], axis=1)
        for n in range(model // 512):
            cols = slice(512 * n, 512 * (n + 1))
            for rows, value in spread(dot_t(d_pre, w1[cols, :]), chunk):
                d_norm[rows, cols] = value
        for start, size in pieces(chunk):
            rows = slice(start, start + size)
            d_normed = d_norm[rows, :]
            hat = xhat[rows, :]
            d_hat = d_normed * gain1[...]
            m_one = jnp.mean(d_hat, axis=-1, keepdims=True)
            m_two = jnp.mean(d_hat * hat, axis=-1, keepdims=True)
            d_h = rstd1[rows, 0:1] * (d_hat - m_one - hat * m_two)
            grad_ref[rows, :] = (e[rows, :].astype(F32) + d_h).astype(BF16)

    @pl.when(last_seg)
    def _():
        for chunk in (EDGES, MIDDLE):
            grad_rows(chunk)
            start_all(grad_copies(chunk))
        for part in (4, 5, 3):
            start_all(turned_copies(part))
        start_all(dpre_copies(0) + dpre_copies(1))
        store_grad.start()
        out_rows(EVERY)
        store_out.start()
        turn_act((0,))
        turn_normed((0,))
        forward_turned((0, 1, 2, 4, 5))
        wait_turned((0, 1, 2, 4, 5))
        turn_act((1, 2, 3))
        for copy in grad_copies(EVERY):
            copy.wait_send()

    low, high = pl.ds(0, n_z // 2), pl.ds(n_z // 2, n_z // 2)
    up, down, far = (dy + 1) % n_y, (dy + n_y - 1) % n_y, (dy + 2) % n_y

    def y_far(buf, inner, base_sem):
        return [
            remote(buf.at[far, low], inner.at[0], sem_y, base_sem, "dp", up),
            remote(buf.at[far, high], inner.at[1], sem_y, base_sem + 1, "dp", down),
        ]

    def y_direct(buf, got, base_sem):
        return [
            remote(buf.at[up, high], got.at[0, high], sem_y, base_sem + 2, "dp", up),
            remote(buf.at[down, low], got.at[1, low], sem_y, base_sem + 3, "dp", down),
        ]

    def y_summed(buf, got, base_sem):
        return [
            remote(buf.at[up, low], got.at[0, low], sem_y, base_sem + 4, "dp", up),
            remote(buf.at[down, high], got.at[1, high], sem_y, base_sem + 5, "dp", down),
        ]

    def z_peer(d):
        return ((z + d + n_z) % n_z) * 4 + j

    def z_far(item):
        q_buf, in_three, in_four, _, base_sem = item[3:]
        parts = q_buf.shape[1] // 2
        copies = []
        for i, d in enumerate((1, -1)):
            over = pl.ds(parts * i, parts if i == 0 else q_buf.shape[1] - parts)
            three, four = (z + 3 * d + n_z) % n_z, (z + 4) % n_z
            to = z_peer(2 * d)
            at = base_sem + 2 * i
            copies.append(remote(q_buf.at[three], in_three.at[i], sem_z, at, "tm", to))
            into = in_four.at[i, pl.ds(0, over.size)]
            copies.append(remote(q_buf.at[four, over], into, sem_z, at + 1, "tm", to))
        return copies

    def z_near(item):
        q_buf, _, _, got, base_sem = item[3:]
        copies = []
        for i, d in enumerate((2, -2, 1, -1)):
            peer = (z + d + n_z) % n_z
            at = base_sem + 4 + i
            copies.append(remote(q_buf.at[peer], got.at[i], sem_z, at, "tm", z_peer(d)))
        return copies

    def z_relay(item):
        q_buf, in_three, in_four, _, _ = item[3:]
        parts = q_buf.shape[1] // 2
        for copy in z_far(item):
            copy.wait()
        copies = z_near(item)
        for i, d in enumerate((2, -2)):
            peer = (z + d + n_z) % n_z
            for m in range(parts if i == 0 else q_buf.shape[1] - parts):
                k = parts * i + m
                q_buf[peer, k] = (q_buf[peer, k].astype(F32) + in_four[i, m].astype(F32)).astype(BF16)
            copies[i].start()
        for i, d in enumerate((1, -1)):
            peer = (z + d + n_z) % n_z
            q_buf[peer] = (q_buf[peer].astype(F32) + in_three[i].astype(F32)).astype(BF16)
            copies[2 + i].start()

    def z_total(item):
        q_buf, _, _, got, _ = item[3:]
        for copy in z_near(item):
            copy.wait()
        total = q_buf[z].astype(F32)
        for i in range(4):
            total = total + got[i].astype(F32)
        return total

    def last_copies(buf, got, base_sem):
        return [
            remote(buf.at[(dy + d) % n_y], got.at[d - 1], sem_y, base_sem + d, "dp", (dy + d) % n_y)
            for d in range(1, n_y)
        ]

    def last_total(buf, got, base_sem):
        for copy in last_copies(buf, got, base_sem):
            copy.wait()
        total = buf[dy].astype(F32)
        for d in range(n_y - 1):
            total = total + got[d].astype(F32)
        return total

    rows_one = model // n_y
    rows_two = width // n_y

    for copy in dout_copies(EVERY):
        copy.wait()
    rhs_two = jnp.concatenate([dout4[j]] + [dout_r[d] for d in range(3)], axis=0)
    item_a = tuple(item_a) + (0,)
    item_b = tuple(item_b) + (8,)
    item_c = (None,) * 3 + tuple(item_c) + (16,)
    qy_c = (qy, y_got, 11)

    def product(turned, peer, rows, rhs):
        start = pl.multiple_of(peer * rows, rows)
        lhs = jnp.concatenate([turned[i, pl.ds(start, rows), :] for i in range(4)], axis=1)
        return dot(lhs, rhs)

    def part_two(peer):
        part = product(a_t, peer, rows_two, rhs_two)
        for i in range(n_z):
            mine = part[24 * i : 24 * (i + 1)]
            blocks = [mine[:, LANE * m : LANE * (m + 1)] for m in range(3)]
            at = pl.multiple_of(peer * rows_two + 24 * i, 8)
            extra = ebuf[pl.ds(at, 24), :]
            fill = extra[:8] + pltpu.roll(extra[8:16], 32, 1) + pltpu.roll(extra[16:], 64, 1)
            whole = jnp.concatenate(blocks + [fill], axis=0).astype(BF16)
            for m in range(5):
                item_b[0][peer, i, m] = whole[16 * m : 16 * (m + 1)]

    def part_one(peer):
        part = product(n_t, peer, rows_one, rhs_one)
        for i in range(n_z):
            for m in range(2):
                mine = part[48 * i : 48 * (i + 1), LANE * m : LANE * (m + 1)]
                item_a[0][peer, i, m] = mine.astype(BF16)

    def part_last(d):
        peer = (z + d + n_z) % n_z
        starts = [pl.multiple_of(rows_one * yy + 48 * peer, 16) for yy in range(n_y)]
        lhs = jnp.concatenate(
            [
                jnp.concatenate([n_t[i, pl.ds(start, 48), :] for i in range(4)], axis=1)
                for start in starts
            ],
            axis=0,
        )
        part = dot(lhs, rhs_last)
        for yy in range(n_y):
            item_c[3][peer, yy] = part[48 * yy : 48 * (yy + 1)].astype(BF16)

    def y_begin(item, fill, base_sem):
        buf, inner, got = item[:3]
        fill(far)
        start_all(y_far(buf, inner, base_sem))
        fill(up)
        fill(down)
        start_all(y_direct(buf, got, base_sem))
        fill(dy)

    def y_relay(item, base_sem):
        buf, inner, got = item[:3]
        for copy in y_far(buf, inner, base_sem):
            copy.wait()
        for i in range(n_z // 2):
            k = n_z // 2 + i
            buf[up, i] = (buf[up, i].astype(F32) + inner[0, i].astype(F32)).astype(BF16)
            buf[down, k] = (buf[down, k].astype(F32) + inner[1, i].astype(F32)).astype(BF16)
        start_all(y_summed(buf, got, base_sem))

    def y_finish(item, base_sem):
        buf, _, got, q_buf = item[:4]
        for copy in y_direct(buf, got, base_sem) + y_summed(buf, got, base_sem):
            copy.wait()

        def total(d):
            at = (z + d) % n_z
            mine = buf[dy, at].astype(F32) + got[0, at].astype(F32) + got[1, at].astype(F32)
            q_buf[at] = mine.astype(BF16)

        for d in (3, 5, 4):
            total(d)
        start_all(z_far(item))
        for d in (2, 6, 1, 7, 0):
            total(d)

    @pl.when(first_seg)
    def _():
        lax.fori_loop(0, width // LANE, tap_grads, 0)

    for i in range(width // LANE):
        cols = slice(LANE * i, LANE * (i + 1))
        ebuf[cols, :] = gk[:, cols].T
    y_begin(item_b, part_two, 6)

    @pl.when(last_seg)
    def _():
        forward_turned((3,))
        wait_turned((3,))
        turn_normed((1, 2, 3))

    for copy in dpre_copies(0):
        copy.wait()
    rhs_one = jnp.concatenate([dpre4[j, :, :256]] + [dpre_r[d, :, :256] for d in range(3)], axis=0)
    part_one(far)
    start_all(y_far(item_a[0], item_a[1], 0))
    for copy in dpre_copies(1):
        copy.wait()
    rhs_last = jnp.concatenate([dpre4[j, :, 256:]] + [dpre_r[d, :, 256:] for d in range(3)], axis=0)
    for d in (3, -3, 4):
        part_last(d)
    start_all(z_far(item_c))
    part_one(up)
    part_one(down)
    y_relay(item_b, 6)
    start_all(y_direct(item_a[0], item_a[2], 0))
    part_one(dy)
    for d in (1, -1, 2, -2, 0):
        part_last(d)

    z_relay(item_c)
    y_relay(item_a, 0)
    y_finish(item_b, 6)
    y_finish(item_a, 0)

    @pl.when(first_seg)
    def _():
        grad_rows(EVERY)
        store_grad.start()

    qy[...] = z_total(item_c).astype(BF16)
    start_all(last_copies(*qy_c))
    z_relay(item_b)
    z_relay(item_a)

    fs[...] = jnp.zeros_like(fs)
    total = z_total(item_b)
    total = jnp.concatenate([total[m] for m in range(5)], axis=0)
    for i in range(4):
        for m in range(3):
            at = 24 * m + 6 * i
            fs[i, 16:22, LANE * m : LANE * (m + 1)] = total[at : at + 6]
    fill = total[72:]
    extra = jnp.concatenate([fill, pltpu.roll(fill, 96, 1), pltpu.roll(fill, 64, 1)], axis=0)
    for i in range(4):
        fs[i, 24:30, 0:LANE] = extra[6 * i : 6 * (i + 1)]
    total = z_total(item_a)
    for i in range(4):
        for m in range(2):
            fs[i, 0:12, LANE * m : LANE * (m + 1)] = total[m, 12 * i : 12 * (i + 1)]
    final = last_total(*qy_c)
    mine = jnp.concatenate([total[0], total[1], final], axis=1)
    place = pl.ds(pl.multiple_of((dy * n_z + z) * 48, 16), 48)
    weights = w1[place, pl.ds(pl.multiple_of(j * 384, LANE), 384)].astype(F32)
    gains = jnp.sum(mine * weights, axis=-1, keepdims=True) * tbuf[place, :]
    for i in range(4):
        fs[i, 0:12, 256:] = final[12 * i : 12 * (i + 1)]
        for m in range(2):
            at = 12 * i + 6 * m
            fs[i, 24:30, LANE * (m + 1) : LANE * (m + 2)] = gains[at : at + 6]
    f_out[...] = fs[...].astype(BF16)
    copies = [remote(f_out.at[peer_j(d)], f_in.at[j], sem_f, d, "tm", group[d]) for d in range(3)]
    start_all(copies)
    f_in[j] = f_out[j]
    for copy in copies:
        copy.wait()
    fs[...] = f_in[...].astype(F32)
    small = jnp.zeros((8, 3 * LANE), F32)
    for i in range(4):
        cols = slice(384 * i, 384 * (i + 1))
        for row in range(12):
            o_one[row, :, cols] = fs[i, row : row + 1, :]
        for row in range(6):
            o_two[row, :, cols] = fs[i, 16 + row : 17 + row, :]
        small = small + fs[i, 24:32, :]
    for i in range(6):
        o_kern[i] = small[i : i + 1, :TAPS]
    fill = jnp.zeros((LANE - 8, LANE), F32)
    turned = [
        jnp.concatenate([small[:, LANE * m : LANE * (m + 1)], fill], axis=0).T for m in range(3)
    ]
    o_gain2[...] = turned[0][TAPS : TAPS + 1, :6]
    for m in range(2):
        o_gain1[:, 6 * m : 6 * (m + 1)] = turned[m + 1][0:1, :6]
    store_out.wait()
    store_grad.wait()


def hand_over(*refs):
    n = (len(refs) - 1) // 3
    sources, results, held, sems = refs[:n], refs[n : 2 * n], refs[2 * n : 3 * n], refs[-1]
    inward = [pltpu.make_async_copy(sources[i], held[i], sems.at[0, i]) for i in range(n)]
    outward = [pltpu.make_async_copy(held[i], results[i], sems.at[1, i]) for i in range(n)]
    for copy in inward:
        copy.start()
    for i in range(n):
        inward[i].wait()
        outward[i].start()
    for copy in outward:
        copy.wait()


def per_device(inputs, lengths, w_first, kernel_w, gain_first, gain_second, w_second, grad_output):
    n_y = lax.axis_size("dp")
    n_tm = lax.axis_size("tm")
    n_z = n_tm // 4
    frames, model = inputs.shape[1:]
    width = w_second.shape[1]
    groups = n_y * n_tm
    vmem = pl.BlockSpec(memory_space=pltpu.VMEM)

    def buf(shape, dtype):
        return pltpu.VMEM(shape, dtype)

    def second(parts, rows):
        return (
            buf((n_z, parts, rows, LANE), BF16),
            buf((2, parts, rows, LANE), BF16),
            buf((2, parts - parts // 2, rows, LANE), BF16),
            buf((4, parts, rows, LANE), BF16),
        )

    def reduced(parts, rows):
        return (
            buf((n_y, n_z, parts, rows, LANE), BF16),
            buf((2, n_z // 2, parts, rows, LANE), BF16),
            buf((2, n_z, parts, rows, LANE), BF16),
        ) + second(parts, rows)

    wide = (frames, model)
    thin = (frames, width)
    padded = (frames + 2 * HALO, width)
    third = (4, frames, 384)
    scratch = [
        buf((model, 2 * width), BF16),
        buf((width, model), BF16),
        buf(wide, BF16),
        buf(wide, BF16),
        buf(wide, BF16),
        buf(wide, BF16),
        buf(wide, F32),
        buf((frames, LANE), F32),
        buf(wide, BF16),
        buf(thin, F32),
        buf(thin, F32),
        buf(padded, F32),
        buf(padded, F32),
        buf(thin, F32),
        buf(thin, F32),
        buf((frames, LANE), F32),
        buf(thin, F32),
        buf(thin, BF16),
        buf(thin, F32),
        buf(wide, F32),
        buf((2, HALO, width), BF16),
        buf((2, HALO, width), BF16),
        buf((2, HALO, width), BF16),
        buf((2, HALO, width), BF16),
        buf(third, BF16),
        buf(third, BF16),
        buf((3, frames, 384), BF16),
        buf((3, frames, 384), BF16),
        buf((3,) + wide, BF16),
        buf((3,) + thin, BF16),
        buf((4, model, LANE), BF16),
        buf((4, width, LANE), BF16),
        buf((LANE, width), F32),
        buf((width, LANE), F32),
        buf((model, LANE), F32),
        reduced(2, 48),
        reduced(5, 16),
        second(4, 48),
        buf((n_y, 48, LANE), BF16),
        buf((n_y - 1, 48, LANE), BF16),
        buf((4, 32, 384), F32),
        buf((4, 32, 384), BF16),
        buf((4, 32, 384), BF16),
        pltpu.SemaphoreType.DMA((4,)),
        pltpu.SemaphoreType.DMA((2, 4)),
        pltpu.SemaphoreType.DMA((2, 4)),
        pltpu.SemaphoreType.DMA((2, 4)),
        pltpu.SemaphoreType.DMA((2, 36)),
        pltpu.SemaphoreType.DMA((2, 15)),
        pltpu.SemaphoreType.DMA((2, 24)),
        pltpu.SemaphoreType.DMA((2, 3)),
    ]
    hbm = pl.BlockSpec(memory_space=pl.ANY)
    shapes = (
        jax.ShapeDtypeStruct(wide, BF16),
        jax.ShapeDtypeStruct(wide, BF16),
        jax.ShapeDtypeStruct((model // groups, 1, model), F32),
        jax.ShapeDtypeStruct((width // groups, 1, model), F32),
        jax.ShapeDtypeStruct((width // groups, 1, TAPS), F32),
        jax.ShapeDtypeStruct((1, model // groups), F32),
        jax.ShapeDtypeStruct((1, width // groups), F32),
    )
    results = pl.pallas_call(
        functools.partial(kernel, n_y, n_z, n_tm),
        out_shape=shapes,
        in_specs=[pl.BlockSpec(memory_space=pltpu.SMEM), vmem, vmem, hbm, hbm, vmem, vmem, vmem],
        out_specs=(hbm, hbm) + (vmem,) * 5,
        scratch_shapes=scratch,
        compiler_params=pltpu.CompilerParams(
            collective_id=0, has_side_effects=True, vmem_limit_bytes=60 * 1024 * 1024
        ),
        cost_estimate=pl.CostEstimate(
            flops=2 * 3 * frames * model * 3 * width, bytes_accessed=12_000_000, transcendentals=0
        ),
    )(
        lengths,
        inputs[0],
        grad_output[0],
        w_first[0],
        w_second[0],
        kernel_w.transpose(1, 0, 2),
        gain_first,
        gain_second,
    )
    out, grad, one, two, taps, g_one, g_two = pl.pallas_call(
        hand_over,
        out_shape=shapes,
        in_specs=[hbm] * 7,
        out_specs=(hbm,) * 7,
        scratch_shapes=[buf(shape.shape, shape.dtype) for shape in shapes]
        + [pltpu.SemaphoreType.DMA((2, 7))],
        compiler_params=pltpu.CompilerParams(vmem_limit_bytes=60 * 1024 * 1024),
    )(*results)
    return (
        out[None, None],
        grad[None, None],
        one.transpose(1, 0, 2),
        taps.transpose(1, 2, 0),
        g_one,
        g_two,
        two.transpose(1, 0, 2),
    )


def solution(mesh):
    in_specs = (
        P("dp", "tm", None),
        P("dp"),
        P("segment", None, None),
        P("segment", None, None),
        P("segment", None),
        P("segment", None),
        P("segment", None, None),
        P("dp", "tm", None),
    )
    out_specs = (
        P("segment", "dp", "tm", None),
        P("segment", "dp", "tm", None),
        P("segment", ("dp", "tm"), None),
        P("segment", None, ("dp", "tm")),
        P("segment", ("dp", "tm")),
        P("segment", ("dp", "tm")),
        P("segment", ("dp", "tm"), None),
    )
    return jax.shard_map(
        per_device, mesh=mesh, in_specs=in_specs, out_specs=out_specs, check_vma=False
    )
```
